512 devices in a mesh: lon: 32 (over z, x_hi, core), lat: 16 (over y, x_lo).
Axes of the slice: x: 4 (x_hi: 2, x_lo: 2; x = x_hi * 2 + x_lo), y: 8, z: 8, core: 2. Of those that a mesh axis runs over, the one named last changes fastest.
Arguments:
- tokens: bfloat16 [2, 192, 384, 192], P(None, 'lat', 'lon'), may hold values from -6 to 6
- cotangent: bfloat16 [2, 192, 384, 192], P(None, 'lat', 'lon'), may hold values from -6 to 6
- qkv_codes: int32 [192, 576], replicated, may hold values from -128 to 127
- proj_codes: int32 [192, 192], replicated, may hold values from -128 to 127
- up_codes: int32 [192, 768], replicated, may hold values from -128 to 127
- down_codes: int32 [768, 192], replicated, may hold values from -128 to 127
- bit_widths: int32 [4], replicated, may hold values from 6 to 8
- quant_scales: int32 [4], replicated, may hold values from 300 to 599
- bias_table: bfloat16 [32, 1, 6, 3312], P('lat'), may hold values from -4 to 302
- bias_index: int32 [20736], replicated, may hold values from 0 to 3311
- merge_weight: bfloat16 [768, 384], replicated, may hold values from -0.21875 to 0.21875
Outputs:
- merged: bfloat16 [2, 96, 192, 384], P(None, 'lat', 'lon')
- grad_tokens: bfloat16 [2, 192, 384, 192], P(None, 'lat', 'lon')
- grad_qkv: bfloat16 [192, 576], replicated
- grad_proj: bfloat16 [192, 192], replicated
- grad_up: bfloat16 [192, 768], replicated
- grad_down: bfloat16 [768, 192], replicated
The draws below stay inside these ranges and needn't reach their ends.
All inputs are finite; a program needn't handle non-finite values.
Results may differ from the reference program's by a relative error of at most 0.024.
The reference program's roundings to bfloat16 on the way count: a program that leaves them out, or rounds other values in their place, can miss the bound.
Values may be sent and summed in bfloat16 or wider, within the bound.
No kernel may reach another device: no remote copies, remote signals or barrier semaphores. Data moves between devices by JAX's collectives and lax.ppermute only.
A program may use at most 128 MiB of HBM per device.

```python
import math
import jax
import jax.numpy as jnp
from jax import lax

C = 192
HEADS = 6
FF = 768
HEAD_DIM = 32
LEV = 2
WLEV = 2
WLAT = 6
WLON = 12
ROWS_DEV = 12
WTOK = 144
POS = 3312
LATT = 192
LATS = 181
LONT = 384
BIAS_ROWS = 32
N_LAT = 16


def draw_bias_table(key, part):
    key = jax.random.fold_in(key, 7)
    key_base = jax.random.fold_in(key, 0)
    table_shape = (BIAS_ROWS, LEV // WLEV, HEADS, POS)
    values = jnp.clip(jax.random.normal(key_base, table_shape, jnp.float32), -4.0, 4.0)
    return values.astype(jnp.bfloat16)


def set_ends(result, own_key, smallest, high):
    index_at = [jax.random.randint(jax.random.fold_in(own_key, axis), (), 0, length) for axis, length in enumerate(result.shape)]
    widest = result.shape.index(max(result.shape))
    beside = index_at[:widest] + [(index_at[widest] + 1) % result.shape[widest]] + index_at[widest + 1:]
    return result.at[tuple(index_at)].set(smallest).at[tuple(beside)].set(high)


def block_scale(stream_key, shape, shards, smallest, top_value):
    def one(dim, blocks):
        heights = jax.random.uniform(jax.random.fold_in(jax.random.fold_in(stream_key, 6), dim), (blocks,), jnp.float32, smallest / len(shards), top_value / len(shards))
        return jnp.repeat(jnp.exp(heights), shape[dim] // blocks).reshape((-1,) + (1,) * (len(shape) - dim - 1))

    level = one(*shards[0])
    for cut in shards[1:]:
        level = level * one(*cut)
    return level


def normal_values(stream_key, extent, deviation, reach, cuts=(), kind=jnp.bfloat16):
    array = jax.random.normal(stream_key, extent, jnp.float32) * deviation
    if len(cuts) > 0:
        array = block_scale(stream_key, extent, cuts, -0.22, 0.18) * array
    return jnp.clip(array, min=-reach, max=reach).astype(kind)


def setup_inputs(seed: int = 0) -> dict:
    key_of = jax.random.split(jax.random.key(seed), 12)
    return {
        "tokens": normal_values(key_of[0], (LEV, LATT, LONT, C), 1.0, 6.0, ((1, 16), (2, 32))),
        "cotangent": normal_values(key_of[1], (LEV, LATT, LONT, C), 1.0, 6.0, ((1, 16), (2, 32))),
        "qkv_codes": set_ends(jax.random.randint(key_of[2], (C, 3 * C), -128, 128), jax.random.fold_in(key_of[2], 1), -128, 127).astype(jnp.int32),
        "proj_codes": set_ends(jax.random.randint(key_of[3], (C, C), -128, 128), jax.random.fold_in(key_of[3], 1), -128, 127).astype(jnp.int32),
        "up_codes": set_ends(jax.random.randint(key_of[4], (C, FF), -128, 128), jax.random.fold_in(key_of[4], 1), -128, 127).astype(jnp.int32),
        "down_codes": set_ends(jax.random.randint(key_of[5], (FF, C), -128, 128), jax.random.fold_in(key_of[5], 1), -128, 127).astype(jnp.int32),
        "bit_widths": set_ends(jax.random.randint(key_of[6], (4,), 6, 9), jax.random.fold_in(key_of[6], 1), 6, 8).astype(jnp.int32),
        "quant_scales": set_ends(jax.random.randint(key_of[7], (4,), 300, 600), jax.random.fold_in(key_of[7], 1), 300, 599).astype(jnp.int32),
        "bias_table": draw_bias_table(jax.random.fold_in(key_of[11], 71), 0),
        "bias_index": set_ends(jax.random.randint(key_of[9], (WTOK * WTOK,), 0, POS), jax.random.fold_in(key_of[9], 1), 0, POS - 1).astype(jnp.int32),
        "merge_weight": normal_values(key_of[10], (4 * C, 2 * C), (4 * C) ** -0.5, 0.21875),
    }


EPSILON = 1e-05
MASKED = -1000000000.0

def product(left, right):
    return jnp.dot(left, right, preferred_element_type=jnp.float32)

def crossed(left, right):
    return jnp.dot(left.T, right, preferred_element_type=jnp.float32)

def dequant(int_codes, bit_count, quant_scale, fan_in):
    largest = jnp.left_shift(jnp.ones((), jnp.int32), bit_count - 1) - 1
    clipped = jnp.clip(int_codes, -largest, largest).astype(jnp.float32)
    factor = math.sqrt(C / fan_in) / quant_scale.astype(jnp.float32)
    return (clipped * factor).astype(jnp.bfloat16)

def normalize(values):
    center = values - lax.optimization_barrier(jnp.mean(values, axis=-1, keepdims=True))
    spread = lax.optimization_barrier(jnp.mean(center * center, axis=-1, keepdims=True))
    return center * lax.rsqrt(spread + EPSILON)

def norm_back(source, upstream):
    pullback = jax.vjp(normalize, source.astype(jnp.float32))[1]
    return pullback(upstream.astype(jnp.float32))[0]

def gelu_back(pre_act, upstream):
    pullback = jax.vjp(jax.nn.gelu, pre_act)[1]
    return pullback(upstream.astype(jnp.float32))[0]

def allowed_table(lat_start, lat_limit, level_count, row_windows):
    position = jnp.arange(WTOK, dtype=jnp.int32)
    level_in = position // (WLAT * WLON)
    row_in = position // WLON % WLAT
    window_level = WLEV * jnp.arange(level_count // WLEV, dtype=jnp.int32)
    levels = (window_level[:, None] + level_in[None, :] + 1) % level_count
    group = (levels + 1) // 2
    same = group[:, :, None] == group[:, None, :]
    lat_rows = lat_start + WLAT * jnp.arange(row_windows, dtype=jnp.int32)[:, None] + row_in[None, :]
    key_ok = (lat_rows >= 0) & (lat_rows < lat_limit)
    allowed = same[:, None, :, :] & key_ok[None, :, None, :]
    return allowed.reshape(-1, WTOK, WTOK)

def window_terms(table_rows, bias_index, lat_start, lat_limit, level_count):
    row_windows = table_rows.shape[0]
    level_windows = level_count // WLEV
    gathered = table_rows[:, :, :, bias_index].astype(jnp.float32)
    gathered = gathered.reshape(row_windows, level_windows, HEADS, WTOK, WTOK).transpose(1, 0, 2, 3, 4)
    gathered = gathered.reshape(level_windows * row_windows, HEADS, WTOK, WTOK)
    return (gathered, allowed_table(lat_start, lat_limit, level_count, row_windows))

def to_windows(window_frame):
    level_count, row_count, col_count, feat_count = window_frame.shape
    rolled = jnp.roll(window_frame, -1, axis=0)
    pieces = rolled.reshape(level_count // WLEV, WLEV, row_count // WLAT, WLAT, col_count // WLON, WLON, feat_count)
    return pieces.transpose(0, 2, 4, 1, 3, 5, 6).reshape(-1, WTOK, feat_count)

def from_windows(windows, level_count, row_count, col_count):
    feat_count = windows.shape[-1]
    pieces = windows.reshape(level_count // WLEV, row_count // WLAT, col_count // WLON, WLEV, WLAT, WLON, feat_count)
    pieces = pieces.transpose(0, 3, 1, 4, 2, 5, 6).reshape(level_count, row_count, col_count, feat_count)
    return jnp.roll(pieces, 1, axis=0)

def attend(windows, bias_terms, allowed):
    window_count = windows.shape[0]
    group_count = bias_terms.shape[0]
    query_part, key_part, value_part = jnp.split(windows.astype(jnp.float32), 3, axis=-1)
    query_part = query_part.reshape(window_count, WTOK, HEADS, HEAD_DIM)
    key_part = key_part.reshape(window_count, WTOK, HEADS, HEAD_DIM)
    value_part = value_part.reshape(window_count, WTOK, HEADS, HEAD_DIM)
    scores = jnp.einsum('wqhd,wkhd->whqk', query_part, key_part) * HEAD_DIM ** (-0.5)
    scores = scores.reshape(group_count, window_count // group_count, HEADS, WTOK, WTOK) + bias_terms[:, None]
    scores = jnp.where(allowed[:, None, None], scores, MASKED)
    top_score = lax.optimization_barrier(jnp.max(scores, axis=-1, keepdims=True))
    weights = jnp.exp(scores - top_score)
    weights = (weights / lax.optimization_barrier(jnp.sum(weights, axis=-1, keepdims=True))).astype(jnp.bfloat16)
    weights = weights.reshape(window_count, HEADS, WTOK, WTOK)
    mixed = jnp.einsum('whqk,wkhd->wqhd', weights.astype(jnp.float32), value_part)
    return mixed.reshape(window_count, WTOK, C)

def merge_patches(final, merge_weight):
    level_count, row_count, col_count, feat_count = final.shape
    grouped = final.reshape(level_count, row_count // 2, 2, col_count // 2, 2, feat_count)
    grouped = grouped.transpose(0, 1, 3, 2, 4, 5).reshape(-1, 4 * feat_count)
    normed = normalize(grouped.astype(jnp.float32)).astype(jnp.bfloat16)
    merged = product(normed, merge_weight).astype(jnp.bfloat16)
    return merged.reshape(level_count, row_count // 2, col_count // 2, 2 * feat_count)

def shift_in(source):
    blank = jnp.zeros_like(source[:, :WLAT // 2])
    moved = jnp.concatenate([blank, source[:, :-(WLAT // 2)]], axis=1)
    return jnp.roll(moved, WLON // 2, axis=2)

def shift_out(source):
    moved = jnp.roll(source, -(WLON // 2), axis=2)
    blank = jnp.zeros_like(moved[:, :WLAT // 2])
    return jnp.concatenate([moved[:, WLAT // 2:], blank], axis=1)

def to_frames(source):
    return source.reshape(LEV, N_LAT, ROWS_DEV, LONT, -1).transpose(1, 0, 2, 3, 4)

def from_frames(stack):
    return stack.transpose(1, 0, 2, 3, 4).reshape(LEV, LATT, LONT, -1)

def reference(tokens, cotangent, qkv_codes, proj_codes, up_codes, down_codes, bit_widths, quant_scales, bias_table, bias_index, merge_weight):
    w_qkv = dequant(qkv_codes, bit_widths[0], quant_scales[0], C)
    w_proj = dequant(proj_codes, bit_widths[1], quant_scales[1], C)
    w_up = dequant(up_codes, bit_widths[2], quant_scales[2], C)
    w_down = dequant(down_codes, bit_widths[3], quant_scales[3], FF)
    token_count = LEV * LATT * LONT
    row_mask = (jnp.arange(LATT, dtype=jnp.int32) < LATS)[None, :, None, None]
    start = jnp.where(row_mask, tokens, jnp.zeros_like(tokens))
    start_flat = start.reshape(token_count, C)
    normed = normalize(start_flat.astype(jnp.float32)).astype(jnp.bfloat16)
    qkv = product(normed, w_qkv).astype(jnp.bfloat16).reshape(LEV, LATT, LONT, 3 * C)
    lat_ids = jnp.arange(N_LAT, dtype=jnp.int32)
    table_frames = bias_table.reshape(N_LAT, ROWS_DEV // WLAT, LEV // WLEV, HEADS, POS)

    def forward_frame(payload):
        frame_qkv, table_rows, lat_id = payload
        bias_terms, allowed = window_terms(table_rows, bias_index, lat_id * ROWS_DEV - WLAT // 2, LATS, LEV)
        outcome = attend(to_windows(frame_qkv), bias_terms, allowed)
        return from_windows(outcome.astype(jnp.bfloat16), LEV, ROWS_DEV, LONT)
    heads_out = shift_out(from_frames(lax.map(forward_frame, (to_frames(shift_in(qkv)), table_frames, lat_ids))))
    heads_flat = heads_out.reshape(token_count, C)
    resid = (start_flat.astype(jnp.float32) + product(heads_flat, w_proj)).astype(jnp.bfloat16)
    normed_two = normalize(resid.astype(jnp.float32)).astype(jnp.bfloat16)
    pre_act = product(normed_two, w_up)
    hidden = jax.nn.gelu(pre_act).astype(jnp.bfloat16)
    final = (resid.astype(jnp.float32) + product(hidden, w_down)).reshape(LEV, LATT, LONT, C)
    final = jnp.where(row_mask, final, 0.0).astype(jnp.bfloat16)
    merged = merge_patches(final, merge_weight)
    d_out = jnp.where(row_mask, cotangent, jnp.zeros_like(cotangent)).reshape(token_count, C)
    down_total = crossed(hidden, d_out)
    d_hidden = product(d_out, w_down.T).astype(jnp.bfloat16)
    d_pre = gelu_back(pre_act, d_hidden).astype(jnp.bfloat16)
    up_total = crossed(normed_two, d_pre)
    d_normed_two = product(d_pre, w_up.T).astype(jnp.bfloat16)
    d_resid = (d_out.astype(jnp.float32) + norm_back(resid, d_normed_two)).astype(jnp.bfloat16)
    proj_total = crossed(heads_flat, d_resid)
    d_heads = product(d_resid, w_proj.T).astype(jnp.bfloat16).reshape(LEV, LATT, LONT, C)

    def backward_frame(payload):
        frame_qkv, frame_grad, table_rows, lat_id = payload
        bias_terms, allowed = window_terms(table_rows, bias_index, lat_id * ROWS_DEV - WLAT // 2, LATS, LEV)

        def local_attend(windows):
            return attend(windows, bias_terms, allowed)
        pullback = jax.vjp(local_attend, to_windows(frame_qkv))[1]
        upstream = to_windows(frame_grad).astype(jnp.float32)
        return from_windows(pullback(upstream)[0], LEV, ROWS_DEV, LONT)
    stacked = lax.map(backward_frame, (to_frames(shift_in(qkv)), to_frames(shift_in(d_heads)), table_frames, lat_ids))
    d_qkv = shift_out(from_frames(stacked)).reshape(token_count, 3 * C)
    qkv_total = crossed(normed, d_qkv)
    d_normed = product(d_qkv, w_qkv.T).astype(jnp.bfloat16)
    grad_flat = d_resid.astype(jnp.float32) + norm_back(start_flat, d_normed)
    grad_tokens = jnp.where(row_mask, grad_flat.reshape(LEV, LATT, LONT, C), 0.0).astype(jnp.bfloat16)
    return (merged, grad_tokens, qkv_total.astype(jnp.bfloat16), proj_total.astype(jnp.bfloat16), up_total.astype(jnp.bfloat16), down_total.astype(jnp.bfloat16))
```

```python
import math

import jax
import jax.numpy as jnp
from jax import lax
from jax.experimental import pallas as pl
from jax.experimental.pallas import tpu as pltpu
from jax.sharding import Mesh
from jax.sharding import PartitionSpec as P

C = 192
HEADS = 6
FF = 768
HEAD_DIM = 32
WLAT = 6
WLON = 12
LAT_PAD = 11
WTOK = 144
POS = 3312

ROWS = 12
COLS = 12
LEVS = 2
OFF = WLAT // 2
HALF = WLON // 2
SUB = 8
FRAME = LEVS * ROWS * 2 * SUB
BLOCK = FRAME // 4
STACK = HEADS * BLOCK
CHUNKS = -(-POS // 128)

EPSILON = 1e-05
MASKED = -1000000000.0
F32 = jnp.float32
BF16 = jnp.bfloat16
VMEM_LIMIT = 56 * 1024 * 1024

LAT = ("y", "xl")
LON = ("z", "xh", "c")
NEAR = ("xh", "c", "xl")
FAR = ("y", "z")


def iota(shape, dim):
    return lax.broadcasted_iota(jnp.int32, shape, dim)


def product(left, right):
    return lax.dot_general(left, right, (((1,), (0,)), ((), ())), preferred_element_type=F32)


def across(left, right):
    return lax.dot_general(left, right, (((1,), (1,)), ((), ())), preferred_element_type=F32)


def crossed(left, right):
    return lax.dot_general(left, right, (((0,), (0,)), ((), ())), preferred_element_type=F32)


def pack_kernel(tok_ref, cot_ref, own_ref, lat_ref, lon_ref, diag_ref, wide):
    wide[...] = jnp.zeros_like(wide)
    wide[:, :, 0:COLS, :] = jnp.concatenate(
        [tok_ref[...].astype(F32), cot_ref[...].astype(F32)], axis=-1
    )
    left = wide[:, :, 0:SUB, :]
    right = wide[:, :, HALF : HALF + SUB, :]

    def flat(piece):
        return piece.reshape(-1, 2 * C).astype(BF16)

    own_ref[...] = flat(left[:, : ROWS - OFF])
    lat_ref[...] = flat(left[:, ROWS - OFF :])
    lon_ref[...] = flat(right[:, : ROWS - OFF])
    diag_ref[...] = flat(right[:, ROWS - OFF :])


def prep_kernel(
    lat_ref,
    lim_ref,
    fac_ref,
    idx_ref,
    tab_ref,
    cq_ref,
    cp_ref,
    cu_ref,
    cd_ref,
    wq_ref,
    wp_ref,
    wu_ref,
    wd_ref,
    bias_ref,
    rows,
):
    def dequant(codes, layer):
        limit = lim_ref[layer]
        clipped = jnp.minimum(jnp.maximum(codes, -limit), limit).astype(F32)
        return clipped * fac_ref[layer]

    full = dequant(cq_ref[...], 0)
    for part in range(3):
        wq_ref[part] = full[:, part * C : (part + 1) * C].astype(BF16)
    wp_ref[...] = dequant(cp_ref[...], 1).astype(BF16)
    wu_ref[...] = dequant(cu_ref[...], 2).astype(BF16)
    wd_ref[...] = dequant(cd_ref[...], 3).astype(BF16)

    for win in range(2):
        table = tab_ref[win, 0].astype(F32)
        for chunk in range(CHUNKS):
            width = min(128, POS - chunk * 128)
            rows[chunk, win * SUB : win * SUB + HEADS, 0:width] = table[
                :, chunk * 128 : chunk * 128 + width
            ]

    index = idx_ref[...]
    high = lax.shift_right_logical(index, 7).astype(F32).astype(BF16)
    low = jnp.bitwise_and(index, 127).astype(F32).astype(BF16)

    def place(where):
        sub = jnp.bitwise_and(where, SUB - 1)
        token = (where >> 4) * WLON + jnp.bitwise_and(where >> 3, 1) * HALF + sub
        return jnp.where((sub < HALF) & (where < BLOCK), token, -1000)

    key = iota((BLOCK, 128), 1)
    for lev in range(LEVS):
        base = (1 - lev) * (WTOK // 2)
        pick_q = (iota((BLOCK, WTOK), 1) == place(iota((BLOCK, WTOK), 0)) + base).astype(F32)
        pick_k = (iota((WTOK, 128), 0) == place(iota((WTOK, 128), 1)) + base).astype(F32)
        pick_q = pick_q.astype(BF16)
        pick_k = pick_k.astype(BF16)
        hi = product(product(pick_q, high).astype(BF16), pick_k).astype(jnp.int32)
        lo = product(product(pick_q, low).astype(BF16), pick_k).astype(jnp.int32)
        for win in range(2):
            row = lat_ref[0] * ROWS - OFF + win * WLAT + (key >> 4)
            usable = (row >= 0) & (row < lat_ref[1])
            usable = usable & (jnp.bitwise_and(key, SUB - 1) < HALF) & (key < BLOCK)

            def one_head(head, carry):
                found = jnp.zeros((BLOCK, 128), F32)
                for chunk in range(CHUNKS):
                    line = rows[chunk, pl.ds(win * SUB + head, 1), :]
                    taken = jnp.take_along_axis(
                        jnp.broadcast_to(line, (BLOCK, 128)), lo, axis=1
                    )
                    found = jnp.where(hi == chunk, taken, found)
                found = jnp.where(usable, found, MASKED)
                at = pl.multiple_of(head * BLOCK, BLOCK)
                bias_ref[lev * 2 + win, pl.ds(at, BLOCK), :] = found.astype(BF16)
                return carry

            lax.fori_loop(0, HEADS, one_head, 0)


def unit(values):
    center = values - jnp.mean(values, axis=-1, keepdims=True)
    spread = jnp.mean(center * center, axis=-1, keepdims=True)
    scale = lax.rsqrt(spread + EPSILON)
    return center * scale, scale


def unit_back(normal, scale, upstream):
    level = jnp.mean(upstream, axis=-1, keepdims=True)
    along = jnp.mean(upstream * normal, axis=-1, keepdims=True)
    return scale * (upstream - level - normal * along)


def main_kernel(
    lat_ref,
    own_ref,
    lat_part_ref,
    lon_part_ref,
    diag_part_ref,
    wq_ref,
    wp_ref,
    wu_ref,
    wd_ref,
    bias_ref,
    own_out,
    lat_out,
    lon_out,
    diag_out,
    sums_ref,
    frame,
):
    below = ROWS - OFF

    def piece(ref, rows):
        return ref[...].astype(F32).reshape(LEVS, rows, SUB, 2 * C)

    frame[:, OFF:, 1] = piece(own_ref, below)
    frame[:, :OFF, 1] = piece(lat_part_ref, OFF)
    frame[:, OFF:, 0] = piece(lon_part_ref, below)
    frame[:, :OFF, 0] = piece(diag_part_ref, OFF)
    both = frame[...].reshape(FRAME, 2 * C)

    place = iota((FRAME, C), 0)
    row = lat_ref[0] * ROWS - OFF + (place >> 4) - jnp.where(place >= FRAME // 2, ROWS, 0)
    valid = (row >= 0) & (row < lat_ref[1]) & (jnp.bitwise_and(place, SUB - 1) < HALF)
    start = jnp.where(valid, both[:, :C], 0.0)
    d_out = jnp.where(valid, both[:, C:], 0.0)
    d_out_low = d_out.astype(BF16)

    normal, scale = unit(start)
    normed = normal.astype(BF16)
    query = product(normed, wq_ref[0]).astype(BF16)
    key = product(normed, wq_ref[1]).astype(BF16)
    value = product(normed, wq_ref[2]).astype(BF16)

    lane_head = iota((HEADS, 1, C), 2) >> 5
    head_mask = lane_head == iota((HEADS, 1, C), 0)
    mask_low = head_mask.astype(F32).astype(BF16)
    mask_full = head_mask.astype(F32)

    def spread_heads(block):
        return (block[None] * mask_low).reshape(STACK, C)

    def join_heads(stacked):
        return jnp.sum(stacked.reshape(HEADS, BLOCK, C) * mask_full, axis=0)

    saved = []
    heads_parts = []
    for block in range(4):
        at = slice(block * BLOCK, (block + 1) * BLOCK)
        q_stack = spread_heads(query[at])
        scores = across(q_stack, key[at]) * HEAD_DIM ** (-0.5)
        scores = scores + bias_ref[block][:, :BLOCK].astype(F32)
        weights = jnp.exp(scores - jnp.max(scores, axis=-1, keepdims=True))
        weights = weights / jnp.sum(weights, axis=-1, keepdims=True)
        weights_low = weights.astype(BF16)
        heads_parts.append(join_heads(product(weights_low, value[at])))
        saved.append((q_stack, weights, weights_low))
    heads = jnp.concatenate(heads_parts, axis=0).astype(BF16)

    resid = (start + product(heads, wp_ref[...])).astype(BF16).astype(F32)
    normal_two, scale_two = unit(resid)
    normed_two = normal_two.astype(BF16)
    pre_act = product(normed_two, wu_ref[...])
    inner = math.sqrt(2 / math.pi)
    square = pre_act * pre_act
    bend = jnp.tanh(inner * (pre_act + 0.044715 * (square * pre_act)))
    half = 0.5 * (1.0 + bend)
    hidden = (pre_act * half).astype(BF16)
    slope = half + 0.5 * pre_act * (1.0 - bend * bend) * (
        inner * (1.0 + (3 * 0.044715) * square)
    )
    final = jnp.where(valid, resid + product(hidden, wd_ref[...]), 0.0)

    d_hidden = across(d_out_low, wd_ref[...]).astype(BF16).astype(F32)
    d_pre = (slope * d_hidden).astype(BF16)
    d_normed_two = across(d_pre, wu_ref[...]).astype(BF16).astype(F32)
    d_resid = (d_out + unit_back(normal_two, scale_two, d_normed_two)).astype(BF16)
    d_heads = across(d_resid, wp_ref[...]).astype(BF16)

    dq_parts = []
    dk_parts = []
    dv_parts = []
    for block in range(4):
        at = slice(block * BLOCK, (block + 1) * BLOCK)
        q_stack, weights, weights_low = saved[block]
        d_stack = spread_heads(d_heads[at])
        d_weights = across(d_stack, value[at]).astype(BF16).astype(F32)
        dv_parts.append(crossed(weights_low, d_stack))
        inside = jnp.sum(weights * d_weights, axis=-1, keepdims=True)
        d_scores = (weights * (d_weights - inside) * HEAD_DIM ** (-0.5)).astype(BF16)
        dq_parts.append(join_heads(product(d_scores, key[at])))
        dk_parts.append(crossed(d_scores, q_stack))
    d_query = jnp.concatenate(dq_parts, axis=0).astype(BF16)
    d_key = jnp.concatenate(dk_parts, axis=0).astype(BF16)
    d_value = jnp.concatenate(dv_parts, axis=0).astype(BF16)

    d_normed = across(d_query, wq_ref[0]) + across(d_key, wq_ref[1]) + across(d_value, wq_ref[2])
    d_normed = d_normed.astype(BF16).astype(F32)
    grad = jnp.where(valid, d_resid.astype(F32) + unit_back(normal, scale, d_normed), 0.0)

    result = jnp.concatenate([final, grad], axis=-1).reshape(LEVS, ROWS, 2, SUB, 2 * C)

    def flat(part):
        return part.reshape(-1, 2 * C).astype(BF16)

    own_out[...] = flat(result[:, OFF:, 1])
    lat_out[...] = flat(result[:, :OFF, 1])
    lon_out[...] = flat(result[:, OFF:, 0])
    diag_out[...] = flat(result[:, :OFF, 0])

    small = [
        crossed(normed, d_query),
        crossed(normed, d_key),
        crossed(normed, d_value),
        crossed(heads, d_resid),
    ]
    tiles = [total[:, :128] for total in small]
    tiles += [
        jnp.concatenate([small[i][:, 128:], small[i + 1][:, 128:]], axis=-1) for i in (0, 2)
    ]
    for wide in (crossed(normed_two, d_pre), crossed(d_out_low, hidden)):
        tiles += [wide[:, i * 128 : (i + 1) * 128] for i in range(6)]
    for i, tile in enumerate(tiles):
        sums_ref[i * C : (i + 1) * C, :] = tile.astype(BF16)


def spread_kernel(sums_ref, qkv_ref, proj_ref, up_ref, down_ref):
    def tile(i):
        return sums_ref[i * C : (i + 1) * C, :].astype(F32)

    ends = [tile(4)[:, :64], tile(4)[:, 64:], tile(5)[:, :64], tile(5)[:, 64:]]
    small = [jnp.concatenate([tile(i), ends[i]], axis=-1) for i in range(4)]
    qkv_ref[...] = jnp.concatenate(small[:3], axis=-1).astype(BF16)
    proj_ref[...] = small[3].astype(BF16)
    for i in range(6):
        up_ref[:, i * 128 : (i + 1) * 128] = sums_ref[(6 + i) * C : (7 + i) * C, :]
        down_ref[i * 128 : (i + 1) * 128, :] = tile(12 + i).T.astype(BF16)


def finish_kernel(
    own_ref, lat_ref, lon_ref, diag_ref, weight_ref, merged_ref, grad_ref, frame
):
    above = ROWS - OFF

    def piece(ref, rows):
        return ref[...].astype(F32).reshape(LEVS, rows, SUB, 2 * C)

    frame[:, :above, 0] = piece(own_ref, above)
    frame[:, above:, 0] = piece(lat_ref, OFF)
    frame[:, :above, 1] = piece(lon_ref, above)
    frame[:, above:, 1] = piece(diag_ref, OFF)
    both = frame[...].reshape(FRAME, 2 * C)
    final = both[:, :C].astype(BF16)
    grad = both[:, C:].astype(BF16)

    def source(col):
        return jnp.where(col >= HALF, col + (SUB - HALF), col)

    to = iota((FRAME, FRAME), 0)
    col = jnp.bitwise_and(to, 15)
    pick = (iota((FRAME, FRAME), 1) == to - col + source(col)) & (col < COLS)
    moved = product(pick.astype(F32).astype(BF16), grad).reshape(LEVS, ROWS, 16, C)
    grad_ref[...] = moved[:, :, :COLS, :].astype(BF16)

    count = LEVS * (ROWS // 2) * SUB
    to = iota((count, FRAME), 0)
    lev = jnp.where(to >= count // 2, 1, 0)
    pair = (to >> 3) - lev * (ROWS // 2)
    parts = []
    for down in range(2):
        for right in range(2):
            col = 2 * jnp.bitwise_and(to, SUB - 1) + right
            wanted = lev * (FRAME // 2) + (2 * pair + down) * 16 + source(col)
            pick = (iota((count, FRAME), 1) == wanted) & (col < COLS)
            parts.append(product(pick.astype(F32).astype(BF16), final))
    width = 4 * C
    mean = sum(jnp.sum(part, axis=-1, keepdims=True) for part in parts) / width
    centers = [part - mean for part in parts]
    spread = sum(jnp.sum(part * part, axis=-1, keepdims=True) for part in centers) / width
    scale = lax.rsqrt(spread + EPSILON)
    total = jnp.zeros((count, 2 * C), F32)
    for i, part in enumerate(centers):
        total = total + product((part * scale).astype(BF16), weight_ref[i * C : (i + 1) * C, :])
    merged_ref[...] = total.reshape(LEVS, ROWS // 2, SUB, 2 * C)[:, :, :HALF, :].astype(BF16)


def call(kernel, outs, args, scratch=(), scalars=0, flops=0):
    vmem = pl.BlockSpec(memory_space=pltpu.VMEM)
    smem = pl.BlockSpec(memory_space=pltpu.SMEM)
    moved = sum(math.prod(a.shape) * a.dtype.itemsize for a in args)
    moved += sum(math.prod(s) * jnp.dtype(t).itemsize for s, t in outs)
    return pl.pallas_call(
        kernel,
        out_shape=[jax.ShapeDtypeStruct(s, t) for s, t in outs],
        in_specs=[smem] * scalars + [vmem] * (len(args) - scalars),
        out_specs=[vmem] * len(outs),
        scratch_shapes=list(scratch),
        compiler_params=pltpu.CompilerParams(vmem_limit_bytes=VMEM_LIMIT),
        cost_estimate=pl.CostEstimate(flops=flops, bytes_accessed=moved, transcendentals=0),
    )(*args)


def shifted(block, lat_step, lon_step):
    rows = lax.axis_size(LAT)
    cols = lax.axis_size(LON)
    if lat_step and lon_step:
        route = [
            (col * rows + row, (col + lon_step) % cols * rows + row + lat_step)
            for col in range(cols)
            for row in range(rows)
            if 0 <= row + lat_step < rows
        ]
        return lax.ppermute(block, LON + LAT, route)
    if lat_step:
        route = [(r, r + lat_step) for r in range(rows) if 0 <= r + lat_step < rows]
        return lax.ppermute(block, LAT, route)
    return lax.ppermute(block, LON, [(c, (c + lon_step) % cols) for c in range(cols)])


def exchange(parts, axes):
    return lax.all_to_all(parts, axes, 0, 0)


def total_of(parts):
    return jnp.sum(parts.astype(F32), axis=0).astype(BF16)


def summed_everywhere(sums):
    near = lax.axis_size(NEAR)
    far = lax.axis_size(FAR)
    rows = sums.shape[0] // near
    padded = -(-rows // (8 * far)) * (8 * far)
    part = total_of(exchange(sums.reshape(near, rows, 128), NEAR))
    part = jnp.pad(part, ((0, padded - rows), (0, 0)))
    part = total_of(exchange(part.reshape(far, padded // far, 128), FAR))
    part = exchange(jnp.broadcast_to(part[None], (far,) + part.shape), FAR)
    part = part.reshape(padded, 128)[:rows]
    whole = exchange(jnp.broadcast_to(part[None], (near,) + part.shape), NEAR)
    return whole.reshape(near * rows, 128)


def per_device(
    tokens,
    cotangent,
    qkv_codes,
    proj_codes,
    up_codes,
    down_codes,
    bit_widths,
    quant_scales,
    bias_table,
    bias_index,
    merge_weight,
):
    lat_limit = lax.axis_size(LAT) * ROWS - LAT_PAD
    lat_info = jnp.stack([lax.axis_index(LAT), lat_limit]).astype(jnp.int32)
    limits = jnp.left_shift(jnp.ones((4,), jnp.int32), bit_widths - 1) - 1
    fan_in = jnp.array([1.0, 1.0, 1.0, math.sqrt(C / FF)], F32)
    factors = fan_in / quant_scales.astype(F32)

    big = ROWS - OFF
    big_shape = (LEVS * big * SUB, 2 * C)
    thin_shape = (LEVS * OFF * SUB, 2 * C)
    pieces = [(big_shape, BF16), (thin_shape, BF16), (big_shape, BF16), (thin_shape, BF16)]
    own, lat_part, lon_part, diag_part = call(
        pack_kernel,
        pieces,
        (tokens, cotangent),
        [pltpu.VMEM((LEVS, ROWS, 16, 2 * C), F32)],
    )
    lon_part = shifted(lon_part, 0, 1)
    lat_part = shifted(lat_part, 1, 0)
    diag_part = shifted(diag_part, 1, 1)

    w_qkv, w_proj, w_up, w_down, bias = call(
        prep_kernel,
        [
            ((3, C, C), BF16),
            ((C, C), BF16),
            ((C, FF), BF16),
            ((FF, C), BF16),
            ((4, STACK, 128), BF16),
        ],
        (
            lat_info,
            limits,
            factors,
            bias_index.reshape(WTOK, WTOK),
            bias_table,
            qkv_codes,
            proj_codes,
            up_codes,
            down_codes,
        ),
        [pltpu.VMEM((CHUNKS, 16, 128), F32)],
        scalars=3,
        flops=2_000_000_000,
    )
    own, lat_part, lon_part, diag_part, sums = call(
        main_kernel,
        pieces + [((18 * C, 128), BF16)],
        (lat_info, own, lat_part, lon_part, diag_part, w_qkv, w_proj, w_up, w_down, bias),
        [pltpu.VMEM((LEVS, ROWS, 2, SUB, 2 * C), F32)],
        scalars=1,
        flops=2_000_000_000,
    )
    lon_part = shifted(lon_part, 0, -1)
    lat_part = shifted(lat_part, -1, 0)
    diag_part = shifted(diag_part, -1, -1)
    whole = summed_everywhere(sums)
    merged, grad_tokens = call(
        finish_kernel,
        [((LEVS, ROWS // 2, COLS // 2, 2 * C), BF16), ((LEVS, ROWS, COLS, C), BF16)],
        (own, lat_part, lon_part, diag_part, merge_weight),
        [pltpu.VMEM((LEVS, ROWS, 2, SUB, 2 * C), F32)],
        flops=400_000_000,
    )
    grads = call(
        spread_kernel,
        [((C, 3 * C), BF16), ((C, C), BF16), ((C, FF), BF16), ((FF, C), BF16)],
        (whole,),
    )
    return (merged, grad_tokens, *grads)


def solution(mesh):
    cols, rows = mesh.devices.shape
    fine = Mesh(mesh.devices.reshape(cols // 4, 2, 2, rows // 2, 2), LON + LAT)
    cells = P(None, LAT, LON, None)
    placed = (
        cells,
        cells,
        P(),
        P(),
        P(),
        P(),
        P(),
        P(),
        P(LAT, None, None, None),
        P(),
        P(),
    )
    return jax.shard_map(
        per_device,
        mesh=fine,
        in_specs=placed,
        out_specs=(cells, cells, P(), P(), P(), P()),
        check_vma=False,
    )
```

```python
import math

import jax
import jax.numpy as jnp
from jax import lax
from jax.experimental import pallas as pl
from jax.experimental.pallas import tpu as pltpu
from jax.sharding import Mesh
from jax.sharding import PartitionSpec as P

C = 192
HEADS = 6
FF = 768
HEAD_DIM = 32
WLAT = 6
WLON = 12
LAT_PAD = 11
WTOK = 144
POS = 3312

ROWS = 12
COLS = 12
LEVS = 2
OFF = WLAT // 2
HALF = WLON // 2
SUB = 8
FRAME = LEVS * ROWS * 2 * SUB
BLOCK = FRAME // 4
STACK = HEADS * BLOCK
LOWS = 256
HIGHS = -(-POS // LOWS)

EPSILON = 1e-05
MASKED = -1000000000.0
F32 = jnp.float32
BF16 = jnp.bfloat16
VMEM_LIMIT = 56 * 1024 * 1024

LAT = ("y", "xl")
LON = ("z", "xh", "c")
NEAR = ("xh", "c", "xl")
FAR = ("y", "z")


def iota(shape, dim):
    return lax.broadcasted_iota(jnp.int32, shape, dim)


def product(left, right):
    return lax.dot_general(left, right, (((1,), (0,)), ((), ())), preferred_element_type=F32)


def across(left, right):
    return lax.dot_general(left, right, (((1,), (1,)), ((), ())), preferred_element_type=F32)


def crossed(left, right):
    return lax.dot_general(left, right, (((0,), (0,)), ((), ())), preferred_element_type=F32)


def pack_kernel(tok_ref, cot_ref, own_ref, lat_ref, lon_ref, diag_ref):
    both = jnp.concatenate(
        [ref[...].astype(F32).reshape(LEVS * ROWS * COLS, C) for ref in (tok_ref, cot_ref)], axis=-1
    ).astype(BF16)

    def pick(first, count, col):
        shape = (LEVS * count * SUB, LEVS * ROWS * COLS)
        to = iota(shape, 0)
        lev = jnp.where(to >= count * SUB, 1, 0)
        row = (to >> 3) - lev * count + first
        sub = jnp.bitwise_and(to, SUB - 1)
        hot = (iota(shape, 1) == (row * COLS + col + sub) * 2 + lev) & (sub < HALF)
        return product(hot.astype(F32).astype(BF16), both).astype(BF16)

    own_ref[...] = pick(0, ROWS - OFF, 0)
    lat_ref[...] = pick(ROWS - OFF, OFF, 0)
    lon_ref[...] = pick(0, ROWS - OFF, HALF)
    diag_ref[...] = pick(ROWS - OFF, OFF, HALF)


def prep_kernel(
    bits_ref,
    scale_ref,
    idx_ref,
    tab_ref,
    cq_ref,
    cp_ref,
    cu_ref,
    cd_ref,
    wq_ref,
    wp_ref,
    wu_ref,
    wd_ref,
    bias_ref,
    rows,
    places,
    found,
):
    def dequant(codes, layer, fan_in):
        limit = jnp.left_shift(1, bits_ref[layer] - 1) - 1
        clipped = jnp.minimum(jnp.maximum(codes, -limit), limit).astype(F32)
        whole = jnp.full((1, 128), scale_ref[layer], jnp.int32).astype(F32)
        return clipped * (math.sqrt(C / fan_in) / whole)[:, :1]

    full = dequant(cq_ref[...], 0, C)
    for part in range(3):
        wq_ref[part] = full[:, part * C : (part + 1) * C].astype(BF16)
    wp_ref[...] = dequant(cp_ref[...], 1, C).astype(BF16)
    wu_ref[...] = dequant(cu_ref[...], 2, C).astype(BF16)
    wd_ref[...] = dequant(cd_ref[...], 3, FF).astype(BF16)

    rows[...] = jnp.zeros_like(rows)
    for head in range(HEADS):
        table = tab_ref[head].astype(F32)
        for high in range(HIGHS):
            width = min(LOWS, POS - high * LOWS)
            rows[high * 16 + head * 2 : high * 16 + head * 2 + 2, 0:width] = table[
                :, high * LOWS : high * LOWS + width
            ]
    table = rows[...].astype(BF16)

    index = idx_ref[...]
    parts = [
        lax.shift_right_logical(index, 8).astype(F32).astype(BF16),
        jnp.bitwise_and(index, LOWS - 1).astype(F32).astype(BF16),
    ]

    def token(where):
        sub = jnp.bitwise_and(where, SUB - 1)
        inside = (where >> 4) * WLON + jnp.bitwise_and(where >> 3, 1) * HALF + sub
        return jnp.where((sub < HALF) & (where < BLOCK), inside, -1000)

    for lev in range(LEVS):
        base = (1 - lev) * (WTOK // 2)
        pick_q = (iota((BLOCK, WTOK), 1) == token(iota((BLOCK, WTOK), 0)) + base).astype(F32)
        pick_k = (iota((WTOK, 128), 0) == token(iota((WTOK, 128), 1)) + base).astype(F32)
        for i, part in enumerate(parts):
            moved = product(product(pick_q.astype(BF16), part).astype(BF16), pick_k.astype(BF16))
            places[i, lev * BLOCK : (lev + 1) * BLOCK, :] = moved

    entry = iota((LOWS, 128), 0).astype(F32)

    def eight(group, carry):
        at = pl.multiple_of(group * SUB, SUB)
        high = places[0, pl.ds(at, SUB), :]
        low = places[1, pl.ds(at, SUB), :]
        hot = [(entry == low[s : s + 1]).astype(F32).astype(BF16) for s in range(HALF)]
        values = product(table, jnp.concatenate(hot, axis=1))
        for s in range(HALF):
            chosen = jnp.zeros((16, 128), F32)
            here = jnp.broadcast_to(high[s : s + 1], (16, 128))
            for i in range(HIGHS):
                candidate = values[i * 16 : (i + 1) * 16, s * 128 : (s + 1) * 128]
                chosen = jnp.where(here == float(i), candidate, chosen)
            found[at + s] = chosen
        found[at + HALF] = jnp.zeros((16, 128), F32)
        found[at + HALF + 1] = jnp.zeros((16, 128), F32)
        return carry

    lax.fori_loop(0, LEVS * BLOCK // SUB, eight, 0, unroll=8)

    key = iota((BLOCK, 128), 1)
    for win in range(2):
        row = lax.axis_index(LAT) * ROWS - OFF + win * WLAT + (key >> 4)
        usable = (row >= 0) & (row < lax.axis_size(LAT) * ROWS - LAT_PAD)
        usable = usable & (jnp.bitwise_and(key, SUB - 1) < HALF) & (key < BLOCK)
        for lev in range(LEVS):
            for head in range(HEADS):
                values = found[lev * BLOCK : (lev + 1) * BLOCK, head * 2 + win, :]
                values = jnp.where(usable, values, MASKED)
                bias_ref[lev * 2 + win, head * BLOCK : (head + 1) * BLOCK, :] = values.astype(BF16)


def unit(values):
    center = values - jnp.mean(values, axis=-1, keepdims=True)
    spread = jnp.mean(center * center, axis=-1, keepdims=True)
    scale = lax.rsqrt(spread + EPSILON)
    return center * scale, scale


def unit_back(normal, scale, upstream):
    level = jnp.mean(upstream, axis=-1, keepdims=True)
    along = jnp.mean(upstream * normal, axis=-1, keepdims=True)
    return scale * (upstream - level - normal * along)


def main_kernel(
    own_ref,
    lat_part_ref,
    lon_part_ref,
    diag_part_ref,
    wq_ref,
    wp_ref,
    wu_ref,
    wd_ref,
    bias_ref,
    own_out,
    lat_out,
    lon_out,
    diag_out,
    sums_ref,
    frame,
):
    below = ROWS - OFF

    def piece(ref, rows):
        return ref[...].astype(F32).reshape(LEVS, rows, SUB, 2 * C)

    frame[:, OFF:, 1] = piece(own_ref, below)
    frame[:, :OFF, 1] = piece(lat_part_ref, OFF)
    frame[:, OFF:, 0] = piece(lon_part_ref, below)
    frame[:, :OFF, 0] = piece(diag_part_ref, OFF)
    both = frame[...].reshape(FRAME, 2 * C)

    place = iota((FRAME, C), 0)
    row = lax.axis_index(LAT) * ROWS - OFF + (place >> 4) - jnp.where(place >= FRAME // 2, ROWS, 0)
    valid = (row >= 0) & (row < lax.axis_size(LAT) * ROWS - LAT_PAD)
    valid = valid & (jnp.bitwise_and(place, SUB - 1) < HALF)
    start = jnp.where(valid, both[:, :C], 0.0)
    d_out = jnp.where(valid, both[:, C:], 0.0)
    d_out_low = d_out.astype(BF16)

    normal, scale = unit(start)
    normed = normal.astype(BF16)
    query = product(normed, wq_ref[0]).astype(BF16)
    key = product(normed, wq_ref[1]).astype(BF16)
    value = product(normed, wq_ref[2]).astype(BF16)

    lane_head = iota((HEADS, 1, C), 2) >> 5
    head_mask = lane_head == iota((HEADS, 1, C), 0)
    mask_low = head_mask.astype(F32).astype(BF16)
    mask_full = head_mask.astype(F32)

    def spread_heads(block):
        return (block[None] * mask_low).reshape(STACK, C)

    def join_heads(stacked):
        return jnp.sum(stacked.reshape(HEADS, BLOCK, C) * mask_full, axis=0)

    saved = []
    heads_parts = []
    for block in range(4):
        at = slice(block * BLOCK, (block + 1) * BLOCK)
        q_stack = spread_heads(query[at])
        scores = across(q_stack, key[at]) * HEAD_DIM ** (-0.5)
        scores = scores + bias_ref[block][:, :BLOCK].astype(F32)
        weights = jnp.exp(scores - jnp.max(scores, axis=-1, keepdims=True))
        weights = weights / jnp.sum(weights, axis=-1, keepdims=True)
        weights_low = weights.astype(BF16)
        heads_parts.append(join_heads(product(weights_low, value[at])))
        saved.append((q_stack, weights, weights_low))
    heads = jnp.concatenate(heads_parts, axis=0).astype(BF16)

    resid = (start + product(heads, wp_ref[...])).astype(BF16).astype(F32)
    normal_two, scale_two = unit(resid)
    normed_two = normal_two.astype(BF16)
    pre_act = product(normed_two, wu_ref[...])
    inner = math.sqrt(2 / math.pi)
    square = pre_act * pre_act
    bend = jnp.tanh(inner * (pre_act + 0.044715 * (square * pre_act)))
    half = 0.5 * (1.0 + bend)
    hidden = (pre_act * half).astype(BF16)
    slope = half + 0.5 * pre_act * (1.0 - bend * bend) * (
        inner * (1.0 + (3 * 0.044715) * square)
    )
    final = jnp.where(valid, resid + across(hidden, wd_ref[...]), 0.0)

    d_hidden = product(d_out_low, wd_ref[...]).astype(BF16).astype(F32)
    d_pre = (slope * d_hidden).astype(BF16)
    d_normed_two = across(d_pre, wu_ref[...]).astype(BF16).astype(F32)
    d_resid = (d_out + unit_back(normal_two, scale_two, d_normed_two)).astype(BF16)
    d_heads = across(d_resid, wp_ref[...]).astype(BF16)

    dq_parts = []
    dk_parts = []
    dv_parts = []
    for block in range(4):
        at = slice(block * BLOCK, (block + 1) * BLOCK)
        q_stack, weights, weights_low = saved[block]
        d_stack = spread_heads(d_heads[at])
        d_weights = across(d_stack, value[at]).astype(BF16).astype(F32)
        dv_parts.append(crossed(weights_low, d_stack))
        inside = jnp.sum(weights * d_weights, axis=-1, keepdims=True)
        d_scores = (weights * (d_weights - inside) * HEAD_DIM ** (-0.5)).astype(BF16)
        dq_parts.append(join_heads(product(d_scores, key[at])))
        dk_parts.append(crossed(d_scores, q_stack))
    d_query = jnp.concatenate(dq_parts, axis=0).astype(BF16)
    d_key = jnp.concatenate(dk_parts, axis=0).astype(BF16)
    d_value = jnp.concatenate(dv_parts, axis=0).astype(BF16)

    d_normed = across(d_query, wq_ref[0]) + across(d_key, wq_ref[1]) + across(d_value, wq_ref[2])
    d_normed = d_normed.astype(BF16).astype(F32)
    grad = jnp.where(valid, d_resid.astype(F32) + unit_back(normal, scale, d_normed), 0.0)

    result = jnp.concatenate([final, grad], axis=-1).reshape(LEVS, ROWS, 2, SUB, 2 * C)

    def flat(part):
        return part.reshape(-1, 2 * C).astype(BF16)

    own_out[...] = flat(result[:, OFF:, 1])
    lat_out[...] = flat(result[:, :OFF, 1])
    lon_out[...] = flat(result[:, OFF:, 0])
    diag_out[...] = flat(result[:, :OFF, 0])

    small = [
        crossed(normed, d_query),
        crossed(normed, d_key),
        crossed(normed, d_value),
        crossed(heads, d_resid),
    ]
    tiles = [total[:, :128] for total in small]
    tiles += [
        jnp.concatenate([small[i][:, 128:], small[i + 1][:, 128:]], axis=-1) for i in (0, 2)
    ]
    for wide in (crossed(normed_two, d_pre), crossed(d_out_low, hidden)):
        tiles += [wide[:, i * 128 : (i + 1) * 128] for i in range(6)]
    for i, tile in enumerate(tiles):
        sums_ref[i * C : (i + 1) * C, :] = tile.astype(BF16)


def spread_kernel(sums_ref, qkv_ref, proj_ref, up_ref, down_ref):
    def tile(i):
        return sums_ref[i * C : (i + 1) * C, :].astype(F32)

    ends = [tile(4)[:, :64], tile(4)[:, 64:], tile(5)[:, :64], tile(5)[:, 64:]]
    small = [jnp.concatenate([tile(i), ends[i]], axis=-1) for i in range(4)]
    qkv_ref[...] = jnp.concatenate(small[:3], axis=-1).astype(BF16)
    proj_ref[...] = small[3].astype(BF16)
    for i in range(6):
        up_ref[:, i * 128 : (i + 1) * 128] = sums_ref[(6 + i) * C : (7 + i) * C, :]
        down_ref[:, i * 128 : (i + 1) * 128] = sums_ref[(12 + i) * C : (13 + i) * C, :]


def finish_kernel(
    own_ref, lat_ref, lon_ref, diag_ref, weight_ref, merged_ref, grad_ref, frame
):
    above = ROWS - OFF

    def piece(ref, rows):
        return ref[...].astype(F32).reshape(LEVS, rows, SUB, 2 * C)

    frame[:, :above, 0] = piece(own_ref, above)
    frame[:, above:, 0] = piece(lat_ref, OFF)
    frame[:, :above, 1] = piece(lon_ref, above)
    frame[:, above:, 1] = piece(diag_ref, OFF)
    both = frame[...].reshape(FRAME, 2 * C)
    final = both[:, :C].astype(BF16)
    grad = both[:, C:].astype(BF16)

    def source(col):
        return jnp.where(col >= HALF, col + (SUB - HALF), col)

    to = iota((FRAME, FRAME), 0)
    col = jnp.bitwise_and(to, 15)
    pick = (iota((FRAME, FRAME), 1) == to - col + source(col)) & (col < COLS)
    moved = product(pick.astype(F32).astype(BF16), grad).reshape(LEVS, ROWS, 16, C)
    grad_ref[...] = moved[:, :, :COLS, :].astype(BF16)

    count = LEVS * (ROWS // 2) * SUB
    to = iota((count, FRAME), 0)
    lev = jnp.where(to >= count // 2, 1, 0)
    pair = (to >> 3) - lev * (ROWS // 2)
    parts = []
    for down in range(2):
        for right in range(2):
            col = 2 * jnp.bitwise_and(to, SUB - 1) + right
            wanted = lev * (FRAME // 2) + (2 * pair + down) * 16 + source(col)
            pick = (iota((count, FRAME), 1) == wanted) & (col < COLS)
            parts.append(product(pick.astype(F32).astype(BF16), final))
    width = 4 * C
    mean = sum(jnp.sum(part, axis=-1, keepdims=True) for part in parts) / width
    centers = [part - mean for part in parts]
    spread = sum(jnp.sum(part * part, axis=-1, keepdims=True) for part in centers) / width
    scale = lax.rsqrt(spread + EPSILON)
    total = jnp.zeros((count, 2 * C), F32)
    for i, part in enumerate(centers):
        total = total + product((part * scale).astype(BF16), weight_ref[i * C : (i + 1) * C, :])
    merged_ref[...] = total.reshape(LEVS, ROWS // 2, SUB, 2 * C)[:, :, :HALF, :].astype(BF16)


def call(kernel, outs, args, scratch=(), scalars=0, flops=0):
    vmem = pl.BlockSpec(memory_space=pltpu.VMEM)
    smem = pl.BlockSpec(memory_space=pltpu.SMEM)
    moved = sum(math.prod(a.shape) * a.dtype.itemsize for a in args)
    moved += sum(math.prod(s) * jnp.dtype(t).itemsize for s, t in outs)
    return pl.pallas_call(
        kernel,
        out_shape=[jax.ShapeDtypeStruct(s, t) for s, t in outs],
        in_specs=[smem] * scalars + [vmem] * (len(args) - scalars),
        out_specs=[vmem] * len(outs),
        scratch_shapes=list(scratch),
        compiler_params=pltpu.CompilerParams(vmem_limit_bytes=VMEM_LIMIT),
        cost_estimate=pl.CostEstimate(flops=flops, bytes_accessed=moved, transcendentals=0),
    )(*args)


def shifted(block, lat_step, lon_step):
    rows = lax.axis_size(LAT)
    cols = lax.axis_size(LON)
    if lat_step and lon_step:
        route = [
            (col * rows + row, (col + lon_step) % cols * rows + row + lat_step)
            for col in range(cols)
            for row in range(rows)
            if 0 <= row + lat_step < rows
        ]
        return lax.ppermute(block, LON + LAT, route)
    if lat_step:
        route = [(r, r + lat_step) for r in range(rows) if 0 <= r + lat_step < rows]
        return lax.ppermute(block, LAT, route)
    return lax.ppermute(block, LON, [(c, (c + lon_step) % cols) for c in range(cols)])


def exchange(parts, axes):
    return lax.all_to_all(parts, axes, 0, 0)


def total_of(parts):
    return jnp.sum(parts.astype(F32), axis=0).astype(BF16)


def summed_everywhere(sums, moved):
    near = lax.axis_size(NEAR)
    far = lax.axis_size(FAR)
    rows = sums.shape[0] // near
    padded = -(-rows // (8 * far)) * (8 * far)
    part = exchange(sums.reshape(near, rows, 128), NEAR)
    part, moved = lax.optimization_barrier((part, moved))
    part = jnp.pad(total_of(part), ((0, padded - rows), (0, 0)))
    part = total_of(exchange(part.reshape(far, padded // far, 128), FAR))
    part = exchange(jnp.broadcast_to(part[None], (far,) + part.shape), FAR)
    part = part.reshape(padded, 128)[:rows]
    part, moved = lax.optimization_barrier((part, moved))
    whole = exchange(jnp.broadcast_to(part[None], (near,) + part.shape), NEAR)
    return whole.reshape(near * rows, 128), moved


def per_device(
    tokens,
    cotangent,
    qkv_codes,
    proj_codes,
    up_codes,
    down_codes,
    bit_widths,
    quant_scales,
    bias_table,
    bias_index,
    merge_weight,
):
    big = ROWS - OFF
    big_shape = (LEVS * big * SUB, 2 * C)
    thin_shape = (LEVS * OFF * SUB, 2 * C)
    pieces = [(big_shape, BF16), (thin_shape, BF16), (big_shape, BF16), (thin_shape, BF16)]
    own, lat_part, lon_part, diag_part = call(
        pack_kernel,
        pieces,
        (tokens.transpose(1, 2, 0, 3), cotangent.transpose(1, 2, 0, 3)),
    )
    lon_part = shifted(lon_part, 0, 1)
    lat_part = shifted(lat_part, 1, 0)
    diag_part = shifted(diag_part, 1, 1)

    w_qkv, w_proj, w_up, w_down, bias = call(
        prep_kernel,
        [
            ((3, C, C), BF16),
            ((C, C), BF16),
            ((C, FF), BF16),
            ((C, FF), BF16),
            ((4, STACK, 128), BF16),
        ],
        (
            bit_widths,
            quant_scales,
            bias_index.reshape(WTOK, WTOK),
            bias_table.transpose(1, 2, 0, 3).reshape(HEADS, 2, POS),
            qkv_codes,
            proj_codes,
            up_codes,
            down_codes.T,
        ),
        [
            pltpu.VMEM((HIGHS * 16, LOWS), F32),
            pltpu.VMEM((2, LEVS * BLOCK, 128), F32),
            pltpu.VMEM((LEVS * BLOCK, 16, 128), F32),
        ],
        scalars=2,
        flops=2_000_000_000,
    )
    own, lat_part, lon_part, diag_part, sums = call(
        main_kernel,
        pieces + [((18 * C, 128), BF16)],
        (own, lat_part, lon_part, diag_part, w_qkv, w_proj, w_up, w_down, bias),
        [pltpu.VMEM((LEVS, ROWS, 2, SUB, 2 * C), F32)],
        flops=2_000_000_000,
    )
    lon_part = shifted(lon_part, 0, -1)
    lat_part = shifted(lat_part, -1, 0)
    diag_part = shifted(diag_part, -1, -1)
    whole, moved = summed_everywhere(sums, (own, lat_part, lon_part, diag_part))
    merged, grad_tokens = call(
        finish_kernel,
        [((LEVS, ROWS // 2, COLS // 2, 2 * C), BF16), ((LEVS, ROWS, COLS, C), BF16)],
        (*moved, merge_weight),
        [pltpu.VMEM((LEVS, ROWS, 2, SUB, 2 * C), F32)],
        flops=400_000_000,
    )
    qkv, proj, up, down = call(
        spread_kernel,
        [((C, 3 * C), BF16), ((C, C), BF16), ((C, FF), BF16), ((C, FF), BF16)],
        (whole,),
    )
    return (merged, grad_tokens, qkv, proj, up, down.T)


def solution(mesh):
    cols, rows = mesh.devices.shape
    fine = Mesh(mesh.devices.reshape(cols // 4, 2, 2, rows // 2, 2), LON + LAT)
    cells = P(None, LAT, LON, None)
    placed = (
        cells,
        cells,
        P(),
        P(),
        P(),
        P(),
        P(),
        P(),
        P(LAT, None, None, None),
        P(),
        P(),
    )
    return jax.shard_map(
        per_device,
        mesh=fine,
        in_specs=placed,
        out_specs=(cells, cells, P(), P(), P(), P()),
        check_vma=False,
    )
```

```python
import math

import jax
import jax.numpy as jnp
from jax import lax
from jax.experimental import pallas as pl
from jax.experimental.pallas import tpu as pltpu
from jax.sharding import Mesh
from jax.sharding import PartitionSpec as P

C = 192
HEADS = 6
FF = 768
HEAD_DIM = 32
WLAT = 6
WLON = 12
LAT_PAD = 11
WTOK = 144
POS = 3312

ROWS = 12
COLS = 12
LEVS = 2
OFF = WLAT // 2
HALF = WLON // 2
SUB = 8
FRAME = LEVS * ROWS * 2 * SUB
BLOCK = FRAME // 4
STACK = HEADS * BLOCK
BIG = LEVS * (ROWS - OFF) * SUB
THIN = LEVS * OFF * SUB
LOWS = 256
HIGHS = -(-POS // LOWS)

EPSILON = 1e-05
MASKED = -1000000000.0
F32 = jnp.float32
BF16 = jnp.bfloat16

LAT = ("y", "xl")
LON = ("z", "xh", "c")
NEAR = ("xh", "c", "xl")
FAR = ("y", "z")


def iota(shape, dim):
    return lax.broadcasted_iota(jnp.int32, shape, dim)


def product(left, right):
    return lax.dot_general(left, right, (((1,), (0,)), ((), ())), preferred_element_type=F32)


def across(left, right):
    return lax.dot_general(left, right, (((1,), (1,)), ((), ())), preferred_element_type=F32)


def crossed(left, right):
    return lax.dot_general(left, right, (((0,), (0,)), ((), ())), preferred_element_type=F32)


def pack_kernel(tok_ref, cot_ref, own_ref, low_ref, side_ref):
    both = jnp.concatenate(
        [ref[...].astype(F32).reshape(LEVS * ROWS * COLS, C) for ref in (tok_ref, cot_ref)], axis=-1
    ).astype(BF16)

    def pick(first, count, col):
        shape = (LEVS * count * SUB, LEVS * ROWS * COLS)
        to = iota(shape, 0)
        lev = jnp.where(to >= count * SUB, 1, 0)
        row = (to >> 3) - lev * count + first
        sub = jnp.bitwise_and(to, SUB - 1)
        hot = (iota(shape, 1) == (row * COLS + col + sub) * 2 + lev) & (sub < HALF)
        return product(hot.astype(F32).astype(BF16), both).astype(BF16)

    own_ref[...] = pick(0, ROWS - OFF, 0)
    low_ref[...] = pick(ROWS - OFF, OFF, 0)
    side_ref[0:BIG, :] = pick(0, ROWS - OFF, HALF)
    side_ref[BIG:, :] = pick(ROWS - OFF, OFF, HALF)


def weight_kernel(
    bits_ref, scale_ref, cq_ref, cp_ref, cu_ref, cd_ref, wq_ref, wp_ref, wu_ref, wd_ref
):
    def dequant(codes, layer, fan_in):
        limit = jnp.left_shift(1, bits_ref[layer] - 1) - 1
        clipped = jnp.minimum(jnp.maximum(codes, -limit), limit).astype(F32)
        whole = jnp.full((1, 128), scale_ref[layer], jnp.int32).astype(F32)
        return clipped * (math.sqrt(C / fan_in) / whole)[:, :1]

    full = dequant(cq_ref[...], 0, C)
    for part in range(3):
        wq_ref[part] = full[:, part * C : (part + 1) * C].astype(BF16)
    wp_ref[...] = dequant(cp_ref[...], 1, C).astype(BF16)
    wu_ref[...] = dequant(cu_ref[...], 2, C).astype(BF16)
    wd_ref[...] = dequant(cd_ref[...], 3, FF).astype(BF16)


def bias_kernel(idx_ref, tab_ref, bias_ref, rows, places, found):
    rows[...] = jnp.zeros_like(rows)
    for head in range(HEADS):
        table = tab_ref[head].astype(F32)
        for high in range(HIGHS):
            width = min(LOWS, POS - high * LOWS)
            rows[high * 16 + head * 2 : high * 16 + head * 2 + 2, 0:width] = table[
                :, high * LOWS : high * LOWS + width
            ]
    table = rows[...].astype(BF16)

    index = idx_ref[...]
    parts = [
        lax.shift_right_logical(index, 8).astype(F32).astype(BF16),
        jnp.bitwise_and(index, LOWS - 1).astype(F32).astype(BF16),
    ]

    def token(where):
        sub = jnp.bitwise_and(where, SUB - 1)
        inside = (where >> 4) * WLON + jnp.bitwise_and(where >> 3, 1) * HALF + sub
        return jnp.where((sub < HALF) & (where < BLOCK), inside, -1000)

    for lev in range(LEVS):
        base = (1 - lev) * (WTOK // 2)
        pick_q = (iota((BLOCK, WTOK), 1) == token(iota((BLOCK, WTOK), 0)) + base).astype(F32)
        pick_k = (iota((WTOK, 128), 0) == token(iota((WTOK, 128), 1)) + base).astype(F32)
        for i, part in enumerate(parts):
            moved = product(product(pick_q.astype(BF16), part).astype(BF16), pick_k.astype(BF16))
            places[i, lev * BLOCK : (lev + 1) * BLOCK, :] = moved

    entry = iota((LOWS, 128), 0).astype(F32)

    def eight(group, carry):
        at = pl.multiple_of(group * SUB, SUB)
        high = places[0, pl.ds(at, SUB), :]
        low = places[1, pl.ds(at, SUB), :]
        hot = [(entry == low[s : s + 1]).astype(F32).astype(BF16) for s in range(HALF)]
        values = product(table, jnp.concatenate(hot, axis=1))
        for s in range(HALF):
            chosen = jnp.zeros((16, 128), F32)
            here = jnp.broadcast_to(high[s : s + 1], (16, 128))
            for i in range(HIGHS):
                candidate = values[i * 16 : (i + 1) * 16, s * 128 : (s + 1) * 128]
                chosen = jnp.where(here == float(i), candidate, chosen)
            found[at + s] = chosen
        found[at + HALF] = jnp.zeros((16, 128), F32)
        found[at + HALF + 1] = jnp.zeros((16, 128), F32)
        return carry

    lax.fori_loop(0, LEVS * BLOCK // SUB, eight, 0, unroll=8)

    key = iota((BLOCK, 128), 1)
    for win in range(2):
        row = lax.axis_index(LAT) * ROWS - OFF + win * WLAT + (key >> 4)
        usable = (row >= 0) & (row < lax.axis_size(LAT) * ROWS - LAT_PAD)
        usable = usable & (jnp.bitwise_and(key, SUB - 1) < HALF) & (key < BLOCK)
        for lev in range(LEVS):
            for head in range(HEADS):
                values = found[lev * BLOCK : (lev + 1) * BLOCK, head * 2 + win, :]
                values = jnp.where(usable, values, MASKED)
                bias_ref[lev * 2 + win, head * BLOCK : (head + 1) * BLOCK, :] = values.astype(BF16)


def unit(values):
    center = values - jnp.mean(values, axis=-1, keepdims=True)
    spread = jnp.mean(center * center, axis=-1, keepdims=True)
    scale = lax.rsqrt(spread + EPSILON)
    return center * scale, scale


def unit_back(normal, scale, upstream):
    level = jnp.mean(upstream, axis=-1, keepdims=True)
    along = jnp.mean(upstream * normal, axis=-1, keepdims=True)
    return scale * (upstream - level - normal * along)


def main_kernel(
    own_ref,
    side_ref,
    edge_ref,
    wq_ref,
    wp_ref,
    wu_ref,
    wd_ref,
    bias_ref,
    own_out,
    side_out,
    edge_out,
    sums_ref,
    frame,
):
    below = ROWS - OFF

    def piece(block, rows):
        return block.astype(F32).reshape(LEVS, rows, SUB, 2 * C)

    frame[:, OFF:, 1] = piece(own_ref[...], below)
    frame[:, OFF:, 0] = piece(side_ref[0:BIG, :], below)
    frame[:, :OFF, 1] = piece(edge_ref[0:THIN, :], OFF)
    frame[:, :OFF, 0] = piece(edge_ref[THIN:, :], OFF)
    both = frame[...].reshape(FRAME, 2 * C)

    place = iota((FRAME, C), 0)
    row = lax.axis_index(LAT) * ROWS - OFF + (place >> 4) - jnp.where(place >= FRAME // 2, ROWS, 0)
    valid = (row >= 0) & (row < lax.axis_size(LAT) * ROWS - LAT_PAD)
    valid = valid & (jnp.bitwise_and(place, SUB - 1) < HALF)
    start = jnp.where(valid, both[:, :C], 0.0)
    d_out = jnp.where(valid, both[:, C:], 0.0)
    d_out_low = d_out.astype(BF16)

    normal, scale = unit(start)
    normed = normal.astype(BF16)
    query = product(normed, wq_ref[0]).astype(BF16)
    key = product(normed, wq_ref[1]).astype(BF16)
    value = product(normed, wq_ref[2]).astype(BF16)

    lane_head = iota((HEADS, 1, C), 2) >> 5
    head_mask = lane_head == iota((HEADS, 1, C), 0)
    mask_low = head_mask.astype(F32).astype(BF16)
    mask_full = head_mask.astype(F32)

    def spread_heads(block):
        return (block[None] * mask_low).reshape(STACK, C)

    def join_heads(stacked):
        return jnp.sum(stacked.reshape(HEADS, BLOCK, C) * mask_full, axis=0)

    saved = []
    heads_parts = []
    for block in range(4):
        at = slice(block * BLOCK, (block + 1) * BLOCK)
        q_stack = spread_heads(query[at])
        scores = across(q_stack, key[at]) * HEAD_DIM ** (-0.5)
        scores = scores + bias_ref[block][:, :BLOCK].astype(F32)
        weights = jnp.exp(scores - jnp.max(scores, axis=-1, keepdims=True))
        weights = weights / jnp.sum(weights, axis=-1, keepdims=True)
        weights_low = weights.astype(BF16)
        heads_parts.append(join_heads(product(weights_low, value[at])))
        saved.append((q_stack, weights, weights_low))
    heads = jnp.concatenate(heads_parts, axis=0).astype(BF16)

    resid = (start + product(heads, wp_ref[...])).astype(BF16).astype(F32)
    normal_two, scale_two = unit(resid)
    normed_two = normal_two.astype(BF16)
    pre_act = product(normed_two, wu_ref[...])
    inner = math.sqrt(2 / math.pi)
    square = pre_act * pre_act
    bend = jnp.tanh(inner * (pre_act + 0.044715 * (square * pre_act)))
    half = 0.5 * (1.0 + bend)
    hidden = (pre_act * half).astype(BF16)
    slope = half + 0.5 * pre_act * (1.0 - bend * bend) * (
        inner * (1.0 + (3 * 0.044715) * square)
    )
    final = jnp.where(valid, resid + across(hidden, wd_ref[...]), 0.0)

    d_hidden = product(d_out_low, wd_ref[...]).astype(BF16).astype(F32)
    d_pre = (slope * d_hidden).astype(BF16)
    d_normed_two = across(d_pre, wu_ref[...]).astype(BF16).astype(F32)
    d_resid = (d_out + unit_back(normal_two, scale_two, d_normed_two)).astype(BF16)
    d_heads = across(d_resid, wp_ref[...]).astype(BF16)

    dq_parts = []
    dk_parts = []
    dv_parts = []
    for block in range(4):
        at = slice(block * BLOCK, (block + 1) * BLOCK)
        q_stack, weights, weights_low = saved[block]
        d_stack = spread_heads(d_heads[at])
        d_weights = across(d_stack, value[at]).astype(BF16).astype(F32)
        dv_parts.append(crossed(weights_low, d_stack))
        inside = jnp.sum(weights * d_weights, axis=-1, keepdims=True)
        d_scores = (weights * (d_weights - inside) * HEAD_DIM ** (-0.5)).astype(BF16)
        dq_parts.append(join_heads(product(d_scores, key[at])))
        dk_parts.append(crossed(d_scores, q_stack))
    d_query = jnp.concatenate(dq_parts, axis=0).astype(BF16)
    d_key = jnp.concatenate(dk_parts, axis=0).astype(BF16)
    d_value = jnp.concatenate(dv_parts, axis=0).astype(BF16)

    d_normed = across(d_query, wq_ref[0]) + across(d_key, wq_ref[1]) + across(d_value, wq_ref[2])
    d_normed = d_normed.astype(BF16).astype(F32)
    grad = jnp.where(valid, d_resid.astype(F32) + unit_back(normal, scale, d_normed), 0.0)

    result = jnp.concatenate([final, grad], axis=-1).reshape(LEVS, ROWS, 2, SUB, 2 * C)

    def flat(part):
        return part.reshape(-1, 2 * C).astype(BF16)

    own_out[...] = flat(result[:, OFF:, 1])
    side_out[...] = flat(result[:, OFF:, 0])
    edge_out[0:THIN, :] = flat(result[:, :OFF, 1])
    edge_out[THIN:, :] = flat(result[:, :OFF, 0])

    small = [
        crossed(normed, d_query),
        crossed(normed, d_key),
        crossed(normed, d_value),
        crossed(heads, d_resid),
    ]
    tiles = [total[:, :128] for total in small]
    tiles += [
        jnp.concatenate([small[i][:, 128:], small[i + 1][:, 128:]], axis=-1) for i in (0, 2)
    ]
    for wide in (crossed(normed_two, d_pre), crossed(d_out_low, hidden)):
        tiles += [wide[:, i * 128 : (i + 1) * 128] for i in range(6)]
    for i, tile in enumerate(tiles):
        sums_ref[i * C : (i + 1) * C, :] = tile.astype(BF16)


def spread_kernel(sums_ref, qkv_ref, proj_ref, up_ref, down_ref):
    def tile(i):
        return sums_ref[i * C : (i + 1) * C, :].astype(F32)

    ends = [tile(4)[:, :64], tile(4)[:, 64:], tile(5)[:, :64], tile(5)[:, 64:]]
    small = [jnp.concatenate([tile(i), ends[i]], axis=-1) for i in range(4)]
    qkv_ref[...] = jnp.concatenate(small[:3], axis=-1).astype(BF16)
    proj_ref[...] = small[3].astype(BF16)
    for i in range(6):
        up_ref[:, i * 128 : (i + 1) * 128] = sums_ref[(6 + i) * C : (7 + i) * C, :]
        down_ref[:, i * 128 : (i + 1) * 128] = sums_ref[(12 + i) * C : (13 + i) * C, :]


def finish_kernel(own_ref, edge_ref, side_ref, weight_ref, merged_ref, grad_ref, frame):
    above = ROWS - OFF

    def piece(block, rows):
        return block.astype(F32).reshape(LEVS, rows, SUB, 2 * C)

    frame[:, :above, 0] = piece(own_ref[...], above)
    frame[:, above:, 0] = piece(edge_ref[0:THIN, :], OFF)
    frame[:, :above, 1] = piece(side_ref[0:BIG, :], above)
    frame[:, above:, 1] = piece(side_ref[BIG:, :], OFF)
    both = frame[...].reshape(FRAME, 2 * C)
    final = both[:, :C].astype(BF16)
    grad = both[:, C:].astype(BF16)

    def source(col):
        return jnp.where(col >= HALF, col + (SUB - HALF), col)

    to = iota((FRAME, FRAME), 0)
    col = jnp.bitwise_and(to, 15)
    pick = (iota((FRAME, FRAME), 1) == to - col + source(col)) & (col < COLS)
    moved = product(pick.astype(F32).astype(BF16), grad).reshape(LEVS, ROWS, 16, C)
    grad_ref[...] = moved[:, :, :COLS, :].astype(BF16)

    count = LEVS * (ROWS // 2) * SUB
    to = iota((count, FRAME), 0)
    lev = jnp.where(to >= count // 2, 1, 0)
    pair = (to >> 3) - lev * (ROWS // 2)
    parts = []
    for down in range(2):
        for right in range(2):
            col = 2 * jnp.bitwise_and(to, SUB - 1) + right
            wanted = lev * (FRAME // 2) + (2 * pair + down) * 16 + source(col)
            pick = (iota((count, FRAME), 1) == wanted) & (col < COLS)
            parts.append(product(pick.astype(F32).astype(BF16), final))
    width = 4 * C
    mean = sum(jnp.sum(part, axis=-1, keepdims=True) for part in parts) / width
    centers = [part - mean for part in parts]
    spread = sum(jnp.sum(part * part, axis=-1, keepdims=True) for part in centers) / width
    scale = lax.rsqrt(spread + EPSILON)
    total = jnp.zeros((count, 2 * C), F32)
    for i, part in enumerate(centers):
        total = total + product((part * scale).astype(BF16), weight_ref[i * C : (i + 1) * C, :])
    merged_ref[...] = total.reshape(LEVS, ROWS // 2, SUB, 2 * C)[:, :, :HALF, :].astype(BF16)


def call(kernel, outs, args, scratch=(), scalars=0, flops=0, mib=16):
    vmem = pl.BlockSpec(memory_space=pltpu.VMEM)
    smem = pl.BlockSpec(memory_space=pltpu.SMEM)
    moved = sum(math.prod(a.shape) * a.dtype.itemsize for a in args)
    moved += sum(math.prod(s) * jnp.dtype(t).itemsize for s, t in outs)
    return pl.pallas_call(
        kernel,
        out_shape=[jax.ShapeDtypeStruct(s, t) for s, t in outs],
        in_specs=[smem] * scalars + [vmem] * (len(args) - scalars),
        out_specs=[vmem] * len(outs),
        scratch_shapes=list(scratch),
        compiler_params=pltpu.CompilerParams(vmem_limit_bytes=mib * 1024 * 1024),
        cost_estimate=pl.CostEstimate(flops=flops, bytes_accessed=moved, transcendentals=0),
    )(*args)


def shifted(block, axes, step):
    count = lax.axis_size(axes)
    if axes == LAT:
        route = [(i, i + step) for i in range(count) if 0 <= i + step < count]
    else:
        route = [(i, (i + step) % count) for i in range(count)]
    return lax.ppermute(block, axes, route)


def exchange(parts, axes):
    return lax.all_to_all(parts, axes, 0, 0)


def total_of(parts):
    return jnp.sum(parts.astype(F32), axis=0).astype(BF16)


def copies(part, count):
    def kernel(part_ref, out_ref):
        for i in range(count):
            out_ref[i] = part_ref[...]

    return call(kernel, [((count,) + part.shape, BF16)], (part,))[0]


def summed_everywhere(sums, own, edge, side):
    near = lax.axis_size(NEAR)
    far = lax.axis_size(FAR)
    rows = sums.shape[0] // near
    padded = -(-rows // (8 * far)) * (8 * far)
    edge = shifted(edge, LAT, -1)
    part = exchange(sums.reshape(near, rows, 128), NEAR)
    part, edge = lax.optimization_barrier((part, edge))
    side = shifted(jnp.concatenate([side, edge[THIN:]], axis=0), LON, -1)
    part = jnp.pad(total_of(part), ((0, padded - rows), (0, 0)))
    part = exchange(part.reshape(far, padded // far, 128), FAR)
    part, side = lax.optimization_barrier((part, side))
    part = exchange(jnp.broadcast_to(total_of(part)[None], part.shape), FAR)
    part = part.reshape(padded, 128)[:rows]
    part, moved = lax.optimization_barrier((part, (own, edge, side)))
    whole = exchange(copies(part, near), NEAR)
    return whole.reshape(near * rows, 128), moved


def per_device(
    tokens,
    cotangent,
    qkv_codes,
    proj_codes,
    up_codes,
    down_codes,
    bit_widths,
    quant_scales,
    bias_table,
    bias_index,
    merge_weight,
):
    own, low, side = call(
        pack_kernel,
        [((BIG, 2 * C), BF16), ((THIN, 2 * C), BF16), ((BIG + THIN, 2 * C), BF16)],
        (tokens.transpose(1, 2, 0, 3), cotangent.transpose(1, 2, 0, 3)),
    )
    side = shifted(side, LON, 1)
    (bias,) = call(
        bias_kernel,
        [((4, STACK, 128), BF16)],
        (
            bias_index.reshape(WTOK, WTOK),
            bias_table.transpose(1, 2, 0, 3).reshape(HEADS, 2, POS),
        ),
        [
            pltpu.VMEM((HIGHS * 16, LOWS), F32),
            pltpu.VMEM((2, LEVS * BLOCK, 128), F32),
            pltpu.VMEM((LEVS * BLOCK, 16, 128), F32),
        ],
        flops=2_000_000_000,
    )
    edge = jnp.concatenate([low, side[BIG:]], axis=0)
    edge, bias, codes = lax.optimization_barrier(
        (edge, bias, (qkv_codes, proj_codes, up_codes, down_codes.T))
    )
    edge = shifted(edge, LAT, 1)
    weights = call(
        weight_kernel,
        [((3, C, C), BF16), ((C, C), BF16), ((C, FF), BF16), ((C, FF), BF16)],
        (bit_widths, quant_scales, *codes),
        scalars=2,
        flops=1_000_000_000,
    )
    own, side, edge, sums = call(
        main_kernel,
        [
            ((BIG, 2 * C), BF16),
            ((BIG, 2 * C), BF16),
            ((2 * THIN, 2 * C), BF16),
            ((18 * C, 128), BF16),
        ],
        (own, side, edge, *weights, bias),
        [pltpu.VMEM((LEVS, ROWS, 2, SUB, 2 * C), F32)],
        flops=2_000_000_000,
        mib=32,
    )
    whole, moved = summed_everywhere(sums, own, edge, side)
    merged, grad_tokens = call(
        finish_kernel,
        [((LEVS, ROWS // 2, COLS // 2, 2 * C), BF16), ((LEVS, ROWS, COLS, C), BF16)],
        (*moved, merge_weight),
        [pltpu.VMEM((LEVS, ROWS, 2, SUB, 2 * C), F32)],
        flops=400_000_000,
    )
    qkv, proj, up, down = call(
        spread_kernel,
        [((C, 3 * C), BF16), ((C, C), BF16), ((C, FF), BF16), ((C, FF), BF16)],
        (whole,),
    )
    return (merged, grad_tokens, qkv, proj, up, down.T)


def solution(mesh):
    cols, rows = mesh.devices.shape
    fine = Mesh(mesh.devices.reshape(cols // 4, 2, 2, rows // 2, 2), LON + LAT)
    cells = P(None, LAT, LON, None)
    placed = (
        cells,
        cells,
        P(),
        P(),
        P(),
        P(),
        P(),
        P(),
        P(LAT, None, None, None),
        P(),
        P(),
    )
    return jax.shard_map(
        per_device,
        mesh=fine,
        in_specs=placed,
        out_specs=(cells, cells, P(), P(), P(), P()),
        check_vma=False,
    )
```

```python
import math

import jax
import jax.numpy as jnp
from jax import lax
from jax.experimental import pallas as pl
from jax.experimental.pallas import tpu as pltpu
from jax.sharding import Mesh
from jax.sharding import PartitionSpec as P

C = 192
HEADS = 6
FF = 768
HEAD_DIM = 32
WLAT = 6
WLON = 12
LAT_PAD = 11
WTOK = 144
POS = 3312

ROWS = 12
COLS = 12
LEVS = 2
OFF = WLAT // 2
HALF = WLON // 2
SUB = 8
FRAME = LEVS * ROWS * 2 * SUB
BLOCK = FRAME // 4
STACK = HEADS * BLOCK
BIG = LEVS * (ROWS - OFF) * SUB
THIN = LEVS * OFF * SUB
LOWS = 256
HIGHS = -(-POS // LOWS)

EPSILON = 1e-05
MASKED = -1000000000.0
F32 = jnp.float32
BF16 = jnp.bfloat16

LAT = ("y", "xl")
LON = ("z", "xh", "c")
NEAR = ("xh", "xl")
FAR = ("y", "z")


def iota(shape, dim):
    return lax.broadcasted_iota(jnp.int32, shape, dim)


def product(left, right):
    return lax.dot_general(left, right, (((1,), (0,)), ((), ())), preferred_element_type=F32)


def across(left, right):
    return lax.dot_general(left, right, (((1,), (1,)), ((), ())), preferred_element_type=F32)


def crossed(left, right):
    return lax.dot_general(left, right, (((0,), (0,)), ((), ())), preferred_element_type=F32)


def pack_kernel(tok_ref, cot_ref, own_ref, low_ref, side_ref):
    both = jnp.concatenate(
        [ref[...].astype(F32).reshape(LEVS * ROWS * COLS, C) for ref in (tok_ref, cot_ref)], axis=-1
    ).astype(BF16)

    def pick(first, count, col):
        shape = (LEVS * count * SUB, LEVS * ROWS * COLS)
        to = iota(shape, 0)
        lev = jnp.where(to >= count * SUB, 1, 0)
        row = (to >> 3) - lev * count + first
        sub = jnp.bitwise_and(to, SUB - 1)
        hot = (iota(shape, 1) == (row * COLS + col + sub) * 2 + lev) & (sub < HALF)
        return product(hot.astype(F32).astype(BF16), both).astype(BF16)

    own_ref[...] = pick(0, ROWS - OFF, 0)
    low_ref[...] = pick(ROWS - OFF, OFF, 0)
    side_ref[0:BIG, :] = pick(0, ROWS - OFF, HALF)
    side_ref[BIG:, :] = pick(ROWS - OFF, OFF, HALF)


def weight_kernel(
    bits_ref, scale_ref, cq_ref, cp_ref, cu_ref, cd_ref, wq_ref, wp_ref, wu_ref, wd_ref
):
    def dequant(codes, layer, fan_in):
        limit = jnp.left_shift(1, bits_ref[layer] - 1) - 1
        clipped = jnp.minimum(jnp.maximum(codes, -limit), limit).astype(F32)
        whole = jnp.full((1, 128), scale_ref[layer], jnp.int32).astype(F32)
        return clipped * (math.sqrt(C / fan_in) / whole)[:, :1]

    full = dequant(cq_ref[...], 0, C)
    for part in range(3):
        wq_ref[part] = full[:, part * C : (part + 1) * C].astype(BF16)
    wp_ref[...] = dequant(cp_ref[...], 1, C).astype(BF16)
    wu_ref[...] = dequant(cu_ref[...], 2, C).astype(BF16)
    wd_ref[...] = dequant(cd_ref[...], 3, FF).astype(BF16)


def bias_kernel(idx_ref, tab_ref, bias_ref, rows, places, found):
    rows[...] = jnp.zeros_like(rows)
    for head in range(HEADS):
        table = tab_ref[head].astype(F32)
        for high in range(HIGHS):
            width = min(LOWS, POS - high * LOWS)
            rows[high * 16 + head * 2 : high * 16 + head * 2 + 2, 0:width] = table[
                :, high * LOWS : high * LOWS + width
            ]
    table = rows[...].astype(BF16)

    index = idx_ref[...]
    parts = [
        lax.shift_right_logical(index, 8).astype(F32).astype(BF16),
        jnp.bitwise_and(index, LOWS - 1).astype(F32).astype(BF16),
    ]

    def token(where):
        sub = jnp.bitwise_and(where, SUB - 1)
        inside = (where >> 4) * WLON + jnp.bitwise_and(where >> 3, 1) * HALF + sub
        return jnp.where((sub < HALF) & (where < BLOCK), inside, -1000)

    for lev in range(LEVS):
        base = (1 - lev) * (WTOK // 2)
        pick_q = (iota((BLOCK, WTOK), 1) == token(iota((BLOCK, WTOK), 0)) + base).astype(F32)
        pick_k = (iota((WTOK, 128), 0) == token(iota((WTOK, 128), 1)) + base).astype(F32)
        for i, part in enumerate(parts):
            moved = product(product(pick_q.astype(BF16), part).astype(BF16), pick_k.astype(BF16))
            places[i, lev * BLOCK : (lev + 1) * BLOCK, :] = moved

    entry = iota((LOWS, 128), 0).astype(F32)

    def eight(group, carry):
        at = pl.multiple_of(group * SUB, SUB)
        high = places[0, pl.ds(at, SUB), :]
        low = places[1, pl.ds(at, SUB), :]
        hot = [(entry == low[s : s + 1]).astype(F32).astype(BF16) for s in range(HALF)]
        values = product(table, jnp.concatenate(hot, axis=1))
        for s in range(HALF):
            chosen = jnp.zeros((16, 128), F32)
            here = jnp.broadcast_to(high[s : s + 1], (16, 128))
            for i in range(HIGHS):
                candidate = values[i * 16 : (i + 1) * 16, s * 128 : (s + 1) * 128]
                chosen = jnp.where(here == float(i), candidate, chosen)
            found[at + s] = chosen
        found[at + HALF] = jnp.zeros((16, 128), F32)
        found[at + HALF + 1] = jnp.zeros((16, 128), F32)
        return carry

    lax.fori_loop(0, LEVS * BLOCK // SUB, eight, 0, unroll=8)

    key = iota((BLOCK, 128), 1)
    for win in range(2):
        row = lax.axis_index(LAT) * ROWS - OFF + win * WLAT + (key >> 4)
        usable = (row >= 0) & (row < lax.axis_size(LAT) * ROWS - LAT_PAD)
        usable = usable & (jnp.bitwise_and(key, SUB - 1) < HALF) & (key < BLOCK)
        for lev in range(LEVS):
            for head in range(HEADS):
                values = found[lev * BLOCK : (lev + 1) * BLOCK, head * 2 + win, :]
                values = jnp.where(usable, values, MASKED)
                bias_ref[lev * 2 + win, head * BLOCK : (head + 1) * BLOCK, :] = values.astype(BF16)


def unit(values):
    center = values - jnp.mean(values, axis=-1, keepdims=True)
    spread = jnp.mean(center * center, axis=-1, keepdims=True)
    scale = lax.rsqrt(spread + EPSILON)
    return center * scale, scale


def unit_back(normal, scale, upstream):
    level = jnp.mean(upstream, axis=-1, keepdims=True)
    along = jnp.mean(upstream * normal, axis=-1, keepdims=True)
    return scale * (upstream - level - normal * along)


def main_kernel(
    own_ref,
    side_ref,
    edge_ref,
    wq_ref,
    wp_ref,
    wu_ref,
    wd_ref,
    bias_ref,
    own_out,
    side_out,
    low_out,
    corner_out,
    keep_ref,
    give_ref,
    frame,
):
    below = ROWS - OFF

    def piece(block, rows):
        return block.astype(F32).reshape(LEVS, rows, SUB, 2 * C)

    frame[:, OFF:, 1] = piece(own_ref[...], below)
    frame[:, OFF:, 0] = piece(side_ref[0:BIG, :], below)
    frame[:, :OFF, 1] = piece(edge_ref[0:THIN, :], OFF)
    frame[:, :OFF, 0] = piece(edge_ref[THIN:, :], OFF)
    both = frame[...].reshape(FRAME, 2 * C)

    place = iota((FRAME, C), 0)
    row = lax.axis_index(LAT) * ROWS - OFF + (place >> 4) - jnp.where(place >= FRAME // 2, ROWS, 0)
    valid = (row >= 0) & (row < lax.axis_size(LAT) * ROWS - LAT_PAD)
    valid = valid & (jnp.bitwise_and(place, SUB - 1) < HALF)
    start = jnp.where(valid, both[:, :C], 0.0)
    d_out = jnp.where(valid, both[:, C:], 0.0)
    d_out_low = d_out.astype(BF16)

    normal, scale = unit(start)
    normed = normal.astype(BF16)
    query = product(normed, wq_ref[0]).astype(BF16)
    key = product(normed, wq_ref[1]).astype(BF16)
    value = product(normed, wq_ref[2]).astype(BF16)

    lane_head = iota((HEADS, 1, C), 2) >> 5
    head_mask = lane_head == iota((HEADS, 1, C), 0)
    mask_low = head_mask.astype(F32).astype(BF16)
    mask_full = head_mask.astype(F32)

    def spread_heads(block):
        return (block[None] * mask_low).reshape(STACK, C)

    def join_heads(stacked):
        return jnp.sum(stacked.reshape(HEADS, BLOCK, C) * mask_full, axis=0)

    saved = []
    heads_parts = []
    for block in range(4):
        at = slice(block * BLOCK, (block + 1) * BLOCK)
        q_stack = spread_heads(query[at])
        scores = across(q_stack, key[at]) * HEAD_DIM ** (-0.5)
        scores = scores + bias_ref[block][:, :BLOCK].astype(F32)
        weights = jnp.exp(scores - jnp.max(scores, axis=-1, keepdims=True))
        weights = weights / jnp.sum(weights, axis=-1, keepdims=True)
        weights_low = weights.astype(BF16)
        heads_parts.append(join_heads(product(weights_low, value[at])))
        saved.append((q_stack, weights, weights_low))
    heads = jnp.concatenate(heads_parts, axis=0).astype(BF16)

    resid = (start + product(heads, wp_ref[...])).astype(BF16).astype(F32)
    normal_two, scale_two = unit(resid)
    normed_two = normal_two.astype(BF16)
    pre_act = product(normed_two, wu_ref[...])
    inner = math.sqrt(2 / math.pi)
    square = pre_act * pre_act
    bend = jnp.tanh(inner * (pre_act + 0.044715 * (square * pre_act)))
    half = 0.5 * (1.0 + bend)
    hidden = (pre_act * half).astype(BF16)
    slope = half + 0.5 * pre_act * (1.0 - bend * bend) * (
        inner * (1.0 + (3 * 0.044715) * square)
    )
    final = jnp.where(valid, resid + across(hidden, wd_ref[...]), 0.0)

    d_hidden = product(d_out_low, wd_ref[...]).astype(BF16).astype(F32)
    d_pre = (slope * d_hidden).astype(BF16)
    d_normed_two = across(d_pre, wu_ref[...]).astype(BF16).astype(F32)
    d_resid = (d_out + unit_back(normal_two, scale_two, d_normed_two)).astype(BF16)
    d_heads = across(d_resid, wp_ref[...]).astype(BF16)

    dq_parts = []
    dk_parts = []
    dv_parts = []
    for block in range(4):
        at = slice(block * BLOCK, (block + 1) * BLOCK)
        q_stack, weights, weights_low = saved[block]
        d_stack = spread_heads(d_heads[at])
        d_weights = across(d_stack, value[at]).astype(BF16).astype(F32)
        dv_parts.append(crossed(weights_low, d_stack))
        inside = jnp.sum(weights * d_weights, axis=-1, keepdims=True)
        d_scores = (weights * (d_weights - inside) * HEAD_DIM ** (-0.5)).astype(BF16)
        dq_parts.append(join_heads(product(d_scores, key[at])))
        dk_parts.append(crossed(d_scores, q_stack))
    d_query = jnp.concatenate(dq_parts, axis=0).astype(BF16)
    d_key = jnp.concatenate(dk_parts, axis=0).astype(BF16)
    d_value = jnp.concatenate(dv_parts, axis=0).astype(BF16)

    d_normed = across(d_query, wq_ref[0]) + across(d_key, wq_ref[1]) + across(d_value, wq_ref[2])
    d_normed = d_normed.astype(BF16).astype(F32)
    grad = jnp.where(valid, d_resid.astype(F32) + unit_back(normal, scale, d_normed), 0.0)

    result = jnp.concatenate([final, grad], axis=-1).reshape(LEVS, ROWS, 2, SUB, 2 * C)

    def flat(part):
        return part.reshape(-1, 2 * C).astype(BF16)

    own_out[...] = flat(result[:, OFF:, 1])
    side_out[...] = flat(result[:, OFF:, 0])
    low_out[...] = flat(result[:, :OFF, 1])
    corner_out[...] = flat(result[:, :OFF, 0])

    small = [
        crossed(normed, d_query),
        crossed(normed, d_key),
        crossed(normed, d_value),
        crossed(heads, d_resid),
    ]
    tiles = [total[:, :128] for total in small]
    tiles += [
        jnp.concatenate([small[i][:, 128:], small[i + 1][:, 128:]], axis=-1) for i in (0, 2)
    ]
    for wide in (crossed(normed_two, d_pre), crossed(d_out_low, hidden)):
        tiles += [wide[:, i * 128 : (i + 1) * 128] for i in range(6)]
    half_tiles = len(tiles) // 2

    def store(ref, first):
        for i in range(half_tiles):
            ref[i * C : (i + 1) * C, :] = tiles[first + i].astype(BF16)

    core = lax.axis_index("c")

    @pl.when(core == 0)
    def _():
        store(keep_ref, 0)
        store(give_ref, half_tiles)

    @pl.when(core != 0)
    def _():
        store(keep_ref, half_tiles)
        store(give_ref, 0)


def spread_kernel(own_ref, other_ref, qkv_ref, proj_ref, up_ref, down_ref):
    first = lax.axis_index("c") == 0
    half_tiles = own_ref.shape[0] // C

    def tile(i):
        at = slice(i % half_tiles * C, (i % half_tiles + 1) * C)
        mine = first if i < half_tiles else jnp.logical_not(first)
        return jnp.where(mine, own_ref[at, :].astype(F32), other_ref[at, :].astype(F32))

    ends = [tile(4)[:, :64], tile(4)[:, 64:], tile(5)[:, :64], tile(5)[:, 64:]]
    small = [jnp.concatenate([tile(i), ends[i]], axis=-1) for i in range(4)]
    qkv_ref[...] = jnp.concatenate(small[:3], axis=-1).astype(BF16)
    proj_ref[...] = small[3].astype(BF16)
    for i in range(6):
        up_ref[:, i * 128 : (i + 1) * 128] = tile(6 + i).astype(BF16)
        down_ref[:, i * 128 : (i + 1) * 128] = tile(12 + i).astype(BF16)


def finish_kernel(
    own_ref, side_ref, low_ref, corner_ref, weight_ref, merged_ref, grad_ref, frame
):
    above = ROWS - OFF

    def piece(ref, rows):
        return ref[...].astype(F32).reshape(LEVS, rows, SUB, 2 * C)

    frame[:, :above, 0] = piece(own_ref, above)
    frame[:, above:, 0] = piece(low_ref, OFF)
    frame[:, :above, 1] = piece(side_ref, above)
    frame[:, above:, 1] = piece(corner_ref, OFF)
    both = frame[...].reshape(FRAME, 2 * C)
    final = both[:, :C].astype(BF16)
    grad = both[:, C:].astype(BF16)

    def source(col):
        return jnp.where(col >= HALF, col + (SUB - HALF), col)

    to = iota((FRAME, FRAME), 0)
    col = jnp.bitwise_and(to, 15)
    pick = (iota((FRAME, FRAME), 1) == to - col + source(col)) & (col < COLS)
    moved = product(pick.astype(F32).astype(BF16), grad).reshape(LEVS, ROWS, 16, C)
    grad_ref[...] = moved[:, :, :COLS, :].astype(BF16)

    count = LEVS * (ROWS // 2) * SUB
    to = iota((count, FRAME), 0)
    lev = jnp.where(to >= count // 2, 1, 0)
    pair = (to >> 3) - lev * (ROWS // 2)
    parts = []
    for down in range(2):
        for right in range(2):
            col = 2 * jnp.bitwise_and(to, SUB - 1) + right
            wanted = lev * (FRAME // 2) + (2 * pair + down) * 16 + source(col)
            pick = (iota((count, FRAME), 1) == wanted) & (col < COLS)
            parts.append(product(pick.astype(F32).astype(BF16), final))
    width = 4 * C
    mean = sum(jnp.sum(part, axis=-1, keepdims=True) for part in parts) / width
    centers = [part - mean for part in parts]
    spread = sum(jnp.sum(part * part, axis=-1, keepdims=True) for part in centers) / width
    scale = lax.rsqrt(spread + EPSILON)
    total = jnp.zeros((count, 2 * C), F32)
    for i, part in enumerate(centers):
        total = total + product((part * scale).astype(BF16), weight_ref[i * C : (i + 1) * C, :])
    merged_ref[...] = total.reshape(LEVS, ROWS // 2, SUB, 2 * C)[:, :, :HALF, :].astype(BF16)


def call(kernel, outs, args, scratch=(), scalars=0, flops=0, mib=16):
    vmem = pl.BlockSpec(memory_space=pltpu.VMEM)
    smem = pl.BlockSpec(memory_space=pltpu.SMEM)
    moved = sum(math.prod(a.shape) * a.dtype.itemsize for a in args)
    moved += sum(math.prod(s) * jnp.dtype(t).itemsize for s, t in outs)
    return pl.pallas_call(
        kernel,
        out_shape=[jax.ShapeDtypeStruct(s, t) for s, t in outs],
        in_specs=[smem] * scalars + [vmem] * (len(args) - scalars),
        out_specs=[vmem] * len(outs),
        scratch_shapes=list(scratch),
        compiler_params=pltpu.CompilerParams(vmem_limit_bytes=mib * 1024 * 1024),
        cost_estimate=pl.CostEstimate(flops=flops, bytes_accessed=moved, transcendentals=0),
    )(*args)


def shifted(block, lat_step, lon_step):
    rows = lax.axis_size(LAT)
    cols = lax.axis_size(LON)
    if lat_step and lon_step:
        route = [
            (col * rows + row, (col + lon_step) % cols * rows + row + lat_step)
            for col in range(cols)
            for row in range(rows)
            if 0 <= row + lat_step < rows
        ]
        return lax.ppermute(block, LON + LAT, route)
    if lat_step:
        route = [(r, r + lat_step) for r in range(rows) if 0 <= r + lat_step < rows]
        return lax.ppermute(block, LAT, route)
    return lax.ppermute(block, LON, [(c, (c + lon_step) % cols) for c in range(cols)])


def exchange(parts, axes):
    return lax.all_to_all(parts, axes, 0, 0)


def swapped(block):
    return lax.ppermute(block, "c", [(0, 1), (1, 0)])


def sum_kernel(parts_ref, out_ref):
    count, rows, _ = parts_ref.shape
    total = parts_ref[0].astype(F32)
    for i in range(1, count):
        total = total + parts_ref[i].astype(F32)
    out_ref[0:rows, :] = total.astype(BF16)
    if rows < out_ref.shape[0]:
        out_ref[rows:, :] = jnp.zeros((out_ref.shape[0] - rows, 128), BF16)


def sum_spread_kernel(parts_ref, out_ref):
    total = jnp.sum(parts_ref[...].astype(F32), axis=0).astype(BF16)
    out_ref[...] = jnp.broadcast_to(total[None], out_ref.shape)


def copies_kernel(part_ref, out_ref):
    count, rows, _ = out_ref.shape
    for i in range(count):
        out_ref[i] = part_ref[0:rows, :]


def per_device(
    tokens,
    cotangent,
    qkv_codes,
    proj_codes,
    up_codes,
    down_codes,
    bit_widths,
    quant_scales,
    bias_table,
    bias_index,
    merge_weight,
):
    own, low, side = call(
        pack_kernel,
        [((BIG, 2 * C), BF16), ((THIN, 2 * C), BF16), ((BIG + THIN, 2 * C), BF16)],
        (tokens.transpose(1, 2, 0, 3), cotangent.transpose(1, 2, 0, 3)),
    )
    side = shifted(side, 0, 1)
    (bias,) = call(
        bias_kernel,
        [((4, STACK, 128), BF16)],
        (
            bias_index.reshape(WTOK, WTOK),
            bias_table.transpose(1, 2, 0, 3).reshape(HEADS, 2, POS),
        ),
        [
            pltpu.VMEM((HIGHS * 16, LOWS), F32),
            pltpu.VMEM((2, LEVS * BLOCK, 128), F32),
            pltpu.VMEM((LEVS * BLOCK, 16, 128), F32),
        ],
        flops=2_000_000_000,
    )
    edge = jnp.concatenate([low, side[BIG:]], axis=0)
    edge, bias, codes = lax.optimization_barrier(
        (edge, bias, (qkv_codes, proj_codes, up_codes, down_codes.T))
    )
    edge = shifted(edge, 1, 0)
    weights = call(
        weight_kernel,
        [((3, C, C), BF16), ((C, C), BF16), ((C, FF), BF16), ((C, FF), BF16)],
        (bit_widths, quant_scales, *codes),
        scalars=2,
        flops=1_000_000_000,
    )
    own, side, low, corner, keep, give = call(
        main_kernel,
        [
            ((BIG, 2 * C), BF16),
            ((BIG, 2 * C), BF16),
            ((THIN, 2 * C), BF16),
            ((THIN, 2 * C), BF16),
            ((9 * C, 128), BF16),
            ((9 * C, 128), BF16),
        ],
        (own, side, edge, *weights, bias),
        [pltpu.VMEM((LEVS, ROWS, 2, SUB, 2 * C), F32)],
        flops=2_000_000_000,
        mib=32,
    )

    near = lax.axis_size(NEAR)
    far = lax.axis_size(FAR)
    rows = 9 * C // near
    padded = -(-rows // (8 * far)) * (8 * far)
    part = (keep.astype(F32) + swapped(give).astype(F32)).astype(BF16)
    part = exchange(part.reshape(near, rows, 128), NEAR)
    side, low = shifted(side, 0, -1), shifted(low, -1, 0)
    part, side, low = lax.optimization_barrier((part, side, low))
    (part,) = call(sum_kernel, [((padded, 128), BF16)], (part,))
    part = exchange(part.reshape(far, padded // far, 128), FAR)
    (part,) = call(sum_spread_kernel, [(part.shape, BF16)], (part,))
    part = exchange(part, FAR).reshape(padded, 128)
    part, own, corner = lax.optimization_barrier((part, own, corner))
    corner = shifted(corner, -1, -1)
    (spread,) = call(copies_kernel, [((near, rows, 128), BF16)], (part,))
    half = exchange(spread, NEAR)
    merged, grad_tokens = call(
        finish_kernel,
        [((LEVS, ROWS // 2, COLS // 2, 2 * C), BF16), ((LEVS, ROWS, COLS, C), BF16)],
        (own, side, low, corner, merge_weight),
        [pltpu.VMEM((LEVS, ROWS, 2, SUB, 2 * C), F32)],
        flops=400_000_000,
    )
    half, merged, grad_tokens = lax.optimization_barrier((half, merged, grad_tokens))
    half = half.reshape(near * rows, 128)
    qkv, proj, up, down = call(
        spread_kernel,
        [((C, 3 * C), BF16), ((C, C), BF16), ((C, FF), BF16), ((C, FF), BF16)],
        (half, swapped(half)),
    )
    return (merged, grad_tokens, qkv, proj, up, down.T)


def solution(mesh):
    cols, rows = mesh.devices.shape
    fine = Mesh(mesh.devices.reshape(cols // 4, 2, 2, rows // 2, 2), LON + LAT)
    cells = P(None, LAT, LON, None)
    placed = (
        cells,
        cells,
        P(),
        P(),
        P(),
        P(),
        P(),
        P(),
        P(LAT, None, None, None),
        P(),
        P(),
    )
    return jax.shard_map(
        per_device,
        mesh=fine,
        in_specs=placed,
        out_specs=(cells, cells, P(), P(), P(), P()),
        check_vma=False,
    )
```

```python
import math

import jax
import jax.numpy as jnp
from jax import lax
from jax.experimental import pallas as pl
from jax.experimental.pallas import tpu as pltpu
from jax.sharding import Mesh
from jax.sharding import PartitionSpec as P

C = 192
HEADS = 6
FF = 768
HEAD_DIM = 32
WLAT = 6
WLON = 12
LAT_PAD = 11
WTOK = 144
POS = 3312

ROWS = 12
COLS = 12
LEVS = 2
OFF = WLAT // 2
HALF = WLON // 2
SUB = 8
FRAME = LEVS * ROWS * 2 * SUB
BLOCK = FRAME // 4
STACK = HEADS * BLOCK
BIG = LEVS * (ROWS - OFF) * SUB
THIN = LEVS * OFF * SUB
LOWS = 256
HIGHS = -(-POS // LOWS)

EPSILON = 1e-05
MASKED = -1000000000.0
F32 = jnp.float32
BF16 = jnp.bfloat16

LAT = ("y", "xl")
LON = ("z", "xh", "c")
NEAR = ("xh", "xl")
FAR = ("y", "z")


def iota(shape, dim):
    return lax.broadcasted_iota(jnp.int32, shape, dim)


def product(left, right):
    return lax.dot_general(left, right, (((1,), (0,)), ((), ())), preferred_element_type=F32)


def across(left, right):
    return lax.dot_general(left, right, (((1,), (1,)), ((), ())), preferred_element_type=F32)


def crossed(left, right):
    return lax.dot_general(left, right, (((0,), (0,)), ((), ())), preferred_element_type=F32)


def pack_kernel(tok_ref, cot_ref, own_ref, low_ref, side_ref):
    both = jnp.concatenate(
        [ref[...].astype(F32).reshape(LEVS * ROWS * COLS, C) for ref in (tok_ref, cot_ref)], axis=-1
    ).astype(BF16)

    def pick(first, count, col):
        shape = (LEVS * count * SUB, LEVS * ROWS * COLS)
        to = iota(shape, 0)
        lev = jnp.where(to >= count * SUB, 1, 0)
        row = (to >> 3) - lev * count + first
        sub = jnp.bitwise_and(to, SUB - 1)
        hot = (iota(shape, 1) == (row * COLS + col + sub) * 2 + lev) & (sub < HALF)
        return product(hot.astype(F32).astype(BF16), both).astype(BF16)

    own_ref[...] = pick(0, ROWS - OFF, 0)
    low_ref[...] = pick(ROWS - OFF, OFF, 0)
    side_ref[0:BIG, :] = pick(0, ROWS - OFF, HALF)
    side_ref[BIG:, :] = pick(ROWS - OFF, OFF, HALF)


def weight_kernel(
    bits_ref, scale_ref, cq_ref, cp_ref, cu_ref, cd_ref, wq_ref, wp_ref, wu_ref, wd_ref
):
    def dequant(codes, layer, fan_in):
        limit = jnp.left_shift(1, bits_ref[layer] - 1) - 1
        clipped = jnp.minimum(jnp.maximum(codes, -limit), limit).astype(F32)
        whole = jnp.full((1, 128), scale_ref[layer], jnp.int32).astype(F32)
        return clipped * (math.sqrt(C / fan_in) / whole)[:, :1]

    full = dequant(cq_ref[...], 0, C)
    for part in range(3):
        wq_ref[part] = full[:, part * C : (part + 1) * C].astype(BF16)
    wp_ref[...] = dequant(cp_ref[...], 1, C).astype(BF16)
    wu_ref[...] = dequant(cu_ref[...], 2, C).astype(BF16)
    wd_ref[...] = dequant(cd_ref[...], 3, FF).astype(BF16)


def bias_kernel(idx_ref, tab_ref, bias_ref, rows, places, found):
    rows[...] = jnp.zeros_like(rows)
    for head in range(HEADS):
        table = tab_ref[head].astype(F32)
        for high in range(HIGHS):
            width = min(LOWS, POS - high * LOWS)
            rows[high * 16 + head * 2 : high * 16 + head * 2 + 2, 0:width] = table[
                :, high * LOWS : high * LOWS + width
            ]
    table = rows[...].astype(BF16)

    index = idx_ref[...]
    parts = [
        lax.shift_right_logical(index, 8).astype(F32).astype(BF16),
        jnp.bitwise_and(index, LOWS - 1).astype(F32).astype(BF16),
    ]

    def token(where):
        sub = jnp.bitwise_and(where, SUB - 1)
        inside = (where >> 4) * WLON + jnp.bitwise_and(where >> 3, 1) * HALF + sub
        return jnp.where((sub < HALF) & (where < BLOCK), inside, -1000)

    for lev in range(LEVS):
        base = (1 - lev) * (WTOK // 2)
        pick_q = (iota((BLOCK, WTOK), 1) == token(iota((BLOCK, WTOK), 0)) + base).astype(F32)
        pick_k = (iota((WTOK, 128), 0) == token(iota((WTOK, 128), 1)) + base).astype(F32)
        for i, part in enumerate(parts):
            moved = product(product(pick_q.astype(BF16), part).astype(BF16), pick_k.astype(BF16))
            places[i, lev * BLOCK : (lev + 1) * BLOCK, :] = moved

    entry = iota((LOWS, 128), 0).astype(F32)

    def eight(group, carry):
        at = pl.multiple_of(group * SUB, SUB)
        high = places[0, pl.ds(at, SUB), :]
        low = places[1, pl.ds(at, SUB), :]
        hot = [(entry == low[s : s + 1]).astype(F32).astype(BF16) for s in range(HALF)]
        values = product(table, jnp.concatenate(hot, axis=1))
        for s in range(HALF):
            chosen = jnp.zeros((16, 128), F32)
            here = jnp.broadcast_to(high[s : s + 1], (16, 128))
            for i in range(HIGHS):
                candidate = values[i * 16 : (i + 1) * 16, s * 128 : (s + 1) * 128]
                chosen = jnp.where(here == float(i), candidate, chosen)
            found[at + s] = chosen
        found[at + HALF] = jnp.zeros((16, 128), F32)
        found[at + HALF + 1] = jnp.zeros((16, 128), F32)
        return carry

    lax.fori_loop(0, LEVS * BLOCK // SUB, eight, 0, unroll=24)

    key = iota((BLOCK, 128), 1)
    for win in range(2):
        row = lax.axis_index(LAT) * ROWS - OFF + win * WLAT + (key >> 4)
        usable = (row >= 0) & (row < lax.axis_size(LAT) * ROWS - LAT_PAD)
        usable = usable & (jnp.bitwise_and(key, SUB - 1) < HALF) & (key < BLOCK)
        for lev in range(LEVS):
            for head in range(HEADS):
                values = found[lev * BLOCK : (lev + 1) * BLOCK, head * 2 + win, :]
                values = jnp.where(usable, values, MASKED)
                bias_ref[lev * 2 + win, head * BLOCK : (head + 1) * BLOCK, :] = values.astype(BF16)


def unit(values):
    center = values - jnp.mean(values, axis=-1, keepdims=True)
    spread = jnp.mean(center * center, axis=-1, keepdims=True)
    scale = lax.rsqrt(spread + EPSILON)
    return center * scale, scale


def unit_back(normal, scale, upstream):
    level = jnp.mean(upstream, axis=-1, keepdims=True)
    along = jnp.mean(upstream * normal, axis=-1, keepdims=True)
    return scale * (upstream - level - normal * along)


def main_kernel(
    own_ref,
    side_ref,
    edge_ref,
    wq_ref,
    wp_ref,
    wu_ref,
    wd_ref,
    bias_ref,
    own_out,
    low_out,
    side_out,
    keep_ref,
    give_ref,
    frame,
):
    below = ROWS - OFF

    def piece(block, rows):
        return block.astype(F32).reshape(LEVS, rows, SUB, 2 * C)

    frame[:, OFF:, 1] = piece(own_ref[...], below)
    frame[:, OFF:, 0] = piece(side_ref[0:BIG, :], below)
    frame[:, :OFF, 1] = piece(edge_ref[0:THIN, :], OFF)
    frame[:, :OFF, 0] = piece(edge_ref[THIN:, :], OFF)
    both = frame[...].reshape(FRAME, 2 * C)

    place = iota((FRAME, C), 0)
    row = lax.axis_index(LAT) * ROWS - OFF + (place >> 4) - jnp.where(place >= FRAME // 2, ROWS, 0)
    valid = (row >= 0) & (row < lax.axis_size(LAT) * ROWS - LAT_PAD)
    valid = valid & (jnp.bitwise_and(place, SUB - 1) < HALF)
    start = jnp.where(valid, both[:, :C], 0.0)
    d_out = jnp.where(valid, both[:, C:], 0.0)
    d_out_low = d_out.astype(BF16)

    normal, scale = unit(start)
    normed = normal.astype(BF16)
    query = product(normed, wq_ref[0]).astype(BF16)
    key = product(normed, wq_ref[1]).astype(BF16)
    value = product(normed, wq_ref[2]).astype(BF16)

    lane_head = iota((HEADS, 1, C), 2) >> 5
    head_mask = lane_head == iota((HEADS, 1, C), 0)
    mask_low = head_mask.astype(F32).astype(BF16)
    mask_full = head_mask.astype(F32)

    def spread_heads(block):
        return (block[None] * mask_low).reshape(STACK, C)

    def join_heads(stacked):
        return jnp.sum(stacked.reshape(HEADS, BLOCK, C) * mask_full, axis=0)

    saved = []
    heads_parts = []
    for block in range(4):
        at = slice(block * BLOCK, (block + 1) * BLOCK)
        q_stack = spread_heads(query[at])
        scores = across(q_stack, key[at]) * HEAD_DIM ** (-0.5)
        scores = scores + bias_ref[block][:, :BLOCK].astype(F32)
        weights = jnp.exp(scores - jnp.max(scores, axis=-1, keepdims=True))
        weights = weights / jnp.sum(weights, axis=-1, keepdims=True)
        weights_low = weights.astype(BF16)
        heads_parts.append(join_heads(product(weights_low, value[at])))
        saved.append((q_stack, weights, weights_low))
    heads = jnp.concatenate(heads_parts, axis=0).astype(BF16)

    resid = (start + product(heads, wp_ref[...])).astype(BF16).astype(F32)
    normal_two, scale_two = unit(resid)
    normed_two = normal_two.astype(BF16)
    pre_act = product(normed_two, wu_ref[...])
    inner = math.sqrt(2 / math.pi)
    square = pre_act * pre_act
    bend = jnp.tanh(inner * (pre_act + 0.044715 * (square * pre_act)))
    half = 0.5 * (1.0 + bend)
    hidden = (pre_act * half).astype(BF16)
    slope = half + 0.5 * pre_act * (1.0 - bend * bend) * (
        inner * (1.0 + (3 * 0.044715) * square)
    )
    final = jnp.where(valid, resid + across(hidden, wd_ref[...]), 0.0)

    d_hidden = product(d_out_low, wd_ref[...]).astype(BF16).astype(F32)
    d_pre = (slope * d_hidden).astype(BF16)
    d_normed_two = across(d_pre, wu_ref[...]).astype(BF16).astype(F32)
    d_resid = (d_out + unit_back(normal_two, scale_two, d_normed_two)).astype(BF16)
    d_heads = across(d_resid, wp_ref[...]).astype(BF16)

    dq_parts = []
    dk_parts = []
    dv_parts = []
    for block in range(4):
        at = slice(block * BLOCK, (block + 1) * BLOCK)
        q_stack, weights, weights_low = saved[block]
        d_stack = spread_heads(d_heads[at])
        d_weights = across(d_stack, value[at]).astype(BF16).astype(F32)
        dv_parts.append(crossed(weights_low, d_stack))
        inside = jnp.sum(weights * d_weights, axis=-1, keepdims=True)
        d_scores = (weights * (d_weights - inside) * HEAD_DIM ** (-0.5)).astype(BF16)
        dq_parts.append(join_heads(product(d_scores, key[at])))
        dk_parts.append(crossed(d_scores, q_stack))
    d_query = jnp.concatenate(dq_parts, axis=0).astype(BF16)
    d_key = jnp.concatenate(dk_parts, axis=0).astype(BF16)
    d_value = jnp.concatenate(dv_parts, axis=0).astype(BF16)

    d_normed = across(d_query, wq_ref[0]) + across(d_key, wq_ref[1]) + across(d_value, wq_ref[2])
    d_normed = d_normed.astype(BF16).astype(F32)
    grad = jnp.where(valid, d_resid.astype(F32) + unit_back(normal, scale, d_normed), 0.0)

    result = jnp.concatenate([final, grad], axis=-1).reshape(LEVS, ROWS, 2, SUB, 2 * C)

    def flat(part):
        return part.reshape(-1, 2 * C).astype(BF16)

    own_out[...] = flat(result[:, OFF:, 1])
    low_out[...] = flat(result[:, :OFF, 1])
    side_out[0:BIG, :] = flat(result[:, OFF:, 0])
    side_out[BIG:, :] = flat(result[:, :OFF, 0])

    small = [
        crossed(normed, d_query),
        crossed(normed, d_key),
        crossed(normed, d_value),
        crossed(heads, d_resid),
    ]
    tiles = [total[:, :128] for total in small]
    tiles += [
        jnp.concatenate([small[i][:, 128:], small[i + 1][:, 128:]], axis=-1) for i in (0, 2)
    ]
    for wide in (crossed(normed_two, d_pre), crossed(d_out_low, hidden)):
        tiles += [wide[:, i * 128 : (i + 1) * 128] for i in range(6)]
    half_tiles = len(tiles) // 2

    def store(ref, first):
        for i in range(half_tiles):
            ref[i * C : (i + 1) * C, :] = tiles[first + i].astype(BF16)

    core = lax.axis_index("c")

    @pl.when(core == 0)
    def _():
        store(keep_ref, 0)
        store(give_ref, half_tiles)

    @pl.when(core != 0)
    def _():
        store(keep_ref, half_tiles)
        store(give_ref, 0)


def spread_kernel(own_ref, other_ref, qkv_ref, proj_ref, up_ref, down_ref):
    first = lax.axis_index("c") == 0
    half_tiles = own_ref.shape[0] // C

    def tile(i):
        at = slice(i % half_tiles * C, (i % half_tiles + 1) * C)
        mine = first if i < half_tiles else jnp.logical_not(first)
        return jnp.where(mine, own_ref[at, :].astype(F32), other_ref[at, :].astype(F32))

    ends = [tile(4)[:, :64], tile(4)[:, 64:], tile(5)[:, :64], tile(5)[:, 64:]]
    small = [jnp.concatenate([tile(i), ends[i]], axis=-1) for i in range(4)]
    qkv_ref[...] = jnp.concatenate(small[:3], axis=-1).astype(BF16)
    proj_ref[...] = small[3].astype(BF16)
    for i in range(6):
        up_ref[:, i * 128 : (i + 1) * 128] = tile(6 + i).astype(BF16)
        down_ref[:, i * 128 : (i + 1) * 128] = tile(12 + i).astype(BF16)


def finish_kernel(own_ref, side_ref, edge_ref, weight_ref, merged_ref, grad_ref, frame):
    above = ROWS - OFF

    def piece(block, rows):
        return block.astype(F32).reshape(LEVS, rows, SUB, 2 * C)

    frame[:, :above, 0] = piece(own_ref[...], above)
    frame[:, above:, 0] = piece(edge_ref[0:THIN, :], OFF)
    frame[:, :above, 1] = piece(side_ref[0:BIG, :], above)
    frame[:, above:, 1] = piece(edge_ref[THIN:, :], OFF)
    both = frame[...].reshape(FRAME, 2 * C)
    final = both[:, :C].astype(BF16)
    grad = both[:, C:].astype(BF16)

    def source(col):
        return jnp.where(col >= HALF, col + (SUB - HALF), col)

    to = iota((FRAME, FRAME), 0)
    col = jnp.bitwise_and(to, 15)
    pick = (iota((FRAME, FRAME), 1) == to - col + source(col)) & (col < COLS)
    moved = product(pick.astype(F32).astype(BF16), grad).reshape(LEVS, ROWS, 16, C)
    grad_ref[...] = moved[:, :, :COLS, :].astype(BF16)

    count = LEVS * (ROWS // 2) * SUB
    to = iota((count, FRAME), 0)
    lev = jnp.where(to >= count // 2, 1, 0)
    pair = (to >> 3) - lev * (ROWS // 2)
    parts = []
    for down in range(2):
        for right in range(2):
            col = 2 * jnp.bitwise_and(to, SUB - 1) + right
            wanted = lev * (FRAME // 2) + (2 * pair + down) * 16 + source(col)
            pick = (iota((count, FRAME), 1) == wanted) & (col < COLS)
            parts.append(product(pick.astype(F32).astype(BF16), final))
    width = 4 * C
    mean = sum(jnp.sum(part, axis=-1, keepdims=True) for part in parts) / width
    centers = [part - mean for part in parts]
    spread = sum(jnp.sum(part * part, axis=-1, keepdims=True) for part in centers) / width
    scale = lax.rsqrt(spread + EPSILON)
    total = jnp.zeros((count, 2 * C), F32)
    for i, part in enumerate(centers):
        total = total + product((part * scale).astype(BF16), weight_ref[i * C : (i + 1) * C, :])
    merged_ref[...] = total.reshape(LEVS, ROWS // 2, SUB, 2 * C)[:, :, :HALF, :].astype(BF16)


def call(kernel, outs, args, scratch=(), scalars=0, flops=0, mib=16):
    vmem = pl.BlockSpec(memory_space=pltpu.VMEM)
    smem = pl.BlockSpec(memory_space=pltpu.SMEM)
    moved = sum(math.prod(a.shape) * a.dtype.itemsize for a in args)
    moved += sum(math.prod(s) * jnp.dtype(t).itemsize for s, t in outs)
    return pl.pallas_call(
        kernel,
        out_shape=[jax.ShapeDtypeStruct(s, t) for s, t in outs],
        in_specs=[smem] * scalars + [vmem] * (len(args) - scalars),
        out_specs=[vmem] * len(outs),
        scratch_shapes=list(scratch),
        compiler_params=pltpu.CompilerParams(vmem_limit_bytes=mib * 1024 * 1024),
        cost_estimate=pl.CostEstimate(flops=flops, bytes_accessed=moved, transcendentals=0),
    )(*args)


def shifted(block, axes, step):
    count = lax.axis_size(axes)
    if axes == LAT:
        route = [(i, i + step) for i in range(count) if 0 <= i + step < count]
    else:
        route = [(i, (i + step) % count) for i in range(count)]
    return lax.ppermute(block, axes, route)


def exchange(parts, axes):
    return lax.all_to_all(parts, axes, 0, 0)


def swapped(block):
    return lax.ppermute(block, "c", [(0, 1), (1, 0)])


def sum_kernel(parts_ref, low_ref, side_ref, out_ref, edge_ref):
    edge_ref[0:THIN, :] = low_ref[...]
    edge_ref[THIN:, :] = side_ref[BIG:, :]
    count, rows, _ = parts_ref.shape
    total = parts_ref[0].astype(F32)
    for i in range(1, count):
        total = total + parts_ref[i].astype(F32)
    out_ref[0:rows, :] = total.astype(BF16)
    if rows < out_ref.shape[0]:
        out_ref[rows:, :] = jnp.zeros((out_ref.shape[0] - rows, 128), BF16)


def sum_spread_kernel(parts_ref, out_ref):
    total = jnp.sum(parts_ref[...].astype(F32), axis=0).astype(BF16)
    out_ref[...] = jnp.broadcast_to(total[None], out_ref.shape)


def copies_kernel(part_ref, out_ref):
    count, rows, _ = out_ref.shape
    for i in range(count):
        out_ref[i] = part_ref[0:rows, :]


def per_device(
    tokens,
    cotangent,
    qkv_codes,
    proj_codes,
    up_codes,
    down_codes,
    bit_widths,
    quant_scales,
    bias_table,
    bias_index,
    merge_weight,
):
    own, low, side = call(
        pack_kernel,
        [((BIG, 2 * C), BF16), ((THIN, 2 * C), BF16), ((BIG + THIN, 2 * C), BF16)],
        (tokens.transpose(1, 2, 0, 3), cotangent.transpose(1, 2, 0, 3)),
    )
    side = shifted(side, LON, 1)
    (bias,) = call(
        bias_kernel,
        [((4, STACK, 128), BF16)],
        (
            bias_index.reshape(WTOK, WTOK),
            bias_table.transpose(1, 2, 0, 3).reshape(HEADS, 2, POS),
        ),
        [
            pltpu.VMEM((HIGHS * 16, LOWS), F32),
            pltpu.VMEM((2, LEVS * BLOCK, 128), F32),
            pltpu.VMEM((LEVS * BLOCK, 16, 128), F32),
        ],
        flops=2_000_000_000,
    )
    edge = jnp.concatenate([low, side[BIG:]], axis=0)
    edge, bias, codes = lax.optimization_barrier(
        (edge, bias, (qkv_codes, proj_codes, up_codes, down_codes.T))
    )
    edge = shifted(edge, LAT, 1)
    weights = call(
        weight_kernel,
        [((3, C, C), BF16), ((C, C), BF16), ((C, FF), BF16), ((C, FF), BF16)],
        (bit_widths, quant_scales, *codes),
        scalars=2,
        flops=1_000_000_000,
    )
    own, low, side, keep, give = call(
        main_kernel,
        [
            ((BIG, 2 * C), BF16),
            ((THIN, 2 * C), BF16),
            ((BIG + THIN, 2 * C), BF16),
            ((9 * C, 128), BF16),
            ((9 * C, 128), BF16),
        ],
        (own, side, edge, *weights, bias),
        [pltpu.VMEM((LEVS, ROWS, 2, SUB, 2 * C), F32)],
        flops=2_000_000_000,
        mib=32,
    )

    near = lax.axis_size(NEAR)
    far = lax.axis_size(FAR)
    rows = 9 * C // near
    padded = -(-rows // (8 * far)) * (8 * far)
    part = (keep.astype(F32) + swapped(give).astype(F32)).astype(BF16)
    part = exchange(part.reshape(near, rows, 128), NEAR)
    side = shifted(side, LON, -1)
    part, edge = call(
        sum_kernel,
        [((padded, 128), BF16), ((2 * THIN, 2 * C), BF16)],
        (part, low, side),
    )
    part = exchange(part.reshape(far, padded // far, 128), FAR)
    (part,) = call(sum_spread_kernel, [(part.shape, BF16)], (part,))
    part = exchange(part, FAR).reshape(padded, 128)
    part, edge = lax.optimization_barrier((part, edge))
    edge = shifted(edge, LAT, -1)
    (spread,) = call(copies_kernel, [((near, rows, 128), BF16)], (part,))
    half = exchange(spread, NEAR)
    merged, grad_tokens = call(
        finish_kernel,
        [((LEVS, ROWS // 2, COLS // 2, 2 * C), BF16), ((LEVS, ROWS, COLS, C), BF16)],
        (own, side, edge, merge_weight),
        [pltpu.VMEM((LEVS, ROWS, 2, SUB, 2 * C), F32)],
        flops=400_000_000,
    )
    half, merged, grad_tokens = lax.optimization_barrier((half, merged, grad_tokens))
    half = half.reshape(near * rows, 128)
    qkv, proj, up, down = call(
        spread_kernel,
        [((C, 3 * C), BF16), ((C, C), BF16), ((C, FF), BF16), ((C, FF), BF16)],
        (half, swapped(half)),
    )
    return (merged, grad_tokens, qkv, proj, up, down.T)


def solution(mesh):
    cols, rows = mesh.devices.shape
    fine = Mesh(mesh.devices.reshape(cols // 4, 2, 2, rows // 2, 2), LON + LAT)
    cells = P(None, LAT, LON, None)
    placed = (
        cells,
        cells,
        P(),
        P(),
        P(),
        P(),
        P(),
        P(),
        P(LAT, None, None, None),
        P(),
        P(),
    )
    return jax.shard_map(
        per_device,
        mesh=fine,
        in_specs=placed,
        out_specs=(cells, cells, P(), P(), P(), P()),
        check_vma=False,
    )
```

```python
import math

import jax
import jax.numpy as jnp
from jax import lax
from jax.experimental import pallas as pl
from jax.experimental.pallas import tpu as pltpu
from jax.sharding import Mesh
from jax.sharding import PartitionSpec as P

C = 192
HEADS = 6
FF = 768
HEAD_DIM = 32
WLAT = 6
WLON = 12
LAT_PAD = 11
WTOK = 144
POS = 3312

ROWS = 12
COLS = 12
LEVS = 2
OFF = WLAT // 2
HALF = WLON // 2
SUB = 8
FRAME = LEVS * ROWS * 2 * SUB
BLOCK = FRAME // 4
STACK = HEADS * BLOCK
BIG = LEVS * (ROWS - OFF) * SUB
THIN = LEVS * OFF * SUB
LOWS = 256
HIGHS = -(-POS // LOWS)

EPSILON = 1e-05
MASKED = -1000000000.0
F32 = jnp.float32
BF16 = jnp.bfloat16

LAT = ("y", "xl")
LON = ("z", "xh", "c")
NEAR = ("xh", "xl")
FAR = ("y", "z")


def iota(shape, dim):
    return lax.broadcasted_iota(jnp.int32, shape, dim)


def product(left, right):
    return lax.dot_general(left, right, (((1,), (0,)), ((), ())), preferred_element_type=F32)


def across(left, right):
    return lax.dot_general(left, right, (((1,), (1,)), ((), ())), preferred_element_type=F32)


def crossed(left, right):
    return lax.dot_general(left, right, (((0,), (0,)), ((), ())), preferred_element_type=F32)


def pack_kernel(tok_ref, cot_ref, own_ref, side_ref, low_ref, corner_ref):
    both = jnp.concatenate(
        [ref[...].astype(F32).reshape(LEVS * ROWS * COLS, C) for ref in (tok_ref, cot_ref)], axis=-1
    ).astype(BF16)

    def pick(first, count, col):
        shape = (LEVS * count * SUB, LEVS * ROWS * COLS)
        to = iota(shape, 0)
        lev = jnp.where(to >= count * SUB, 1, 0)
        row = (to >> 3) - lev * count + first
        sub = jnp.bitwise_and(to, SUB - 1)
        hot = (iota(shape, 1) == (row * COLS + col + sub) * 2 + lev) & (sub < HALF)
        return product(hot.astype(F32).astype(BF16), both).astype(BF16)

    own_ref[...] = pick(0, ROWS - OFF, 0)
    side_ref[...] = pick(0, ROWS - OFF, HALF)
    low_ref[...] = pick(ROWS - OFF, OFF, 0)
    corner_ref[...] = pick(ROWS - OFF, OFF, HALF)


def weight_kernel(
    bits_ref, scale_ref, cq_ref, cp_ref, cu_ref, cd_ref, wq_ref, wp_ref, wu_ref, wd_ref
):
    def dequant(codes, layer, fan_in):
        limit = jnp.left_shift(1, bits_ref[layer] - 1) - 1
        clipped = jnp.minimum(jnp.maximum(codes, -limit), limit).astype(F32)
        whole = jnp.full((1, 128), scale_ref[layer], jnp.int32).astype(F32)
        return clipped * (math.sqrt(C / fan_in) / whole)[:, :1]

    full = dequant(cq_ref[...], 0, C)
    for part in range(3):
        wq_ref[part] = full[:, part * C : (part + 1) * C].astype(BF16)
    wp_ref[...] = dequant(cp_ref[...], 1, C).astype(BF16)
    wu_ref[...] = dequant(cu_ref[...], 2, C).astype(BF16)
    wd_ref[...] = dequant(cd_ref[...], 3, FF).astype(BF16)


def bias_kernel(idx_ref, tab_ref, bias_ref, rows, places, found):
    rows[...] = jnp.zeros_like(rows)
    for head in range(HEADS):
        table = tab_ref[head].astype(F32)
        for high in range(HIGHS):
            width = min(LOWS, POS - high * LOWS)
            rows[high * 16 + head * 2 : high * 16 + head * 2 + 2, 0:width] = table[
                :, high * LOWS : high * LOWS + width
            ]
    table = rows[...].astype(BF16)

    index = idx_ref[...]
    parts = [
        lax.shift_right_logical(index, 8).astype(F32).astype(BF16),
        jnp.bitwise_and(index, LOWS - 1).astype(F32).astype(BF16),
    ]

    def token(where):
        sub = jnp.bitwise_and(where, SUB - 1)
        inside = (where >> 4) * WLON + jnp.bitwise_and(where >> 3, 1) * HALF + sub
        return jnp.where((sub < HALF) & (where < BLOCK), inside, -1000)

    for lev in range(LEVS):
        base = (1 - lev) * (WTOK // 2)
        pick_q = (iota((BLOCK, WTOK), 1) == token(iota((BLOCK, WTOK), 0)) + base).astype(F32)
        pick_k = (iota((WTOK, 128), 0) == token(iota((WTOK, 128), 1)) + base).astype(F32)
        for i, part in enumerate(parts):
            moved = product(product(pick_q.astype(BF16), part).astype(BF16), pick_k.astype(BF16))
            places[i, lev * BLOCK : (lev + 1) * BLOCK, :] = moved

    entry = iota((LOWS, 128), 0).astype(F32)

    def eight(group, carry):
        at = pl.multiple_of(group * SUB, SUB)
        high = places[0, pl.ds(at, SUB), :]
        low = places[1, pl.ds(at, SUB), :]
        hot = [(entry == low[s : s + 1]).astype(F32).astype(BF16) for s in range(HALF)]
        values = product(table, jnp.concatenate(hot, axis=1))
        for s in range(HALF):
            chosen = jnp.zeros((16, 128), F32)
            here = jnp.broadcast_to(high[s : s + 1], (16, 128))
            for i in range(HIGHS):
                candidate = values[i * 16 : (i + 1) * 16, s * 128 : (s + 1) * 128]
                chosen = jnp.where(here == float(i), candidate, chosen)
            found[at + s] = chosen
        found[at + HALF] = jnp.zeros((16, 128), F32)
        found[at + HALF + 1] = jnp.zeros((16, 128), F32)
        return carry

    lax.fori_loop(0, LEVS * BLOCK // SUB, eight, 0, unroll=24)

    key = iota((BLOCK, 128), 1)
    for win in range(2):
        row = lax.axis_index(LAT) * ROWS - OFF + win * WLAT + (key >> 4)
        usable = (row >= 0) & (row < lax.axis_size(LAT) * ROWS - LAT_PAD)
        usable = usable & (jnp.bitwise_and(key, SUB - 1) < HALF) & (key < BLOCK)
        for lev in range(LEVS):
            for head in range(HEADS):
                values = found[lev * BLOCK : (lev + 1) * BLOCK, head * 2 + win, :]
                values = jnp.where(usable, values, MASKED)
                bias_ref[lev * 2 + win, head * BLOCK : (head + 1) * BLOCK, :] = values.astype(BF16)


def unit(values):
    center = values - jnp.mean(values, axis=-1, keepdims=True)
    spread = jnp.mean(center * center, axis=-1, keepdims=True)
    scale = lax.rsqrt(spread + EPSILON)
    return center * scale, scale


def unit_back(normal, scale, upstream):
    level = jnp.mean(upstream, axis=-1, keepdims=True)
    along = jnp.mean(upstream * normal, axis=-1, keepdims=True)
    return scale * (upstream - level - normal * along)


def main_kernel(
    own_ref,
    side_ref,
    low_ref,
    corner_ref,
    wq_ref,
    wp_ref,
    wu_ref,
    wd_ref,
    bias_ref,
    own_out,
    low_out,
    side_out,
    keep_ref,
    give_ref,
    frame,
):
    below = ROWS - OFF

    def piece(ref, rows):
        return ref[...].astype(F32).reshape(LEVS, rows, SUB, 2 * C)

    frame[:, OFF:, 1] = piece(own_ref, below)
    frame[:, OFF:, 0] = piece(side_ref, below)
    frame[:, :OFF, 1] = piece(low_ref, OFF)
    frame[:, :OFF, 0] = piece(corner_ref, OFF)
    both = frame[...].reshape(FRAME, 2 * C)

    place = iota((FRAME, C), 0)
    row = lax.axis_index(LAT) * ROWS - OFF + (place >> 4) - jnp.where(place >= FRAME // 2, ROWS, 0)
    valid = (row >= 0) & (row < lax.axis_size(LAT) * ROWS - LAT_PAD)
    valid = valid & (jnp.bitwise_and(place, SUB - 1) < HALF)
    start = jnp.where(valid, both[:, :C], 0.0)
    d_out = jnp.where(valid, both[:, C:], 0.0)
    d_out_low = d_out.astype(BF16)

    normal, scale = unit(start)
    normed = normal.astype(BF16)
    query = product(normed, wq_ref[0]).astype(BF16)
    key = product(normed, wq_ref[1]).astype(BF16)
    value = product(normed, wq_ref[2]).astype(BF16)

    lane_head = iota((HEADS, 1, C), 2) >> 5
    head_mask = lane_head == iota((HEADS, 1, C), 0)
    mask_low = head_mask.astype(F32).astype(BF16)
    mask_full = head_mask.astype(F32)

    def spread_heads(block):
        return (block[None] * mask_low).reshape(STACK, C)

    def join_heads(stacked):
        return jnp.sum(stacked.reshape(HEADS, BLOCK, C) * mask_full, axis=0)

    saved = []
    heads_parts = []
    for block in range(4):
        at = slice(block * BLOCK, (block + 1) * BLOCK)
        q_stack = spread_heads(query[at])
        scores = across(q_stack, key[at]) * HEAD_DIM ** (-0.5)
        scores = scores + bias_ref[block][:, :BLOCK].astype(F32)
        weights = jnp.exp(scores - jnp.max(scores, axis=-1, keepdims=True))
        weights = weights / jnp.sum(weights, axis=-1, keepdims=True)
        weights_low = weights.astype(BF16)
        heads_parts.append(join_heads(product(weights_low, value[at])))
        saved.append((q_stack, weights, weights_low))
    heads = jnp.concatenate(heads_parts, axis=0).astype(BF16)

    resid = (start + product(heads, wp_ref[...])).astype(BF16).astype(F32)
    normal_two, scale_two = unit(resid)
    normed_two = normal_two.astype(BF16)
    pre_act = product(normed_two, wu_ref[...])
    inner = math.sqrt(2 / math.pi)
    square = pre_act * pre_act
    bend = jnp.tanh(inner * (pre_act + 0.044715 * (square * pre_act)))
    half = 0.5 * (1.0 + bend)
    hidden = (pre_act * half).astype(BF16)
    slope = half + 0.5 * pre_act * (1.0 - bend * bend) * (
        inner * (1.0 + (3 * 0.044715) * square)
    )
    final = jnp.where(valid, resid + across(hidden, wd_ref[...]), 0.0)

    d_hidden = product(d_out_low, wd_ref[...]).astype(BF16).astype(F32)
    d_pre = (slope * d_hidden).astype(BF16)
    d_normed_two = across(d_pre, wu_ref[...]).astype(BF16).astype(F32)
    d_resid = (d_out + unit_back(normal_two, scale_two, d_normed_two)).astype(BF16)
    d_heads = across(d_resid, wp_ref[...]).astype(BF16)

    dq_parts = []
    dk_parts = []
    dv_parts = []
    for block in range(4):
        at = slice(block * BLOCK, (block + 1) * BLOCK)
        q_stack, weights, weights_low = saved[block]
        d_stack = spread_heads(d_heads[at])
        d_weights = across(d_stack, value[at]).astype(BF16).astype(F32)
        dv_parts.append(crossed(weights_low, d_stack))
        inside = jnp.sum(weights * d_weights, axis=-1, keepdims=True)
        d_scores = (weights * (d_weights - inside) * HEAD_DIM ** (-0.5)).astype(BF16)
        dq_parts.append(join_heads(product(d_scores, key[at])))
        dk_parts.append(crossed(d_scores, q_stack))
    d_query = jnp.concatenate(dq_parts, axis=0).astype(BF16)
    d_key = jnp.concatenate(dk_parts, axis=0).astype(BF16)
    d_value = jnp.concatenate(dv_parts, axis=0).astype(BF16)

    d_normed = across(d_query, wq_ref[0]) + across(d_key, wq_ref[1]) + across(d_value, wq_ref[2])
    d_normed = d_normed.astype(BF16).astype(F32)
    grad = jnp.where(valid, d_resid.astype(F32) + unit_back(normal, scale, d_normed), 0.0)

    result = jnp.concatenate([final, grad], axis=-1).reshape(LEVS, ROWS, 2, SUB, 2 * C)

    def flat(part):
        return part.reshape(-1, 2 * C).astype(BF16)

    own_out[...] = flat(result[:, OFF:, 1])
    low_out[...] = flat(result[:, :OFF, 1])
    side_out[0:BIG, :] = flat(result[:, OFF:, 0])
    side_out[BIG:, :] = flat(result[:, :OFF, 0])

    small = [
        crossed(normed, d_query),
        crossed(normed, d_key),
        crossed(normed, d_value),
        crossed(heads, d_resid),
    ]
    tiles = [total[:, :128] for total in small]
    tiles += [
        jnp.concatenate([small[i][:, 128:], small[i + 1][:, 128:]], axis=-1) for i in (0, 2)
    ]
    for wide in (crossed(normed_two, d_pre), crossed(d_out_low, hidden)):
        tiles += [wide[:, i * 128 : (i + 1) * 128] for i in range(6)]
    half_tiles = len(tiles) // 2

    def store(ref, first):
        for i in range(half_tiles):
            ref[i * C : (i + 1) * C, :] = tiles[first + i].astype(BF16)

    core = lax.axis_index("c")

    @pl.when(core == 0)
    def _():
        store(keep_ref, 0)
        store(give_ref, half_tiles)

    @pl.when(core != 0)
    def _():
        store(keep_ref, half_tiles)
        store(give_ref, 0)


def spread_kernel(own_ref, other_ref, qkv_ref, proj_ref, up_ref, down_ref):
    first = lax.axis_index("c") == 0
    half_tiles = own_ref.shape[0] // C

    def tile(i):
        at = slice(i % half_tiles * C, (i % half_tiles + 1) * C)
        mine = first if i < half_tiles else jnp.logical_not(first)
        return jnp.where(mine, own_ref[at, :].astype(F32), other_ref[at, :].astype(F32))

    ends = [tile(4)[:, :64], tile(4)[:, 64:], tile(5)[:, :64], tile(5)[:, 64:]]
    small = [jnp.concatenate([tile(i), ends[i]], axis=-1) for i in range(4)]
    qkv_ref[...] = jnp.concatenate(small[:3], axis=-1).astype(BF16)
    proj_ref[...] = small[3].astype(BF16)
    for i in range(6):
        up_ref[:, i * 128 : (i + 1) * 128] = tile(6 + i).astype(BF16)
        down_ref[:, i * 128 : (i + 1) * 128] = tile(12 + i).astype(BF16)


def finish_kernel(own_ref, side_ref, edge_ref, weight_ref, merged_ref, grad_ref, frame):
    above = ROWS - OFF

    def piece(block, rows):
        return block.astype(F32).reshape(LEVS, rows, SUB, 2 * C)

    frame[:, :above, 0] = piece(own_ref[...], above)
    frame[:, above:, 0] = piece(edge_ref[0:THIN, :], OFF)
    frame[:, :above, 1] = piece(side_ref[0:BIG, :], above)
    frame[:, above:, 1] = piece(edge_ref[THIN:, :], OFF)
    both = frame[...].reshape(FRAME, 2 * C)
    final = both[:, :C].astype(BF16)
    grad = both[:, C:].astype(BF16)

    def source(col):
        return jnp.where(col >= HALF, col + (SUB - HALF), col)

    to = iota((FRAME, FRAME), 0)
    col = jnp.bitwise_and(to, 15)
    pick = (iota((FRAME, FRAME), 1) == to - col + source(col)) & (col < COLS)
    moved = product(pick.astype(F32).astype(BF16), grad).reshape(LEVS, ROWS, 16, C)
    grad_ref[...] = moved[:, :, :COLS, :].astype(BF16)

    count = LEVS * (ROWS // 2) * SUB
    to = iota((count, FRAME), 0)
    lev = jnp.where(to >= count // 2, 1, 0)
    pair = (to >> 3) - lev * (ROWS // 2)
    parts = []
    for down in range(2):
        for right in range(2):
            col = 2 * jnp.bitwise_and(to, SUB - 1) + right
            wanted = lev * (FRAME // 2) + (2 * pair + down) * 16 + source(col)
            pick = (iota((count, FRAME), 1) == wanted) & (col < COLS)
            parts.append(product(pick.astype(F32).astype(BF16), final))
    width = 4 * C
    mean = sum(jnp.sum(part, axis=-1, keepdims=True) for part in parts) / width
    centers = [part - mean for part in parts]
    spread = sum(jnp.sum(part * part, axis=-1, keepdims=True) for part in centers) / width
    scale = lax.rsqrt(spread + EPSILON)
    total = jnp.zeros((count, 2 * C), F32)
    for i, part in enumerate(centers):
        total = total + product((part * scale).astype(BF16), weight_ref[i * C : (i + 1) * C, :])
    merged_ref[...] = total.reshape(LEVS, ROWS // 2, SUB, 2 * C)[:, :, :HALF, :].astype(BF16)


def call(kernel, outs, args, scratch=(), scalars=0, flops=0, mib=16):
    vmem = pl.BlockSpec(memory_space=pltpu.VMEM)
    smem = pl.BlockSpec(memory_space=pltpu.SMEM)
    moved = sum(math.prod(a.shape) * a.dtype.itemsize for a in args)
    moved += sum(math.prod(s) * jnp.dtype(t).itemsize for s, t in outs)
    return pl.pallas_call(
        kernel,
        out_shape=[jax.ShapeDtypeStruct(s, t) for s, t in outs],
        in_specs=[smem] * scalars + [vmem] * (len(args) - scalars),
        out_specs=[vmem] * len(outs),
        scratch_shapes=list(scratch),
        compiler_params=pltpu.CompilerParams(vmem_limit_bytes=mib * 1024 * 1024),
        cost_estimate=pl.CostEstimate(flops=flops, bytes_accessed=moved, transcendentals=0),
    )(*args)


def shifted(block, lat_step, lon_step):
    rows = lax.axis_size(LAT)
    cols = lax.axis_size(LON)
    if lat_step and lon_step:
        route = [
            (col * rows + row, (col + lon_step) % cols * rows + row + lat_step)
            for col in range(cols)
            for row in range(rows)
            if 0 <= row + lat_step < rows
        ]
        return lax.ppermute(block, LON + LAT, route)
    if lat_step:
        route = [(r, r + lat_step) for r in range(rows) if 0 <= r + lat_step < rows]
        return lax.ppermute(block, LAT, route)
    return lax.ppermute(block, LON, [(c, (c + lon_step) % cols) for c in range(cols)])


def exchange(parts, axes):
    return lax.all_to_all(parts, axes, 0, 0)


def swapped(block):
    return lax.ppermute(block, "c", [(0, 1), (1, 0)])


def sum_kernel(parts_ref, low_ref, side_ref, out_ref, edge_ref):
    edge_ref[0:THIN, :] = low_ref[...]
    edge_ref[THIN:, :] = side_ref[BIG:, :]
    count, rows, _ = parts_ref.shape
    total = parts_ref[0].astype(F32)
    for i in range(1, count):
        total = total + parts_ref[i].astype(F32)
    out_ref[0:rows, :] = total.astype(BF16)
    if rows < out_ref.shape[0]:
        out_ref[rows:, :] = jnp.zeros((out_ref.shape[0] - rows, 128), BF16)


def sum_spread_kernel(parts_ref, out_ref):
    total = jnp.sum(parts_ref[...].astype(F32), axis=0).astype(BF16)
    out_ref[...] = jnp.broadcast_to(total[None], out_ref.shape)


def copies_kernel(part_ref, out_ref):
    count, rows, _ = out_ref.shape
    for i in range(count):
        out_ref[i] = part_ref[0:rows, :]


def per_device(
    tokens,
    cotangent,
    qkv_codes,
    proj_codes,
    up_codes,
    down_codes,
    bit_widths,
    quant_scales,
    bias_table,
    bias_index,
    merge_weight,
):
    own, side, low, corner = call(
        pack_kernel,
        [((BIG, 2 * C), BF16)] * 2 + [((THIN, 2 * C), BF16)] * 2,
        (tokens.transpose(1, 2, 0, 3), cotangent.transpose(1, 2, 0, 3)),
    )
    side, low, corner = shifted(side, 0, 1), shifted(low, 1, 0), shifted(corner, 1, 1)
    (bias,) = call(
        bias_kernel,
        [((4, STACK, 128), BF16)],
        (
            bias_index.reshape(WTOK, WTOK),
            bias_table.transpose(1, 2, 0, 3).reshape(HEADS, 2, POS),
        ),
        [
            pltpu.VMEM((HIGHS * 16, LOWS), F32),
            pltpu.VMEM((2, LEVS * BLOCK, 128), F32),
            pltpu.VMEM((LEVS * BLOCK, 16, 128), F32),
        ],
        flops=2_000_000_000,
    )
    weights = call(
        weight_kernel,
        [((3, C, C), BF16), ((C, C), BF16), ((C, FF), BF16), ((C, FF), BF16)],
        (bit_widths, quant_scales, qkv_codes, proj_codes, up_codes, down_codes.T),
        scalars=2,
        flops=1_000_000_000,
    )
    own, low, side, keep, give = call(
        main_kernel,
        [
            ((BIG, 2 * C), BF16),
            ((THIN, 2 * C), BF16),
            ((BIG + THIN, 2 * C), BF16),
            ((9 * C, 128), BF16),
            ((9 * C, 128), BF16),
        ],
        (own, side, low, corner, *weights, bias),
        [pltpu.VMEM((LEVS, ROWS, 2, SUB, 2 * C), F32)],
        flops=2_000_000_000,
        mib=32,
    )

    near = lax.axis_size(NEAR)
    far = lax.axis_size(FAR)
    rows = 9 * C // near
    padded = -(-rows // (8 * far)) * (8 * far)
    part = (keep.astype(F32) + swapped(give).astype(F32)).astype(BF16)
    part = exchange(part.reshape(near, rows, 128), NEAR)
    side = shifted(side, 0, -1)
    part, edge = call(
        sum_kernel,
        [((padded, 128), BF16), ((2 * THIN, 2 * C), BF16)],
        (part, low, side),
    )
    part = exchange(part.reshape(far, padded // far, 128), FAR)
    (part,) = call(sum_spread_kernel, [(part.shape, BF16)], (part,))
    part = exchange(part, FAR).reshape(padded, 128)
    part, edge = lax.optimization_barrier((part, edge))
    edge = shifted(edge, -1, 0)
    (spread,) = call(copies_kernel, [((near, rows, 128), BF16)], (part,))
    half = exchange(spread, NEAR)
    merged, grad_tokens = call(
        finish_kernel,
        [((LEVS, ROWS // 2, COLS // 2, 2 * C), BF16), ((LEVS, ROWS, COLS, C), BF16)],
        (own, side, edge, merge_weight),
        [pltpu.VMEM((LEVS, ROWS, 2, SUB, 2 * C), F32)],
        flops=400_000_000,
    )
    half, merged, grad_tokens = lax.optimization_barrier((half, merged, grad_tokens))
    half = half.reshape(near * rows, 128)
    qkv, proj, up, down = call(
        spread_kernel,
        [((C, 3 * C), BF16), ((C, C), BF16), ((C, FF), BF16), ((C, FF), BF16)],
        (half, swapped(half)),
    )
    return (merged, grad_tokens, qkv, proj, up, down.T)


def solution(mesh):
    cols, rows = mesh.devices.shape
    fine = Mesh(mesh.devices.reshape(cols // 4, 2, 2, rows // 2, 2), LON + LAT)
    cells = P(None, LAT, LON, None)
    placed = (
        cells,
        cells,
        P(),
        P(),
        P(),
        P(),
        P(),
        P(),
        P(LAT, None, None, None),
        P(),
        P(),
    )
    return jax.shard_map(
        per_device,
        mesh=fine,
        in_specs=placed,
        out_specs=(cells, cells, P(), P(), P(), P()),
        check_vma=False,
    )
```

```python
import math

import jax
import jax.numpy as jnp
from jax import lax
from jax.experimental import pallas as pl
from jax.experimental.pallas import tpu as pltpu
from jax.sharding import Mesh
from jax.sharding import PartitionSpec as P

C = 192
HEADS = 6
FF = 768
HEAD_DIM = 32
WLAT = 6
WLON = 12
LAT_PAD = 11
WTOK = 144
POS = 3312

ROWS = 12
COLS = 12
LEVS = 2
OFF = WLAT // 2
HALF = WLON // 2
SUB = 8
FRAME = LEVS * ROWS * COLS
BLOCK = FRAME // 4
STACK = HEADS * BLOCK
BIG = 112
THIN = 48
LOWS = 256
HIGHS = -(-POS // LOWS)

EPSILON = 1e-05
MASKED = -1000000000.0
F32 = jnp.float32
BF16 = jnp.bfloat16

LAT = ("y", "xl")
LON = ("z", "xh", "c")
NEAR = ("xh", "xl")
FAR = ("y", "z")


def iota(shape, dim):
    return lax.broadcasted_iota(jnp.int32, shape, dim)


def product(left, right):
    return lax.dot_general(left, right, (((1,), (0,)), ((), ())), preferred_element_type=F32)


def across(left, right):
    return lax.dot_general(left, right, (((1,), (1,)), ((), ())), preferred_element_type=F32)


def crossed(left, right):
    return lax.dot_general(left, right, (((0,), (0,)), ((), ())), preferred_element_type=F32)


def over(values, size):
    return ((values.astype(F32) + 0.5) * (1.0 / size)).astype(jnp.int32)


def in_piece(at, count):
    lev = jnp.where(at >= count * HALF, 1, 0)
    rest = at - lev * (count * HALF)
    row = over(rest, HALF)
    return lev, row, rest - row * HALF, (at >= 0) & (at < LEVS * count * HALF)


def frame_place(at):
    place = jnp.full(at.shape, -1, jnp.int32)
    first = 0
    for size, count, half in ((BIG, ROWS - OFF, 1), (THIN, OFF, 1), (BIG, ROWS - OFF, 0), (THIN, OFF, 0)):
        lev, row, sub, used = in_piece(at - first, count)
        skip = ROWS - count if count != OFF else 0
        token = (lev * ROWS + row + skip) * COLS + half * HALF + sub
        place = jnp.where(used, token, place)
        first += size
    return place


def one_hot(match):
    return match.astype(F32).astype(BF16)


def pack_kernel(tok_ref, cot_ref, own_ref, side_ref, low_ref, corner_ref):
    both = jnp.concatenate(
        [ref[...].astype(F32).reshape(LEVS * ROWS * COLS, C) for ref in (tok_ref, cot_ref)], axis=-1
    ).astype(BF16)

    def pick(first, count, col, size):
        shape = (size, LEVS * ROWS * COLS)
        lev, row, sub, used = in_piece(iota(shape, 0), count)
        token = ((row + first) * COLS + col + sub) * 2 + lev
        return product(one_hot((iota(shape, 1) == token) & used), both).astype(BF16)

    own_ref[...] = pick(0, ROWS - OFF, 0, BIG)
    side_ref[...] = pick(0, ROWS - OFF, HALF, BIG)
    low_ref[...] = pick(ROWS - OFF, OFF, 0, THIN)
    corner_ref[...] = pick(ROWS - OFF, OFF, HALF, THIN)


def weight_kernel(quant_ref, cq_ref, cp_ref, cu_ref, cd_ref, wq_ref, wp_ref, wu_ref, wd_ref):
    def dequant(codes, layer):
        limit = quant_ref[layer : layer + 1, 0:1]
        factor = quant_ref[layer + 4 : layer + 5, 0:1]
        return jnp.minimum(jnp.maximum(codes.astype(F32), -limit), limit) * factor

    full = dequant(cq_ref[...], 0)
    for part in range(3):
        wq_ref[part] = full[:, part * C : (part + 1) * C].astype(BF16)
    wp_ref[...] = dequant(cp_ref[...], 1).astype(BF16)
    wu_ref[...] = dequant(cu_ref[...], 2).astype(BF16)
    wd_ref[...] = dequant(cd_ref[...], 3).astype(BF16)


def bias_kernel(
    bits_ref, scale_ref, idx_ref, tab_ref, bias_ref, quant_ref, rows, places, found
):
    for layer, fan_in in enumerate((C, C, C, FF)):
        limit = jnp.left_shift(1, bits_ref[layer] - 1) - 1
        quant_ref[layer : layer + 1, :] = jnp.full((1, 128), limit, jnp.int32).astype(F32)
        scale = jnp.full((1, 128), scale_ref[layer], jnp.int32).astype(F32)
        quant_ref[layer + 4 : layer + 5, :] = math.sqrt(C / fan_in) / scale

    rows[...] = jnp.zeros_like(rows)
    for head in range(HEADS):
        table = tab_ref[head].astype(F32)
        for high in range(HIGHS):
            width = min(LOWS, POS - high * LOWS)
            rows[high * 16 + head * 2 : high * 16 + head * 2 + 2, 0:width] = table[
                :, high * LOWS : high * LOWS + width
            ]
    table = rows[...].astype(BF16)

    index = idx_ref[...]
    places[...] = jnp.zeros_like(places)
    for lev in range(LEVS):
        base = (1 - lev) * BLOCK
        inside = index[base : base + BLOCK, base : base + BLOCK]
        at = slice(lev * BLOCK, (lev + 1) * BLOCK)
        places[0, at, 0:BLOCK] = lax.shift_right_logical(inside, 8).astype(F32)
        places[1, at, 0:BLOCK] = jnp.bitwise_and(inside, LOWS - 1).astype(F32)

    entry = iota((LOWS, 128), 0).astype(F32)

    def eight(group, carry):
        at = pl.multiple_of(group * SUB, SUB)
        high = places[0, pl.ds(at, SUB), :]
        low = places[1, pl.ds(at, SUB), :]
        hot = [one_hot(entry == low[s : s + 1]) for s in range(SUB)]
        values = product(table, jnp.concatenate(hot, axis=1))
        for s in range(SUB):
            chosen = jnp.zeros((16, 128), F32)
            here = jnp.broadcast_to(high[s : s + 1], (16, 128))
            for i in range(HIGHS):
                candidate = values[i * 16 : (i + 1) * 16, s * 128 : (s + 1) * 128]
                chosen = jnp.where(here == float(i), candidate, chosen)
            found[at + s] = chosen
        return carry

    lax.fori_loop(0, LEVS * BLOCK // SUB, eight, 0, unroll=18)

    key = iota((BLOCK, 128), 1)
    for win in range(2):
        row = lax.axis_index(LAT) * ROWS - OFF + win * WLAT + over(key, WLON)
        usable = (row >= 0) & (row < lax.axis_size(LAT) * ROWS - LAT_PAD) & (key < BLOCK)
        for lev in range(LEVS):
            for head in range(HEADS):
                values = found[lev * BLOCK : (lev + 1) * BLOCK, head * 2 + win, :]
                bias_ref[lev * 2 + win, head] = jnp.where(usable, values, MASKED)


def unit(values):
    center = values - jnp.mean(values, axis=-1, keepdims=True)
    spread = jnp.mean(center * center, axis=-1, keepdims=True)
    scale = lax.rsqrt(spread + EPSILON)
    return center * scale, scale


def unit_back(normal, scale, upstream):
    level = jnp.mean(upstream, axis=-1, keepdims=True)
    along = jnp.mean(upstream * normal, axis=-1, keepdims=True)
    return scale * (upstream - level - normal * along)


def main_kernel(
    own_ref,
    side_ref,
    low_ref,
    corner_ref,
    wq_ref,
    wp_ref,
    wu_ref,
    wd_ref,
    bias_ref,
    own_out,
    low_out,
    side_out,
    keep_ref,
    give_ref,
):
    total = 2 * (BIG + THIN)
    pieces = [ref[...] for ref in (own_ref, low_ref, side_ref, corner_ref)]
    shape = (FRAME, total)
    order = one_hot(iota(shape, 0) == frame_place(iota(shape, 1)))
    both = product(order, jnp.concatenate(pieces, axis=0))

    place = iota((FRAME, C), 0)
    row = lax.axis_index(LAT) * ROWS - OFF + over(place, COLS)
    row = row - jnp.where(place >= FRAME // 2, ROWS, 0)
    valid = (row >= 0) & (row < lax.axis_size(LAT) * ROWS - LAT_PAD)
    start = jnp.where(valid, both[:, :C], 0.0)
    d_out = jnp.where(valid, both[:, C:], 0.0)
    d_out_low = d_out.astype(BF16)

    normal, scale = unit(start)
    normed = normal.astype(BF16)
    query = product(normed, wq_ref[0]).astype(BF16).astype(F32)
    key = product(normed, wq_ref[1]).astype(BF16).astype(F32)
    value = product(normed, wq_ref[2]).astype(BF16).astype(F32)

    lane_head = iota((HEADS, 1, C), 2) >> 5
    head_mask = lane_head == iota((HEADS, 1, C), 0)
    mask_full = head_mask.astype(F32)

    def spread_heads(block):
        return (block[None] * mask_full).reshape(STACK, C).astype(BF16)

    def join_heads(stacked):
        return jnp.sum(stacked.reshape(HEADS, BLOCK, C) * mask_full, axis=0)

    saved = []
    heads_parts = []
    for block in range(4):
        at = slice(block * BLOCK, (block + 1) * BLOCK)
        q_stack = spread_heads(query[at])
        scores = across(q_stack, key[at].astype(BF16)) * HEAD_DIM ** (-0.5)
        scores = scores + bias_ref[block].reshape(STACK, 128)[:, :BLOCK]
        weights = jnp.exp(scores - jnp.max(scores, axis=-1, keepdims=True))
        weights = weights / jnp.sum(weights, axis=-1, keepdims=True)
        weights_low = weights.astype(BF16)
        heads_parts.append(join_heads(product(weights_low, value[at].astype(BF16))))
        saved.append((q_stack, weights, weights_low))
    heads = jnp.concatenate(heads_parts, axis=0).astype(BF16)

    resid = (start + product(heads, wp_ref[...])).astype(BF16).astype(F32)
    normal_two, scale_two = unit(resid)
    normed_two = normal_two.astype(BF16)
    pre_act = product(normed_two, wu_ref[...])
    inner = math.sqrt(2 / math.pi)
    square = pre_act * pre_act
    bend = jnp.tanh(inner * (pre_act + 0.044715 * (square * pre_act)))
    half = 0.5 * (1.0 + bend)
    hidden = (pre_act * half).astype(BF16)
    slope = half + 0.5 * pre_act * (1.0 - bend * bend) * (
        inner * (1.0 + (3 * 0.044715) * square)
    )
    final = jnp.where(valid, resid + across(hidden, wd_ref[...]), 0.0)

    d_hidden = product(d_out_low, wd_ref[...]).astype(BF16).astype(F32)
    d_pre = (slope * d_hidden).astype(BF16)
    d_normed_two = across(d_pre, wu_ref[...]).astype(BF16).astype(F32)
    d_resid = (d_out + unit_back(normal_two, scale_two, d_normed_two)).astype(BF16)
    d_heads = across(d_resid, wp_ref[...]).astype(BF16).astype(F32)

    dq_parts = []
    dk_parts = []
    dv_parts = []
    for block in range(4):
        at = slice(block * BLOCK, (block + 1) * BLOCK)
        q_stack, weights, weights_low = saved[block]
        d_stack = spread_heads(d_heads[at])
        d_weights = across(d_stack, value[at].astype(BF16)).astype(BF16).astype(F32)
        dv_parts.append(crossed(weights_low, d_stack))
        inside = jnp.sum(weights * d_weights, axis=-1, keepdims=True)
        d_scores = (weights * (d_weights - inside) * HEAD_DIM ** (-0.5)).astype(BF16)
        dq_parts.append(join_heads(product(d_scores, key[at].astype(BF16))))
        dk_parts.append(crossed(d_scores, q_stack))
    d_query = jnp.concatenate(dq_parts, axis=0).astype(BF16)
    d_key = jnp.concatenate(dk_parts, axis=0).astype(BF16)
    d_value = jnp.concatenate(dv_parts, axis=0).astype(BF16)

    d_normed = across(d_query, wq_ref[0]) + across(d_key, wq_ref[1]) + across(d_value, wq_ref[2])
    d_normed = d_normed.astype(BF16).astype(F32)
    grad = jnp.where(valid, d_resid.astype(F32) + unit_back(normal, scale, d_normed), 0.0)

    result = jnp.concatenate([final, grad], axis=-1).astype(BF16)
    shape = (total, FRAME)
    order = one_hot(iota(shape, 1) == frame_place(iota(shape, 0)))
    parted = product(order, result).astype(BF16)
    own_out[...] = parted[0:BIG]
    low_out[...] = parted[BIG : BIG + THIN]
    side_out[...] = parted[BIG + THIN :]

    small = [
        crossed(normed, d_query),
        crossed(normed, d_key),
        crossed(normed, d_value),
        crossed(heads, d_resid),
    ]
    tiles = [total[:, :128] for total in small]
    tiles += [
        jnp.concatenate([small[i][:, 128:], small[i + 1][:, 128:]], axis=-1) for i in (0, 2)
    ]
    for wide in (crossed(normed_two, d_pre), crossed(d_out_low, hidden)):
        tiles += [wide[:, i * 128 : (i + 1) * 128] for i in range(6)]
    half_tiles = len(tiles) // 2

    def store(ref, first):
        for i in range(half_tiles):
            ref[i * C : (i + 1) * C, :] = tiles[first + i].astype(BF16)

    core = lax.axis_index("c")

    @pl.when(core == 0)
    def _():
        store(keep_ref, 0)
        store(give_ref, half_tiles)

    @pl.when(core != 0)
    def _():
        store(keep_ref, half_tiles)
        store(give_ref, 0)


def spread_kernel(own_ref, other_ref, qkv_ref, proj_ref, up_ref, down_ref):
    first = lax.axis_index("c") == 0
    half_tiles = own_ref.shape[0] // C

    def tile(i):
        at = slice(i % half_tiles * C, (i % half_tiles + 1) * C)
        mine = first if i < half_tiles else jnp.logical_not(first)
        return jnp.where(mine, own_ref[at, :].astype(F32), other_ref[at, :].astype(F32))

    ends = [tile(4)[:, :64], tile(4)[:, 64:], tile(5)[:, :64], tile(5)[:, 64:]]
    small = [jnp.concatenate([tile(i), ends[i]], axis=-1) for i in range(4)]
    qkv_ref[...] = jnp.concatenate(small[:3], axis=-1).astype(BF16)
    proj_ref[...] = small[3].astype(BF16)
    for i in range(6):
        up_ref[:, i * 128 : (i + 1) * 128] = tile(6 + i).astype(BF16)
        down_ref[:, i * 128 : (i + 1) * 128] = tile(12 + i).astype(BF16)


def finish_kernel(own_ref, side_ref, edge_ref, weight_ref, merged_ref, grad_ref):
    both = jnp.concatenate([own_ref[...], edge_ref[...], side_ref[0:BIG, :]], axis=0)
    final = both[:, :C]
    grad = both[:, C:]
    total = 2 * (BIG + THIN)
    above = ROWS - OFF

    def source(lev, row, col):
        right = col >= HALF
        below = row >= above
        thin = (lev * OFF + row - above) * HALF + jnp.where(right, BIG + THIN, BIG)
        big = (lev * above + row) * HALF + jnp.where(right, BIG + 2 * THIN, 0)
        return jnp.where(below, thin, big) + col - jnp.where(right, HALF, 0)

    count = LEVS * ROWS * 16
    to = iota((count, total), 0)
    lev = jnp.where(to >= count // 2, 1, 0)
    col = jnp.bitwise_and(to, 15)
    pick = (iota((count, total), 1) == source(lev, (to >> 4) - lev * ROWS, col)) & (col < COLS)
    moved = product(one_hot(pick), grad).reshape(LEVS, ROWS, 16, C)
    grad_ref[...] = moved[:, :, :COLS, :].astype(BF16)

    count = LEVS * (ROWS // 2) * SUB
    to = iota((count, total), 0)
    lev = jnp.where(to >= count // 2, 1, 0)
    pair = (to >> 3) - lev * (ROWS // 2)
    parts = []
    for down in range(2):
        for right in range(2):
            col = 2 * jnp.bitwise_and(to, SUB - 1) + right
            pick = (iota((count, total), 1) == source(lev, 2 * pair + down, col)) & (col < COLS)
            parts.append(product(one_hot(pick), final))
    width = 4 * C
    mean = sum(jnp.sum(part, axis=-1, keepdims=True) for part in parts) / width
    centers = [part - mean for part in parts]
    spread = sum(jnp.sum(part * part, axis=-1, keepdims=True) for part in centers) / width
    scale = lax.rsqrt(spread + EPSILON)
    total = jnp.zeros((count, 2 * C), F32)
    for i, part in enumerate(centers):
        total = total + product((part * scale).astype(BF16), weight_ref[i * C : (i + 1) * C, :])
    merged_ref[...] = total.reshape(LEVS, ROWS // 2, SUB, 2 * C)[:, :, :HALF, :].astype(BF16)


def call(kernel, outs, args, scratch=(), scalars=0, flops=0, mib=16):
    vmem = pl.BlockSpec(memory_space=pltpu.VMEM)
    smem = pl.BlockSpec(memory_space=pltpu.SMEM)
    moved = sum(math.prod(a.shape) * a.dtype.itemsize for a in args)
    moved += sum(math.prod(s) * jnp.dtype(t).itemsize for s, t in outs)
    return pl.pallas_call(
        kernel,
        out_shape=[jax.ShapeDtypeStruct(s, t) for s, t in outs],
        in_specs=[smem] * scalars + [vmem] * (len(args) - scalars),
        out_specs=[vmem] * len(outs),
        scratch_shapes=list(scratch),
        compiler_params=pltpu.CompilerParams(vmem_limit_bytes=mib * 1024 * 1024),
        cost_estimate=pl.CostEstimate(flops=flops, bytes_accessed=moved, transcendentals=0),
    )(*args)


def shifted(block, lat_step, lon_step):
    rows = lax.axis_size(LAT)
    cols = lax.axis_size(LON)
    if lat_step and lon_step:
        route = [
            (col * rows + row, (col + lon_step) % cols * rows + row + lat_step)
            for col in range(cols)
            for row in range(rows)
            if 0 <= row + lat_step < rows
        ]
        return lax.ppermute(block, LON + LAT, route)
    if lat_step:
        route = [(r, r + lat_step) for r in range(rows) if 0 <= r + lat_step < rows]
        return lax.ppermute(block, LAT, route)
    return lax.ppermute(block, LON, [(c, (c + lon_step) % cols) for c in range(cols)])


def exchange(parts, axes):
    return lax.all_to_all(parts, axes, 0, 0)


def swapped(block):
    return lax.ppermute(block, "c", [(0, 1), (1, 0)])


def sum_kernel(parts_ref, low_ref, side_ref, out_ref, edge_ref):
    edge_ref[0:THIN, :] = low_ref[...]
    edge_ref[THIN:, :] = side_ref[BIG:, :]
    count, rows, _ = parts_ref.shape
    total = parts_ref[0].astype(F32)
    for i in range(1, count):
        total = total + parts_ref[i].astype(F32)
    out_ref[0:rows, :] = total.astype(BF16)
    if rows < out_ref.shape[0]:
        out_ref[rows:, :] = jnp.zeros((out_ref.shape[0] - rows, 128), BF16)


def sum_spread_kernel(parts_ref, out_ref):
    total = jnp.sum(parts_ref[...].astype(F32), axis=0).astype(BF16)
    out_ref[...] = jnp.broadcast_to(total[None], out_ref.shape)


def copies_kernel(part_ref, out_ref):
    count, rows, _ = out_ref.shape
    for i in range(count):
        out_ref[i] = part_ref[0:rows, :]


def per_device(
    tokens,
    cotangent,
    qkv_codes,
    proj_codes,
    up_codes,
    down_codes,
    bit_widths,
    quant_scales,
    bias_table,
    bias_index,
    merge_weight,
):
    own, side, low, corner = call(
        pack_kernel,
        [((BIG, 2 * C), BF16)] * 2 + [((THIN, 2 * C), BF16)] * 2,
        (tokens.transpose(1, 2, 0, 3), cotangent.transpose(1, 2, 0, 3)),
    )
    side, low, corner = shifted(side, 0, 1), shifted(low, 1, 0), shifted(corner, 1, 1)
    bias, quant = call(
        bias_kernel,
        [((4, HEADS, BLOCK, 128), F32), ((8, 128), F32)],
        (
            bit_widths,
            quant_scales,
            bias_index.reshape(WTOK, WTOK),
            bias_table.transpose(1, 2, 0, 3).reshape(HEADS, 2, POS),
        ),
        [
            pltpu.VMEM((HIGHS * 16, LOWS), F32),
            pltpu.VMEM((2, LEVS * BLOCK, 128), F32),
            pltpu.VMEM((LEVS * BLOCK, 16, 128), F32),
        ],
        scalars=2,
        flops=2_000_000_000,
    )
    weights = call(
        weight_kernel,
        [((3, C, C), BF16), ((C, C), BF16), ((C, FF), BF16), ((C, FF), BF16)],
        (quant, qkv_codes, proj_codes, up_codes, down_codes.T),
        flops=1_000_000_000,
    )
    own, low, side, keep, give = call(
        main_kernel,
        [
            ((BIG, 2 * C), BF16),
            ((THIN, 2 * C), BF16),
            ((BIG + THIN, 2 * C), BF16),
            ((9 * C, 128), BF16),
            ((9 * C, 128), BF16),
        ],
        (own, side, low, corner, *weights, bias),
        flops=2_000_000_000,
        mib=32,
    )

    near = lax.axis_size(NEAR)
    far = lax.axis_size(FAR)
    rows = 9 * C // near
    padded = -(-rows // (8 * far)) * (8 * far)
    part = (keep.astype(F32) + swapped(give).astype(F32)).astype(BF16)
    part = exchange(part.reshape(near, rows, 128), NEAR)
    side = shifted(side, 0, -1)
    part, edge = call(
        sum_kernel,
        [((padded, 128), BF16), ((2 * THIN, 2 * C), BF16)],
        (part, low, side),
    )
    part = exchange(part.reshape(far, padded // far, 128), FAR)
    (part,) = call(sum_spread_kernel, [(part.shape, BF16)], (part,))
    part = exchange(part, FAR).reshape(padded, 128)
    part, edge = lax.optimization_barrier((part, edge))
    edge = shifted(edge, -1, 0)
    (spread,) = call(copies_kernel, [((near, rows, 128), BF16)], (part,))
    half = exchange(spread, NEAR)
    merged, grad_tokens = call(
        finish_kernel,
        [((LEVS, ROWS // 2, COLS // 2, 2 * C), BF16), ((LEVS, ROWS, COLS, C), BF16)],
        (own, side, edge, merge_weight),
        flops=400_000_000,
    )
    half, merged, grad_tokens = lax.optimization_barrier((half, merged, grad_tokens))
    half = half.reshape(near * rows, 128)
    qkv, proj, up, down = call(
        spread_kernel,
        [((C, 3 * C), BF16), ((C, C), BF16), ((C, FF), BF16), ((C, FF), BF16)],
        (half, swapped(half)),
    )
    return (merged, grad_tokens, qkv, proj, up, down.T)


def solution(mesh):
    cols, rows = mesh.devices.shape
    fine = Mesh(mesh.devices.reshape(cols // 4, 2, 2, rows // 2, 2), LON + LAT)
    cells = P(None, LAT, LON, None)
    placed = (
        cells,
        cells,
        P(),
        P(),
        P(),
        P(),
        P(),
        P(),
        P(LAT, None, None, None),
        P(),
        P(),
    )
    return jax.shard_map(
        per_device,
        mesh=fine,
        in_specs=placed,
        out_specs=(cells, cells, P(), P(), P(), P()),
        check_vma=False,
    )
```

```python
import math

import jax
import jax.numpy as jnp
from jax import lax
from jax.experimental import pallas as pl
from jax.experimental.pallas import tpu as pltpu
from jax.sharding import Mesh
from jax.sharding import PartitionSpec as P

C = 192
HEADS = 6
FF = 768
HEAD_DIM = 32
WLAT = 6
WLON = 12
LAT_PAD = 11
WTOK = 144
POS = 3312

ROWS = 12
COLS = 12
LEVS = 2
OFF = WLAT // 2
HALF = WLON // 2
SUB = 8
FRAME = LEVS * ROWS * COLS
BLOCK = FRAME // 4
STACK = HEADS * BLOCK
BIG = 112
THIN = 48
LOWS = 256
HIGHS = -(-POS // LOWS)

EPSILON = 1e-05
MASKED = -1000000000.0
F32 = jnp.float32
BF16 = jnp.bfloat16

LAT = ("y", "xl")
LON = ("z", "xh", "c")
NEAR = ("xh", "xl")
FAR = ("y", "z")


def iota(shape, dim):
    return lax.broadcasted_iota(jnp.int32, shape, dim)


def product(left, right):
    return lax.dot_general(left, right, (((1,), (0,)), ((), ())), preferred_element_type=F32)


def across(left, right):
    return lax.dot_general(left, right, (((1,), (1,)), ((), ())), preferred_element_type=F32)


def crossed(left, right):
    return lax.dot_general(left, right, (((0,), (0,)), ((), ())), preferred_element_type=F32)


def over(values, size):
    return ((values.astype(F32) + 0.5) * (1.0 / size)).astype(jnp.int32)


def in_piece(at, count):
    lev = jnp.where(at >= count * HALF, 1, 0)
    rest = at - lev * (count * HALF)
    row = over(rest, HALF)
    return lev, row, rest - row * HALF, (at >= 0) & (at < LEVS * count * HALF)


def frame_place(at):
    place = jnp.full(at.shape, -1, jnp.int32)
    first = 0
    for size, count, half in ((BIG, ROWS - OFF, 1), (THIN, OFF, 1), (BIG, ROWS - OFF, 0), (THIN, OFF, 0)):
        lev, row, sub, used = in_piece(at - first, count)
        skip = ROWS - count if count != OFF else 0
        token = (lev * ROWS + row + skip) * COLS + half * HALF + sub
        place = jnp.where(used, token, place)
        first += size
    return place


def one_hot(match):
    return match.astype(F32).astype(BF16)


def pack_kernel(tok_ref, cot_ref, own_ref, side_ref, low_ref, corner_ref):
    both = jnp.concatenate(
        [ref[...].astype(F32).reshape(LEVS * ROWS * COLS, C) for ref in (tok_ref, cot_ref)], axis=-1
    ).astype(BF16)

    def pick(first, count, col, size):
        shape = (size, LEVS * ROWS * COLS)
        lev, row, sub, used = in_piece(iota(shape, 0), count)
        token = ((row + first) * COLS + col + sub) * 2 + lev
        return product(one_hot((iota(shape, 1) == token) & used), both).astype(BF16)

    own_ref[...] = pick(0, ROWS - OFF, 0, BIG)
    side_ref[...] = pick(0, ROWS - OFF, HALF, BIG)
    low_ref[...] = pick(ROWS - OFF, OFF, 0, THIN)
    corner_ref[...] = pick(ROWS - OFF, OFF, HALF, THIN)


def weight_kernel(quant_ref, cq_ref, cp_ref, cu_ref, cd_ref, wq_ref, wp_ref, wu_ref, wd_ref):
    def dequant(codes, layer):
        limit = quant_ref[layer : layer + 1, 0:1]
        factor = quant_ref[layer + 4 : layer + 5, 0:1]
        return jnp.minimum(jnp.maximum(codes.astype(F32), -limit), limit) * factor

    full = dequant(cq_ref[...], 0)
    for part in range(3):
        wq_ref[part] = full[:, part * C : (part + 1) * C].astype(BF16)
    wp_ref[...] = dequant(cp_ref[...], 1).astype(BF16)
    wu_ref[...] = dequant(cu_ref[...], 2).astype(BF16)
    wd_ref[...] = dequant(cd_ref[...], 3).astype(BF16)


def bias_kernel(
    bits_ref, scale_ref, idx_ref, tab_ref, bias_ref, quant_ref, rows, places, found
):
    for layer, fan_in in enumerate((C, C, C, FF)):
        limit = jnp.left_shift(1, bits_ref[layer] - 1) - 1
        quant_ref[layer : layer + 1, :] = jnp.full((1, 128), limit, jnp.int32).astype(F32)
        scale = jnp.full((1, 128), scale_ref[layer], jnp.int32).astype(F32)
        quant_ref[layer + 4 : layer + 5, :] = math.sqrt(C / fan_in) / scale

    rows[...] = jnp.zeros_like(rows)
    for head in range(HEADS):
        table = tab_ref[head].astype(F32)
        for high in range(HIGHS):
            width = min(LOWS, POS - high * LOWS)
            rows[high * 16 + head * 2 : high * 16 + head * 2 + 2, 0:width] = table[
                :, high * LOWS : high * LOWS + width
            ]
    table = rows[...].astype(BF16)

    index = idx_ref[...]
    places[...] = jnp.zeros_like(places)
    for lev in range(LEVS):
        base = (1 - lev) * BLOCK
        inside = index[base : base + BLOCK, base : base + BLOCK]
        at = slice(lev * BLOCK, (lev + 1) * BLOCK)
        places[0, at, 0:BLOCK] = lax.shift_right_logical(inside, 8).astype(F32)
        places[1, at, 0:BLOCK] = jnp.bitwise_and(inside, LOWS - 1).astype(F32)

    entry = iota((LOWS, 128), 0).astype(F32)

    def eight(group, carry):
        at = pl.multiple_of(group * SUB, SUB)
        high = places[0, pl.ds(at, SUB), :]
        low = places[1, pl.ds(at, SUB), :]
        hot = [one_hot(entry == low[s : s + 1]) for s in range(SUB)]
        values = product(table, jnp.concatenate(hot, axis=1))
        for s in range(SUB):
            chosen = jnp.zeros((16, 128), F32)
            here = jnp.broadcast_to(high[s : s + 1], (16, 128))
            for i in range(HIGHS):
                candidate = values[i * 16 : (i + 1) * 16, s * 128 : (s + 1) * 128]
                chosen = jnp.where(here == float(i), candidate, chosen)
            found[at + s] = chosen
        return carry

    lax.fori_loop(0, LEVS * BLOCK // SUB, eight, 0, unroll=18)

    key = iota((BLOCK, 128), 1)
    for win in range(2):
        row = lax.axis_index(LAT) * ROWS - OFF + win * WLAT + over(key, WLON)
        usable = (row >= 0) & (row < lax.axis_size(LAT) * ROWS - LAT_PAD) & (key < BLOCK)
        for lev in range(LEVS):
            for head in range(HEADS):
                values = found[lev * BLOCK : (lev + 1) * BLOCK, head * 2 + win, :]
                bias_ref[lev * 2 + win, head] = jnp.where(usable, values, MASKED)


def unit(values):
    center = values - jnp.mean(values, axis=-1, keepdims=True)
    spread = jnp.mean(center * center, axis=-1, keepdims=True)
    scale = lax.rsqrt(spread + EPSILON)
    return center * scale, scale


def unit_back(normal, scale, upstream):
    level = jnp.mean(upstream, axis=-1, keepdims=True)
    along = jnp.mean(upstream * normal, axis=-1, keepdims=True)
    return scale * (upstream - level - normal * along)


def main_kernel(
    own_ref,
    side_ref,
    low_ref,
    corner_ref,
    wq_ref,
    wp_ref,
    wu_ref,
    wd_ref,
    bias_ref,
    own_out,
    low_out,
    side_out,
    keep_ref,
    give_ref,
):
    total = 2 * (BIG + THIN)
    pieces = [ref[...] for ref in (own_ref, low_ref, side_ref, corner_ref)]
    shape = (FRAME, total)
    order = one_hot(iota(shape, 0) == frame_place(iota(shape, 1)))
    both = product(order, jnp.concatenate(pieces, axis=0))

    place = iota((FRAME, C), 0)
    row = lax.axis_index(LAT) * ROWS - OFF + over(place, COLS)
    row = row - jnp.where(place >= FRAME // 2, ROWS, 0)
    valid = (row >= 0) & (row < lax.axis_size(LAT) * ROWS - LAT_PAD)
    start = jnp.where(valid, both[:, :C], 0.0)
    d_out = jnp.where(valid, both[:, C:], 0.0)
    d_out_low = d_out.astype(BF16)

    normal, scale = unit(start)
    normed = normal.astype(BF16)
    query = product(normed, wq_ref[0]).astype(BF16).astype(F32)
    key = product(normed, wq_ref[1]).astype(BF16).astype(F32)
    value = product(normed, wq_ref[2]).astype(BF16).astype(F32)

    lane_head = iota((HEADS, 1, C), 2) >> 5
    head_mask = lane_head == iota((HEADS, 1, C), 0)
    mask_full = head_mask.astype(F32)

    def spread_heads(block):
        return (block[None] * mask_full).reshape(STACK, C).astype(BF16)

    def join_heads(stacked):
        return jnp.sum(stacked.reshape(HEADS, BLOCK, C) * mask_full, axis=0)

    saved = []
    heads_parts = []
    for block in range(4):
        at = slice(block * BLOCK, (block + 1) * BLOCK)
        q_stack = spread_heads(query[at])
        scores = across(q_stack, key[at].astype(BF16)) * HEAD_DIM ** (-0.5)
        scores = scores + bias_ref[block].reshape(STACK, 128)[:, :BLOCK]
        weights = jnp.exp(scores - jnp.max(scores, axis=-1, keepdims=True))
        weights = weights / jnp.sum(weights, axis=-1, keepdims=True)
        weights_low = weights.astype(BF16)
        heads_parts.append(join_heads(product(weights_low, value[at].astype(BF16))))
        saved.append((q_stack, weights, weights_low))
    heads = jnp.concatenate(heads_parts, axis=0).astype(BF16)

    resid = (start + product(heads, wp_ref[...])).astype(BF16).astype(F32)
    normal_two, scale_two = unit(resid)
    normed_two = normal_two.astype(BF16)
    pre_act = product(normed_two, wu_ref[...])
    inner = math.sqrt(2 / math.pi)
    square = pre_act * pre_act
    bend = jnp.tanh(inner * (pre_act + 0.044715 * (square * pre_act)))
    half = 0.5 * (1.0 + bend)
    hidden = (pre_act * half).astype(BF16)
    slope = half + 0.5 * pre_act * (1.0 - bend * bend) * (
        inner * (1.0 + (3 * 0.044715) * square)
    )
    final = jnp.where(valid, resid + across(hidden, wd_ref[...]), 0.0)

    d_hidden = product(d_out_low, wd_ref[...]).astype(BF16).astype(F32)
    d_pre = (slope * d_hidden).astype(BF16)
    d_normed_two = across(d_pre, wu_ref[...]).astype(BF16).astype(F32)
    d_resid = (d_out + unit_back(normal_two, scale_two, d_normed_two)).astype(BF16)
    d_heads = across(d_resid, wp_ref[...]).astype(BF16).astype(F32)

    dq_parts = []
    dk_parts = []
    dv_parts = []
    for block in range(4):
        at = slice(block * BLOCK, (block + 1) * BLOCK)
        q_stack, weights, weights_low = saved[block]
        d_stack = spread_heads(d_heads[at])
        d_weights = across(d_stack, value[at].astype(BF16)).astype(BF16).astype(F32)
        dv_parts.append(crossed(weights_low, d_stack))
        inside = jnp.sum(weights * d_weights, axis=-1, keepdims=True)
        d_scores = (weights * (d_weights - inside) * HEAD_DIM ** (-0.5)).astype(BF16)
        dq_parts.append(join_heads(product(d_scores, key[at].astype(BF16))))
        dk_parts.append(crossed(d_scores, q_stack))
    d_query = jnp.concatenate(dq_parts, axis=0).astype(BF16)
    d_key = jnp.concatenate(dk_parts, axis=0).astype(BF16)
    d_value = jnp.concatenate(dv_parts, axis=0).astype(BF16)

    d_normed = across(d_query, wq_ref[0]) + across(d_key, wq_ref[1]) + across(d_value, wq_ref[2])
    d_normed = d_normed.astype(BF16).astype(F32)
    grad = jnp.where(valid, d_resid.astype(F32) + unit_back(normal, scale, d_normed), 0.0)

    result = jnp.concatenate([final, grad], axis=-1).astype(BF16)
    shape = (total, FRAME)
    order = one_hot(iota(shape, 1) == frame_place(iota(shape, 0)))
    parted = product(order, result).astype(BF16)
    own_out[...] = parted[0:BIG]
    low_out[...] = parted[BIG : BIG + THIN]
    side_out[...] = parted[BIG + THIN :]

    small = [
        crossed(normed, d_query),
        crossed(normed, d_key),
        crossed(normed, d_value),
        crossed(heads, d_resid),
    ]
    tiles = [total[:, :128] for total in small]
    tiles += [
        jnp.concatenate([small[i][:, 128:], small[i + 1][:, 128:]], axis=-1) for i in (0, 2)
    ]
    for wide in (crossed(normed_two, d_pre), crossed(d_out_low, hidden)):
        tiles += [wide[:, i * 128 : (i + 1) * 128] for i in range(6)]
    half_tiles = len(tiles) // 2

    def store(ref, first):
        for i in range(half_tiles):
            ref[i * C : (i + 1) * C, :] = tiles[first + i].astype(BF16)

    core = lax.axis_index("c")

    @pl.when(core == 0)
    def _():
        store(keep_ref, 0)
        store(give_ref, half_tiles)

    @pl.when(core != 0)
    def _():
        store(keep_ref, half_tiles)
        store(give_ref, 0)


def spread_kernel(own_ref, other_ref, qkv_ref, proj_ref, up_ref, down_ref):
    first = lax.axis_index("c") == 0
    half_tiles = own_ref.shape[0] // C

    def tile(i):
        at = slice(i % half_tiles * C, (i % half_tiles + 1) * C)
        mine = first if i < half_tiles else jnp.logical_not(first)
        return jnp.where(mine, own_ref[at, :].astype(F32), other_ref[at, :].astype(F32))

    ends = [tile(4)[:, :64], tile(4)[:, 64:], tile(5)[:, :64], tile(5)[:, 64:]]
    small = [jnp.concatenate([tile(i), ends[i]], axis=-1) for i in range(4)]
    qkv_ref[...] = jnp.concatenate(small[:3], axis=-1).astype(BF16)
    proj_ref[...] = small[3].astype(BF16)
    for i in range(6):
        up_ref[:, i * 128 : (i + 1) * 128] = tile(6 + i).astype(BF16)
        down_ref[:, i * 128 : (i + 1) * 128] = tile(12 + i).astype(BF16)


def finish_kernel(own_ref, side_ref, edge_ref, weight_ref, merged_ref, grad_ref):
    both = jnp.concatenate([own_ref[...], edge_ref[...], side_ref[0:BIG, :]], axis=0)
    final = both[:, :C]
    grad = both[:, C:]
    total = 2 * (BIG + THIN)
    above = ROWS - OFF

    def source(lev, row, col):
        right = col >= HALF
        below = row >= above
        thin = (lev * OFF + row - above) * HALF + jnp.where(right, BIG + THIN, BIG)
        big = (lev * above + row) * HALF + jnp.where(right, BIG + 2 * THIN, 0)
        return jnp.where(below, thin, big) + col - jnp.where(right, HALF, 0)

    count = ROWS * COLS * LEVS
    to = iota((count, total), 0)
    lev = jnp.bitwise_and(to, 1)
    row = over(to, COLS * LEVS)
    col = (to >> 1) - row * COLS
    pick = iota((count, total), 1) == source(lev, row, col)
    grad_ref[...] = product(one_hot(pick), grad).reshape(ROWS, COLS, LEVS, C).astype(BF16)

    count = (ROWS // 2) * (COLS // 2) * LEVS
    to = iota((count, total), 0)
    lev = jnp.bitwise_and(to, 1)
    pair = over(to, COLS // 2 * LEVS)
    beside = (to >> 1) - pair * (COLS // 2)
    parts = []
    for down in range(2):
        for right in range(2):
            pick = iota((count, total), 1) == source(lev, 2 * pair + down, 2 * beside + right)
            parts.append(product(one_hot(pick), final))
    width = 4 * C
    mean = sum(jnp.sum(part, axis=-1, keepdims=True) for part in parts) / width
    centers = [part - mean for part in parts]
    spread = sum(jnp.sum(part * part, axis=-1, keepdims=True) for part in centers) / width
    scale = lax.rsqrt(spread + EPSILON)
    total = jnp.zeros((count, 2 * C), F32)
    for i, part in enumerate(centers):
        total = total + product((part * scale).astype(BF16), weight_ref[i * C : (i + 1) * C, :])
    merged_ref[...] = total.reshape(ROWS // 2, COLS // 2, LEVS, 2 * C).astype(BF16)


def call(kernel, outs, args, scratch=(), scalars=0, flops=0, mib=16):
    vmem = pl.BlockSpec(memory_space=pltpu.VMEM)
    smem = pl.BlockSpec(memory_space=pltpu.SMEM)
    moved = sum(math.prod(a.shape) * a.dtype.itemsize for a in args)
    moved += sum(math.prod(s) * jnp.dtype(t).itemsize for s, t in outs)
    return pl.pallas_call(
        kernel,
        out_shape=[jax.ShapeDtypeStruct(s, t) for s, t in outs],
        in_specs=[smem] * scalars + [vmem] * (len(args) - scalars),
        out_specs=[vmem] * len(outs),
        scratch_shapes=list(scratch),
        compiler_params=pltpu.CompilerParams(vmem_limit_bytes=mib * 1024 * 1024),
        cost_estimate=pl.CostEstimate(flops=flops, bytes_accessed=moved, transcendentals=0),
    )(*args)


def shifted(block, lat_step, lon_step):
    rows = lax.axis_size(LAT)
    cols = lax.axis_size(LON)
    if lat_step and lon_step:
        route = [
            (col * rows + row, (col + lon_step) % cols * rows + row + lat_step)
            for col in range(cols)
            for row in range(rows)
            if 0 <= row + lat_step < rows
        ]
        return lax.ppermute(block, LON + LAT, route)
    if lat_step:
        route = [(r, r + lat_step) for r in range(rows) if 0 <= r + lat_step < rows]
        return lax.ppermute(block, LAT, route)
    return lax.ppermute(block, LON, [(c, (c + lon_step) % cols) for c in range(cols)])


def exchange(parts, axes):
    return lax.all_to_all(parts, axes, 0, 0)


def swapped(block):
    return lax.ppermute(block, "c", [(0, 1), (1, 0)])


def sum_kernel(parts_ref, low_ref, side_ref, out_ref, edge_ref):
    edge_ref[0:THIN, :] = low_ref[...]
    edge_ref[THIN:, :] = side_ref[BIG:, :]
    count, rows, _ = parts_ref.shape
    total = parts_ref[0].astype(F32)
    for i in range(1, count):
        total = total + parts_ref[i].astype(F32)
    out_ref[0:rows, :] = total.astype(BF16)
    if rows < out_ref.shape[0]:
        out_ref[rows:, :] = jnp.zeros((out_ref.shape[0] - rows, 128), BF16)


def sum_spread_kernel(parts_ref, out_ref):
    total = jnp.sum(parts_ref[...].astype(F32), axis=0).astype(BF16)
    out_ref[...] = jnp.broadcast_to(total[None], out_ref.shape)


def copies_kernel(part_ref, out_ref):
    count, rows, _ = out_ref.shape
    for i in range(count):
        out_ref[i] = part_ref[0:rows, :]


def per_device(
    tokens,
    cotangent,
    qkv_codes,
    proj_codes,
    up_codes,
    down_codes,
    bit_widths,
    quant_scales,
    bias_table,
    bias_index,
    merge_weight,
):
    own, side, low, corner = call(
        pack_kernel,
        [((BIG, 2 * C), BF16)] * 2 + [((THIN, 2 * C), BF16)] * 2,
        (tokens.transpose(1, 2, 0, 3), cotangent.transpose(1, 2, 0, 3)),
    )
    side, low, corner = shifted(side, 0, 1), shifted(low, 1, 0), shifted(corner, 1, 1)
    bias, quant = call(
        bias_kernel,
        [((4, HEADS, BLOCK, 128), F32), ((8, 128), F32)],
        (
            bit_widths,
            quant_scales,
            bias_index.reshape(WTOK, WTOK),
            bias_table.transpose(1, 2, 0, 3).reshape(HEADS, 2, POS),
        ),
        [
            pltpu.VMEM((HIGHS * 16, LOWS), F32),
            pltpu.VMEM((2, LEVS * BLOCK, 128), F32),
            pltpu.VMEM((LEVS * BLOCK, 16, 128), F32),
        ],
        scalars=2,
        flops=2_000_000_000,
    )
    weights = call(
        weight_kernel,
        [((3, C, C), BF16), ((C, C), BF16), ((C, FF), BF16), ((C, FF), BF16)],
        (quant, qkv_codes, proj_codes, up_codes, down_codes.T),
        flops=1_000_000_000,
    )
    own, low, side, keep, give = call(
        main_kernel,
        [
            ((BIG, 2 * C), BF16),
            ((THIN, 2 * C), BF16),
            ((BIG + THIN, 2 * C), BF16),
            ((9 * C, 128), BF16),
            ((9 * C, 128), BF16),
        ],
        (own, side, low, corner, *weights, bias),
        flops=2_000_000_000,
        mib=32,
    )

    near = lax.axis_size(NEAR)
    far = lax.axis_size(FAR)
    rows = 9 * C // near
    padded = -(-rows // (8 * far)) * (8 * far)
    part = (keep.astype(F32) + swapped(give).astype(F32)).astype(BF16)
    part = exchange(part.reshape(near, rows, 128), NEAR)
    side = shifted(side, 0, -1)
    part, edge = call(
        sum_kernel,
        [((padded, 128), BF16), ((2 * THIN, 2 * C), BF16)],
        (part, low, side),
    )
    part = exchange(part.reshape(far, padded // far, 128), FAR)
    (part,) = call(sum_spread_kernel, [(part.shape, BF16)], (part,))
    part = exchange(part, FAR).reshape(padded, 128)
    part, edge = lax.optimization_barrier((part, edge))
    edge = shifted(edge, -1, 0)
    (spread,) = call(copies_kernel, [((near, rows, 128), BF16)], (part,))
    half = exchange(spread, NEAR)
    half, edge = lax.optimization_barrier((half, edge))
    merged, grad_tokens = call(
        finish_kernel,
        [((ROWS // 2, COLS // 2, LEVS, 2 * C), BF16), ((ROWS, COLS, LEVS, C), BF16)],
        (own, side, edge, merge_weight),
        flops=400_000_000,
    )
    merged, grad_tokens = merged.transpose(2, 0, 1, 3), grad_tokens.transpose(2, 0, 1, 3)
    half = half.reshape(near * rows, 128)
    qkv, proj, up, down = call(
        spread_kernel,
        [((C, 3 * C), BF16), ((C, C), BF16), ((C, FF), BF16), ((C, FF), BF16)],
        (half, swapped(half)),
    )
    return (merged, grad_tokens, qkv, proj, up, down.T)


def solution(mesh):
    cols, rows = mesh.devices.shape
    fine = Mesh(mesh.devices.reshape(cols // 4, 2, 2, rows // 2, 2), LON + LAT)
    cells = P(None, LAT, LON, None)
    placed = (
        cells,
        cells,
        P(),
        P(),
        P(),
        P(),
        P(),
        P(),
        P(LAT, None, None, None),
        P(),
        P(),
    )
    return jax.shard_map(
        per_device,
        mesh=fine,
        in_specs=placed,
        out_specs=(cells, cells, P(), P(), P(), P()),
        check_vma=False,
    )
```

```python
import math

import jax
import jax.numpy as jnp
from jax import lax
from jax.experimental import pallas as pl
from jax.experimental.pallas import tpu as pltpu
from jax.sharding import Mesh
from jax.sharding import PartitionSpec as P

C = 192
HEADS = 6
FF = 768
HEAD_DIM = 32
WLAT = 6
WLON = 12
LAT_PAD = 11
WTOK = 144
POS = 3312

ROWS = 12
COLS = 12
LEVS = 2
OFF = WLAT // 2
HALF = WLON // 2
SUB = 8
FRAME = LEVS * ROWS * COLS
BLOCK = FRAME // 4
STACK = HEADS * BLOCK
BIG = 112
THIN = 48
LOWS = 256
HIGHS = -(-POS // LOWS)

EPSILON = 1e-05
MASKED = -1000000000.0
F32 = jnp.float32
BF16 = jnp.bfloat16

LAT = ("y", "xl")
LON = ("z", "xh", "c")
NEAR = ("xh", "xl")
FAR = ("y", "z")


def iota(shape, dim):
    return lax.broadcasted_iota(jnp.int32, shape, dim)


def product(left, right):
    return lax.dot_general(left, right, (((1,), (0,)), ((), ())), preferred_element_type=F32)


def across(left, right):
    return lax.dot_general(left, right, (((1,), (1,)), ((), ())), preferred_element_type=F32)


def crossed(left, right):
    return lax.dot_general(left, right, (((0,), (0,)), ((), ())), preferred_element_type=F32)


def over(values, size):
    return ((values.astype(F32) + 0.5) * (1.0 / size)).astype(jnp.int32)


def in_piece(at, count):
    lev = jnp.where(at >= count * HALF, 1, 0)
    rest = at - lev * (count * HALF)
    row = over(rest, HALF)
    return lev, row, rest - row * HALF, (at >= 0) & (at < LEVS * count * HALF)


def frame_place(at):
    place = jnp.full(at.shape, -1, jnp.int32)
    first = 0
    for size, count, half in ((BIG, ROWS - OFF, 1), (THIN, OFF, 1), (BIG, ROWS - OFF, 0), (THIN, OFF, 0)):
        lev, row, sub, used = in_piece(at - first, count)
        skip = ROWS - count if count != OFF else 0
        token = (lev * ROWS + row + skip) * COLS + half * HALF + sub
        place = jnp.where(used, token, place)
        first += size
    return place


def one_hot(match):
    return match.astype(F32).astype(BF16)


def pack_kernel(tok_ref, cot_ref, own_ref, side_ref, low_ref, corner_ref):
    both = jnp.concatenate(
        [ref[...].astype(F32).reshape(LEVS * ROWS * COLS, C) for ref in (tok_ref, cot_ref)], axis=-1
    ).astype(BF16)

    def pick(first, count, col, size):
        shape = (size, LEVS * ROWS * COLS)
        lev, row, sub, used = in_piece(iota(shape, 0), count)
        token = ((row + first) * COLS + col + sub) * 2 + lev
        return product(one_hot((iota(shape, 1) == token) & used), both).astype(BF16)

    own_ref[...] = pick(0, ROWS - OFF, 0, BIG)
    side_ref[...] = pick(0, ROWS - OFF, HALF, BIG)
    low_ref[...] = pick(ROWS - OFF, OFF, 0, THIN)
    corner_ref[...] = pick(ROWS - OFF, OFF, HALF, THIN)


def weight_kernel(quant_ref, cq_ref, cp_ref, cu_ref, cd_ref, wq_ref, wp_ref, wu_ref, wd_ref):
    def dequant(codes, layer):
        limit = quant_ref[layer : layer + 1, 0:1]
        factor = quant_ref[layer + 4 : layer + 5, 0:1]
        return jnp.minimum(jnp.maximum(codes.astype(F32), -limit), limit) * factor

    full = dequant(cq_ref[...], 0)
    for part in range(3):
        wq_ref[part] = full[:, part * C : (part + 1) * C].astype(BF16)
    wp_ref[...] = dequant(cp_ref[...], 1).astype(BF16)
    wu_ref[...] = dequant(cu_ref[...], 2).astype(BF16)
    wd_ref[...] = dequant(cd_ref[...], 3).astype(BF16)


def bias_kernel(
    bits_ref, scale_ref, idx_ref, tab_ref, bias_ref, quant_ref, rows, places, found
):
    for layer, fan_in in enumerate((C, C, C, FF)):
        limit = jnp.left_shift(1, bits_ref[layer] - 1) - 1
        quant_ref[layer : layer + 1, :] = jnp.full((1, 128), limit, jnp.int32).astype(F32)
        scale = jnp.full((1, 128), scale_ref[layer], jnp.int32).astype(F32)
        quant_ref[layer + 4 : layer + 5, :] = math.sqrt(C / fan_in) / scale

    rows[...] = jnp.zeros_like(rows)
    for head in range(HEADS):
        table = tab_ref[head].astype(F32)
        for high in range(HIGHS):
            width = min(LOWS, POS - high * LOWS)
            rows[high * 16 + head * 2 : high * 16 + head * 2 + 2, 0:width] = table[
                :, high * LOWS : high * LOWS + width
            ]
    table = rows[...].astype(BF16)

    index = idx_ref[...]
    places[...] = jnp.zeros_like(places)
    for lev in range(LEVS):
        base = (1 - lev) * BLOCK
        inside = index[base : base + BLOCK, base : base + BLOCK]
        at = slice(lev * BLOCK, (lev + 1) * BLOCK)
        places[0, at, 0:BLOCK] = lax.shift_right_logical(inside, 8).astype(F32)
        places[1, at, 0:BLOCK] = jnp.bitwise_and(inside, LOWS - 1).astype(F32)

    entry = iota((LOWS, 128), 0).astype(F32)

    def eight(group, carry):
        at = pl.multiple_of(group * SUB, SUB)
        high = places[0, pl.ds(at, SUB), :]
        low = places[1, pl.ds(at, SUB), :]
        hot = [one_hot(entry == low[s : s + 1]) for s in range(SUB)]
        values = product(table, jnp.concatenate(hot, axis=1))
        for s in range(SUB):
            chosen = jnp.zeros((16, 128), F32)
            here = jnp.broadcast_to(high[s : s + 1], (16, 128))
            for i in range(HIGHS):
                candidate = values[i * 16 : (i + 1) * 16, s * 128 : (s + 1) * 128]
                chosen = jnp.where(here == float(i), candidate, chosen)
            found[at + s] = chosen
        return carry

    lax.fori_loop(0, LEVS * BLOCK // SUB, eight, 0, unroll=18)

    key = iota((BLOCK, 128), 1)
    for win in range(2):
        row = lax.axis_index(LAT) * ROWS - OFF + win * WLAT + over(key, WLON)
        usable = (row >= 0) & (row < lax.axis_size(LAT) * ROWS - LAT_PAD) & (key < BLOCK)
        for lev in range(LEVS):
            for head in range(HEADS):
                values = found[lev * BLOCK : (lev + 1) * BLOCK, head * 2 + win, :]
                bias_ref[lev * 2 + win, head] = jnp.where(usable, values, MASKED)


def unit(values):
    center = values - jnp.mean(values, axis=-1, keepdims=True)
    spread = jnp.mean(center * center, axis=-1, keepdims=True)
    scale = lax.rsqrt(spread + EPSILON)
    return center * scale, scale


def unit_back(normal, scale, upstream):
    level = jnp.mean(upstream, axis=-1, keepdims=True)
    along = jnp.mean(upstream * normal, axis=-1, keepdims=True)
    return scale * (upstream - level - normal * along)


def main_kernel(
    own_ref,
    side_ref,
    low_ref,
    corner_ref,
    wq_ref,
    wp_ref,
    wu_ref,
    wd_ref,
    bias_ref,
    own_out,
    low_out,
    side_out,
    keep_ref,
    give_ref,
):
    total = 2 * (BIG + THIN)
    pieces = [ref[...] for ref in (own_ref, low_ref, side_ref, corner_ref)]
    shape = (FRAME, total)
    order = one_hot(iota(shape, 0) == frame_place(iota(shape, 1)))
    both = product(order, jnp.concatenate(pieces, axis=0))

    place = iota((FRAME, C), 0)
    row = lax.axis_index(LAT) * ROWS - OFF + over(place, COLS)
    row = row - jnp.where(place >= FRAME // 2, ROWS, 0)
    valid = (row >= 0) & (row < lax.axis_size(LAT) * ROWS - LAT_PAD)
    start = jnp.where(valid, both[:, :C], 0.0)
    d_out = jnp.where(valid, both[:, C:], 0.0)
    d_out_low = d_out.astype(BF16)

    normal, scale = unit(start)
    normed = normal.astype(BF16)
    query = product(normed, wq_ref[0]).astype(BF16).astype(F32)
    key = product(normed, wq_ref[1]).astype(BF16).astype(F32)
    value = product(normed, wq_ref[2]).astype(BF16).astype(F32)

    lane_head = iota((HEADS, 1, C), 2) >> 5
    head_mask = lane_head == iota((HEADS, 1, C), 0)
    mask_full = head_mask.astype(F32)

    def spread_heads(block):
        return (block[None] * mask_full).reshape(STACK, C).astype(BF16)

    def join_heads(stacked):
        return jnp.sum(stacked.reshape(HEADS, BLOCK, C) * mask_full, axis=0)

    saved = []
    heads_parts = []
    for block in range(4):
        at = slice(block * BLOCK, (block + 1) * BLOCK)
        q_stack = spread_heads(query[at])
        scores = across(q_stack, key[at].astype(BF16)) * HEAD_DIM ** (-0.5)
        scores = scores + bias_ref[block].reshape(STACK, 128)[:, :BLOCK]
        weights = jnp.exp(scores - jnp.max(scores, axis=-1, keepdims=True))
        weights = weights * (1.0 / jnp.sum(weights, axis=-1, keepdims=True))
        weights_low = weights.astype(BF16)
        heads_parts.append(join_heads(product(weights_low, value[at].astype(BF16))))
        saved.append((q_stack, weights, weights_low))
    heads = jnp.concatenate(heads_parts, axis=0).astype(BF16)

    resid = (start + product(heads, wp_ref[...])).astype(BF16).astype(F32)
    normal_two, scale_two = unit(resid)
    normed_two = normal_two.astype(BF16)
    pre_act = product(normed_two, wu_ref[...])
    inner = math.sqrt(2 / math.pi)
    square = pre_act * pre_act
    bend = jnp.tanh(inner * (pre_act + 0.044715 * (square * pre_act)))
    half = 0.5 * (1.0 + bend)
    hidden = (pre_act * half).astype(BF16)
    slope = half + 0.5 * pre_act * (1.0 - bend * bend) * (
        inner * (1.0 + (3 * 0.044715) * square)
    )
    final = jnp.where(valid, resid + across(hidden, wd_ref[...]), 0.0)

    d_hidden = product(d_out_low, wd_ref[...]).astype(BF16).astype(F32)
    d_pre = (slope * d_hidden).astype(BF16)
    d_normed_two = across(d_pre, wu_ref[...]).astype(BF16).astype(F32)
    d_resid = (d_out + unit_back(normal_two, scale_two, d_normed_two)).astype(BF16)
    d_heads = across(d_resid, wp_ref[...]).astype(BF16).astype(F32)

    dq_parts = []
    dk_parts = []
    dv_parts = []
    for block in range(4):
        at = slice(block * BLOCK, (block + 1) * BLOCK)
        q_stack, weights, weights_low = saved[block]
        d_stack = spread_heads(d_heads[at])
        d_weights = across(d_stack, value[at].astype(BF16)).astype(BF16).astype(F32)
        dv_parts.append(crossed(weights_low, d_stack))
        inside = jnp.sum(weights * d_weights, axis=-1, keepdims=True)
        d_scores = (weights * (d_weights - inside) * HEAD_DIM ** (-0.5)).astype(BF16)
        dq_parts.append(join_heads(product(d_scores, key[at].astype(BF16))))
        dk_parts.append(crossed(d_scores, q_stack))
    d_query = jnp.concatenate(dq_parts, axis=0).astype(BF16)
    d_key = jnp.concatenate(dk_parts, axis=0).astype(BF16)
    d_value = jnp.concatenate(dv_parts, axis=0).astype(BF16)

    d_normed = across(d_query, wq_ref[0]) + across(d_key, wq_ref[1]) + across(d_value, wq_ref[2])
    d_normed = d_normed.astype(BF16).astype(F32)
    grad = jnp.where(valid, d_resid.astype(F32) + unit_back(normal, scale, d_normed), 0.0)

    result = jnp.concatenate([final, grad], axis=-1).astype(BF16)
    shape = (total, FRAME)
    order = one_hot(iota(shape, 1) == frame_place(iota(shape, 0)))
    parted = product(order, result).astype(BF16)
    own_out[...] = parted[0:BIG]
    low_out[...] = parted[BIG : BIG + THIN]
    side_out[...] = parted[BIG + THIN :]

    small = [
        crossed(normed, d_query),
        crossed(normed, d_key),
        crossed(normed, d_value),
        crossed(heads, d_resid),
    ]
    tiles = [total[:, :128] for total in small]
    tiles += [
        jnp.concatenate([small[i][:, 128:], small[i + 1][:, 128:]], axis=-1) for i in (0, 2)
    ]
    for wide in (crossed(normed_two, d_pre), crossed(d_out_low, hidden)):
        tiles += [wide[:, i * 128 : (i + 1) * 128] for i in range(6)]
    half_tiles = len(tiles) // 2

    def store(ref, first):
        for i in range(half_tiles):
            ref[i * C : (i + 1) * C, :] = tiles[first + i].astype(BF16)

    core = lax.axis_index("c")

    @pl.when(core == 0)
    def _():
        store(keep_ref, 0)
        store(give_ref, half_tiles)

    @pl.when(core != 0)
    def _():
        store(keep_ref, half_tiles)
        store(give_ref, 0)


def spread_kernel(own_ref, other_ref, qkv_ref, proj_ref, up_ref, down_ref):
    first = lax.axis_index("c") == 0
    half_tiles = own_ref.shape[0] // C

    def tile(i):
        at = slice(i % half_tiles * C, (i % half_tiles + 1) * C)
        mine = first if i < half_tiles else jnp.logical_not(first)
        return jnp.where(mine, own_ref[at, :].astype(F32), other_ref[at, :].astype(F32))

    ends = [tile(4)[:, :64], tile(4)[:, 64:], tile(5)[:, :64], tile(5)[:, 64:]]
    small = [jnp.concatenate([tile(i), ends[i]], axis=-1) for i in range(4)]
    qkv_ref[...] = jnp.concatenate(small[:3], axis=-1).astype(BF16)
    proj_ref[...] = small[3].astype(BF16)
    for i in range(6):
        up_ref[:, i * 128 : (i + 1) * 128] = tile(6 + i).astype(BF16)
        down_ref[:, i * 128 : (i + 1) * 128] = tile(12 + i).astype(BF16)


def finish_kernel(own_ref, side_ref, edge_ref, weight_ref, merged_ref, grad_ref):
    both = jnp.concatenate([own_ref[...], edge_ref[...], side_ref[0:BIG, :]], axis=0)
    final = both[:, :C]
    grad = both[:, C:]
    total = 2 * (BIG + THIN)
    above = ROWS - OFF

    def source(lev, row, col):
        right = col >= HALF
        below = row >= above
        thin = (lev * OFF + row - above) * HALF + jnp.where(right, BIG + THIN, BIG)
        big = (lev * above + row) * HALF + jnp.where(right, BIG + 2 * THIN, 0)
        return jnp.where(below, thin, big) + col - jnp.where(right, HALF, 0)

    count = ROWS * COLS * LEVS
    to = iota((count, total), 0)
    lev = jnp.bitwise_and(to, 1)
    row = over(to, COLS * LEVS)
    col = (to >> 1) - row * COLS
    pick = iota((count, total), 1) == source(lev, row, col)
    grad_ref[...] = product(one_hot(pick), grad).reshape(ROWS, COLS, LEVS, C).astype(BF16)

    count = (ROWS // 2) * (COLS // 2) * LEVS
    to = iota((count, total), 0)
    lev = jnp.bitwise_and(to, 1)
    pair = over(to, COLS // 2 * LEVS)
    beside = (to >> 1) - pair * (COLS // 2)
    parts = []
    for down in range(2):
        for right in range(2):
            pick = iota((count, total), 1) == source(lev, 2 * pair + down, 2 * beside + right)
            parts.append(product(one_hot(pick), final))
    width = 4 * C
    mean = sum(jnp.sum(part, axis=-1, keepdims=True) for part in parts) / width
    centers = [part - mean for part in parts]
    spread = sum(jnp.sum(part * part, axis=-1, keepdims=True) for part in centers) / width
    scale = lax.rsqrt(spread + EPSILON)
    total = jnp.zeros((count, 2 * C), F32)
    for i, part in enumerate(centers):
        total = total + product((part * scale).astype(BF16), weight_ref[i * C : (i + 1) * C, :])
    merged_ref[...] = total.reshape(ROWS // 2, COLS // 2, LEVS, 2 * C).astype(BF16)


def call(kernel, outs, args, scratch=(), scalars=0, flops=0, mib=16):
    vmem = pl.BlockSpec(memory_space=pltpu.VMEM)
    smem = pl.BlockSpec(memory_space=pltpu.SMEM)
    moved = sum(math.prod(a.shape) * a.dtype.itemsize for a in args)
    moved += sum(math.prod(s) * jnp.dtype(t).itemsize for s, t in outs)
    return pl.pallas_call(
        kernel,
        out_shape=[jax.ShapeDtypeStruct(s, t) for s, t in outs],
        in_specs=[smem] * scalars + [vmem] * (len(args) - scalars),
        out_specs=[vmem] * len(outs),
        scratch_shapes=list(scratch),
        compiler_params=pltpu.CompilerParams(vmem_limit_bytes=mib * 1024 * 1024),
        cost_estimate=pl.CostEstimate(flops=flops, bytes_accessed=moved, transcendentals=0),
    )(*args)


def shifted(block, lat_step, lon_step):
    rows = lax.axis_size(LAT)
    cols = lax.axis_size(LON)
    if lat_step and lon_step:
        route = [
            (col * rows + row, (col + lon_step) % cols * rows + row + lat_step)
            for col in range(cols)
            for row in range(rows)
            if 0 <= row + lat_step < rows
        ]
        return lax.ppermute(block, LON + LAT, route)
    if lat_step:
        route = [(r, r + lat_step) for r in range(rows) if 0 <= r + lat_step < rows]
        return lax.ppermute(block, LAT, route)
    return lax.ppermute(block, LON, [(c, (c + lon_step) % cols) for c in range(cols)])


def exchange(parts, axes):
    return lax.all_to_all(parts, axes, 0, 0)


def swapped(block):
    return lax.ppermute(block, "c", [(0, 1), (1, 0)])


def sum_kernel(parts_ref, low_ref, side_ref, out_ref, edge_ref):
    edge_ref[0:THIN, :] = low_ref[...]
    edge_ref[THIN:, :] = side_ref[BIG:, :]
    count, rows, _ = parts_ref.shape
    total = parts_ref[0].astype(F32)
    for i in range(1, count):
        total = total + parts_ref[i].astype(F32)
    out_ref[0:rows, :] = total.astype(BF16)
    if rows < out_ref.shape[0]:
        out_ref[rows:, :] = jnp.zeros((out_ref.shape[0] - rows, 128), BF16)


def sum_spread_kernel(parts_ref, out_ref):
    total = jnp.sum(parts_ref[...].astype(F32), axis=0).astype(BF16)
    out_ref[...] = jnp.broadcast_to(total[None], out_ref.shape)


def add_kernel(one_ref, two_ref, out_ref):
    count, rows, _ = out_ref.shape
    for i in range(count):
        at = slice(i * rows, (i + 1) * rows)
        out_ref[i] = (one_ref[at, :].astype(F32) + two_ref[at, :].astype(F32)).astype(BF16)


def copies_kernel(part_ref, out_ref):
    count, rows, _ = out_ref.shape
    for i in range(count):
        out_ref[i] = part_ref[0:rows, :]


def per_device(
    tokens,
    cotangent,
    qkv_codes,
    proj_codes,
    up_codes,
    down_codes,
    bit_widths,
    quant_scales,
    bias_table,
    bias_index,
    merge_weight,
):
    own, side, low, corner = call(
        pack_kernel,
        [((BIG, 2 * C), BF16)] * 2 + [((THIN, 2 * C), BF16)] * 2,
        (tokens.transpose(1, 2, 0, 3), cotangent.transpose(1, 2, 0, 3)),
    )
    side, low, corner = shifted(side, 0, 1), shifted(low, 1, 0), shifted(corner, 1, 1)
    bias, quant = call(
        bias_kernel,
        [((4, HEADS, BLOCK, 128), F32), ((8, 128), F32)],
        (
            bit_widths,
            quant_scales,
            bias_index.reshape(WTOK, WTOK),
            bias_table.transpose(1, 2, 0, 3).reshape(HEADS, 2, POS),
        ),
        [
            pltpu.VMEM((HIGHS * 16, LOWS), F32),
            pltpu.VMEM((2, LEVS * BLOCK, 128), F32),
            pltpu.VMEM((LEVS * BLOCK, 16, 128), F32),
        ],
        scalars=2,
        flops=2_000_000_000,
    )
    weights = call(
        weight_kernel,
        [((3, C, C), BF16), ((C, C), BF16), ((C, FF), BF16), ((C, FF), BF16)],
        (quant, qkv_codes, proj_codes, up_codes, down_codes.T),
        flops=1_000_000_000,
    )
    own, low, side, keep, give = call(
        main_kernel,
        [
            ((BIG, 2 * C), BF16),
            ((THIN, 2 * C), BF16),
            ((BIG + THIN, 2 * C), BF16),
            ((9 * C, 128), BF16),
            ((9 * C, 128), BF16),
        ],
        (own, side, low, corner, *weights, bias),
        flops=2_000_000_000,
        mib=32,
    )

    near = lax.axis_size(NEAR)
    far = lax.axis_size(FAR)
    rows = 9 * C // near
    padded = -(-rows // (8 * far)) * (8 * far)
    (part,) = call(add_kernel, [((near, rows, 128), BF16)], (keep, swapped(give)))
    part = exchange(part, NEAR)
    side = shifted(side, 0, -1)
    part, edge = call(
        sum_kernel,
        [((padded, 128), BF16), ((2 * THIN, 2 * C), BF16)],
        (part, low, side),
    )
    part = exchange(part.reshape(far, padded // far, 128), FAR)
    (part,) = call(sum_spread_kernel, [(part.shape, BF16)], (part,))
    part = exchange(part, FAR).reshape(padded, 128)
    part, edge = lax.optimization_barrier((part, edge))
    edge = shifted(edge, -1, 0)
    (spread,) = call(copies_kernel, [((near, rows, 128), BF16)], (part,))
    half = exchange(spread, NEAR)
    half, edge = lax.optimization_barrier((half, edge))
    merged, grad_tokens = call(
        finish_kernel,
        [((ROWS // 2, COLS // 2, LEVS, 2 * C), BF16), ((ROWS, COLS, LEVS, C), BF16)],
        (own, side, edge, merge_weight),
        flops=400_000_000,
    )
    merged, grad_tokens = merged.transpose(2, 0, 1, 3), grad_tokens.transpose(2, 0, 1, 3)
    half = half.reshape(near * rows, 128)
    qkv, proj, up, down = call(
        spread_kernel,
        [((C, 3 * C), BF16), ((C, C), BF16), ((C, FF), BF16), ((C, FF), BF16)],
        (half, swapped(half)),
    )
    return (merged, grad_tokens, qkv, proj, up, down.T)


def solution(mesh):
    cols, rows = mesh.devices.shape
    fine = Mesh(mesh.devices.reshape(cols // 4, 2, 2, rows // 2, 2), LON + LAT)
    cells = P(None, LAT, LON, None)
    placed = (
        cells,
        cells,
        P(),
        P(),
        P(),
        P(),
        P(),
        P(),
        P(LAT, None, None, None),
        P(),
        P(),
    )
    return jax.shard_map(
        per_device,
        mesh=fine,
        in_specs=placed,
        out_specs=(cells, cells, P(), P(), P(), P()),
        check_vma=False,
    )
```
